32 devices in a mesh: dp: 4 (over x, core), head: 2 (over y), hidden: 4 (over z).
Axes of the slice: x: 2, y: 2, z: 4, core: 2. Of those that a mesh axis runs over, the one named last changes fastest.
Arguments:
- tokens: bfloat16 [16, 512, 1024], P(('dp', 'hidden'), 'head'), may hold values from -6 to 6
- lengths: int32 [16, 1], P(('dp', 'hidden')), may hold values from 449 to 512, as said below
- norm_first: float32 [1024], replicated, may hold values from 0.5 to 1.5
- w_qkv: bfloat16 [1024, 3, 1024], P(None, None, 'head'), may hold values from -0.1875 to 0.1875
- w_feature: bfloat16 [2, 16, 64, 64], P(None, 'head'), may hold values from -1.5 to 1.5
- w_out: bfloat16 [1024, 1024], P('head'), may hold values from -2 to 2
- norm_second: float32 [1024], replicated, may hold values from 0.5 to 1.5
- w_up: bfloat16 [1024, 4096], P(None, 'hidden'), may hold values from -0.1875 to 0.1875
- w_down: bfloat16 [4096, 1024], P('hidden'), may hold values from -0.09375 to 0.09375
- cotangent: bfloat16 [16, 512, 1024], P(('dp', 'hidden'), 'head'), may hold values from -6 to 6
Outputs:
- block_out: bfloat16 [16, 512, 1024], P(('dp', 'hidden'), 'head')
- grad_tokens: float32 [16, 512, 1024], P(('dp', 'hidden'), 'head')
- grad_norm_first: float32 [1024], replicated
- grad_qkv: float32 [1024, 3, 1024], P(None, None, 'head')
- grad_feature: float32 [2, 16, 64, 64], P(None, 'head')
- grad_out: float32 [1024, 1024], P('head')
- grad_norm_second: float32 [1024], replicated
- grad_up: float32 [1024, 4096], P(None, 'hidden')
- grad_down: float32 [4096, 1024], P('hidden')
The draws below stay inside these ranges and needn't reach their ends.
Inputs may be any that keep to these rules, and one draw needn't show every extreme that they name: `lengths`: each bin holds a single sequence, padded up to whole blocks of 64 tokens, that fills the 512 slots of its bin exactly. In every draw some bin holds a sequence of exactly 512 tokens.
All inputs are finite; a program needn't handle non-finite values.
Results may differ from the reference program's by a relative error of at most 0.019.
Values may be sent and summed in bfloat16 or wider, within the bound.
A program may use at most 192 MiB of HBM per device.

```python
import jax
import jax.numpy as jnp
from jax import lax

D = 1024
HEADS = 16
HD = 64
FF = 4096
BLOCK = 64
BIN_TOK = 512
BINS = 16
BIN_CH = 8
LEAST_CH = 16
MOST_CH = 8
SEQS = 1


def spread_blocks(base_key, total_extra, count):
    head_room = MOST_CH - LEAST_CH
    remaining = jnp.full((BINS,), total_extra, jnp.int32)
    pieces = []
    for order_index in range(count - 1):
        later_count = count - 2 - order_index
        least_extra = jnp.maximum(remaining - head_room * later_count, 0)
        most_extra = jnp.minimum(remaining, head_room)
        extra_blocks = jax.random.randint(jax.random.fold_in(base_key, order_index), (BINS,), least_extra, most_extra + 1)
        pieces.append((LEAST_CH + extra_blocks).astype(jnp.int32))
        remaining = (remaining - extra_blocks).astype(jnp.int32)
    pieces.append((LEAST_CH + remaining).astype(jnp.int32))
    return pieces


def draw_lengths(key, part):
    key = jax.random.fold_in(key, 11)
    pick_key, spread_key, pad_key, free_key, bin_key = jax.random.split(key, 5)
    position = jnp.arange(SEQS, dtype=jnp.int32)[None, :]
    if SEQS > 1:
        free_counts = jnp.stack(spread_blocks(free_key, BIN_CH - SEQS * LEAST_CH, SEQS), axis=1).astype(jnp.int32)
        others = spread_blocks(spread_key, BIN_CH - MOST_CH - (SEQS - 1) * LEAST_CH, SEQS - 1)
    else:
        free_counts = jnp.full((BINS, 1), BIN_CH, jnp.int32)
        others = []
    others.append(jnp.full((BINS,), MOST_CH, jnp.int32))
    stacked = jnp.stack(others, axis=1).astype(jnp.int32)
    longest = jax.random.randint(pick_key, (BINS, 1), 0, SEQS)
    source = jnp.where(position < longest, position, position - 1)
    source = jnp.where(position == longest, SEQS - 1, source)
    forced_counts = jnp.take_along_axis(stacked, source, axis=1)
    forced_bin = jax.random.randint(bin_key, (), 0, BINS)
    bin_index = jnp.arange(BINS, dtype=jnp.int32)[:, None]
    is_forced = bin_index == forced_bin
    counts = jnp.where(is_forced, forced_counts, free_counts)
    shortfall = jax.random.randint(pad_key, (BINS, SEQS), 0, BLOCK)
    shortfall = jnp.where(is_forced & (position == longest), 0, shortfall)
    return (counts * BLOCK - shortfall).astype(jnp.int32)


def block_scale(key, shape, cuts, low, top_value):
    def one(dim, shards_of):
        steps = jax.random.uniform(jax.random.fold_in(jax.random.fold_in(key, 6), dim), (shards_of,), jnp.float32, low / len(cuts), top_value / len(cuts))
        return jnp.repeat(jnp.exp(steps), shape[dim] // shards_of).reshape((-1,) + (1,) * (len(shape) - dim - 1))

    level = one(*cuts[0])
    for cut in cuts[1:]:
        level = level * one(*cut)
    return level


def normal_values(key, shape, deviation, most, cuts=(), kind=jnp.bfloat16):
    level = block_scale(key, shape, cuts, -0.22, 0.18) if cuts else 1.0
    values = jax.random.normal(key, shape, jnp.float32) * deviation * level
    return jnp.minimum(jnp.maximum(values, -most), most).astype(kind)


def setup_inputs(seed: int = 0) -> dict:
    splits = jax.random.split(jax.random.key(seed), 11)
    tokens = normal_values(splits[0], (BINS, BIN_TOK, D), 1.0, 6.0, ((0, 16), (1, 2)))
    lengths = draw_lengths(jax.random.fold_in(splits[10], 71), 0)
    norm_first = jnp.clip(1.0 + 0.1 * jax.random.normal(splits[2], (D,), jnp.float32), 0.5, 1.5)
    w_qkv = normal_values(splits[3], (D, 3, HEADS * HD), D ** -0.5, 0.1875, ((2, 2),))
    w_feature = normal_values(splits[4], (2, HEADS, HD, HD), 0.25, 1.5, ((1, 2),))
    w_out = normal_values(splits[5], (HEADS * HD, D), (max(1, HEADS * HD * 4 // (MOST_CH * BLOCK))) ** -0.5, 2.0, ((0, 2),))
    norm_second = jnp.clip(1.0 + 0.1 * jax.random.normal(splits[6], (D,), jnp.float32), 0.5, 1.5)
    w_up = normal_values(splits[7], (D, FF), D ** -0.5, 0.1875, ((1, 4),))
    w_down = normal_values(splits[8], (FF, D), FF ** -0.5, 0.09375, ((0, 4),))
    cotangent = normal_values(splits[9], (BINS, BIN_TOK, D), 1.0, 6.0, ((0, 16), (1, 2)))
    return {"tokens": tokens, "lengths": lengths, "norm_first": norm_first, "w_qkv": w_qkv, "w_feature": w_feature, "w_out": w_out, "norm_second": norm_second, "w_up": w_up, "w_down": w_down, "cotangent": cotangent}


EPS = 1e-05
HIGH = lax.Precision.HIGHEST

@jax.custom_vjp
def low(v):
    return lax.optimization_barrier(v.astype(jnp.bfloat16)).astype(jnp.float32)

@jax.custom_vjp
def low_back(v):
    return v

def low_keep(v):
    return (low(v), None)

def low_pass(kept, grad):
    return (grad,)

def back_keep(v):
    return (v, None)

def back_low(kept, grad):
    return (low(grad),)
low.defvjp(low_keep, low_pass)
low_back.defvjp(back_keep, back_low)

def normalize(values, gain):
    average = lax.optimization_barrier(jnp.mean(values, axis=-1, keepdims=True))
    centred = values - average
    spread = lax.optimization_barrier(jnp.mean(centred * centred, axis=-1, keepdims=True))
    return centred * lax.rsqrt(spread + EPS) * gain

def hedgehog_map(logits):
    return jnp.concatenate([jax.nn.softmax(logits, axis=-1), jax.nn.softmax(-logits, axis=-1)], axis=-1)

def packing(lengths, row_count, block_len):
    lengths = lengths.astype(jnp.int32)
    padded = ((lengths + block_len - 1) // block_len * block_len).astype(jnp.int32)
    ends = jnp.cumsum(padded).astype(jnp.int32)
    starts = (ends - padded).astype(jnp.int32)
    slots = jnp.arange(row_count, dtype=jnp.int32)
    segment = lax.optimization_barrier(jnp.sum((ends[None, :] <= slots[:, None]).astype(jnp.int32), axis=1)).astype(jnp.int32)
    member = segment[:, None] == jnp.arange(lengths.shape[0], dtype=jnp.int32)[None, :]
    begin = lax.optimization_barrier(jnp.sum(jnp.where(member, starts[None, :], 0), axis=1)).astype(jnp.int32)
    extent = lax.optimization_barrier(jnp.sum(jnp.where(member, lengths[None, :], 0), axis=1)).astype(jnp.int32)
    valid = (slots - begin < extent).astype(jnp.float32)
    block_count = row_count // block_len
    block_segment = segment.reshape(block_count, block_len)[:, 0]
    blocks = jnp.arange(block_count, dtype=jnp.int32)
    earlier = (blocks[None, :] < blocks[:, None]) & (block_segment[None, :] == block_segment[:, None])
    return (valid, earlier.astype(jnp.float32))

def residual_layer(inputs, gain_a, w_qkv, w_feat, w_out, gain_m, w_up, w_down, valid, earlier):
    row_count, width = inputs.shape
    head_count = w_feat.shape[1]
    head_size = w_feat.shape[2]
    block_count = earlier.shape[0]
    block_len = row_count // block_count
    normed = low(normalize(inputs, gain_a))
    projected = low(low_back(jnp.dot(normed, w_qkv.reshape(width, -1), precision=HIGH)))
    projected = projected.reshape(row_count, 3, head_count, head_size)
    query, key, value = (projected[:, 0], projected[:, 1], projected[:, 2])
    u_query = low_back(jnp.einsum('nhd,hde->nhe', query, w_feat[0], precision=HIGH))
    u_key = low_back(jnp.einsum('nhd,hde->nhe', key, w_feat[1], precision=HIGH))
    f_query = low(hedgehog_map(u_query)).reshape(block_count, block_len, head_count, 2 * head_size)
    f_key = low(hedgehog_map(u_key) * valid[:, None, None]).reshape(block_count, block_len, head_count, 2 * head_size)
    value_blocks = value.reshape(block_count, block_len, head_count, head_size)
    lower_mask = (jnp.arange(block_len)[:, None] >= jnp.arange(block_len)[None, :]).astype(jnp.float32)
    scores = low_back(jnp.einsum('cihf,cjhf->chij', f_query, f_key, precision=HIGH) * lower_mask)
    inner = jnp.einsum('chij,cjhd->cihd', low(scores), value_blocks, precision=HIGH)
    inner_sum = jnp.transpose(lax.optimization_barrier(jnp.sum(scores, axis=-1)), (0, 2, 1))
    states = low_back(jnp.einsum('cjhf,cjhd->chfd', f_key, value_blocks, precision=HIGH))
    key_sums = lax.optimization_barrier(jnp.sum(f_key, axis=1))
    prior = low(jnp.einsum('ce,ehfd->chfd', earlier, states, precision=HIGH))
    prior_sum = jnp.einsum('ce,ehf->chf', earlier, key_sums, precision=HIGH)
    outer = jnp.einsum('cihf,chfd->cihd', f_query, prior, precision=HIGH)
    outer_sum = jnp.einsum('cihf,chf->cih', f_query, prior_sum, precision=HIGH)
    numer = low_back(inner + outer)
    denom = inner_sum + outer_sum
    mixed = low((numer / denom[..., None]).reshape(row_count, head_count * head_size))
    branch = low_back(jnp.dot(mixed, w_out, precision=HIGH))
    middle = inputs + branch
    normed_second = low(normalize(middle, gain_m))
    hidden_pre = low_back(jnp.dot(normed_second, w_up, precision=HIGH))
    active = low(jax.nn.gelu(hidden_pre, approximate=True))
    return middle + jnp.dot(active, w_down, precision=HIGH)

def reference(tokens, lengths, norm_first, w_qkv, w_feature, w_out, norm_second, w_up, w_down, cotangent):
    params = (norm_first.astype(jnp.float32), w_qkv.astype(jnp.float32), w_feature.astype(jnp.float32), w_out.astype(jnp.float32), norm_second.astype(jnp.float32), w_up.astype(jnp.float32), w_down.astype(jnp.float32))

    def bin_step(totals, entry):
        bin_tokens, bin_lengths, bin_cot = entry
        valid, earlier = packing(bin_lengths, BIN_TOK, BLOCK)

        def forward(inputs, *weights):
            return residual_layer(inputs, *weights, valid, earlier)
        result, back = jax.vjp(forward, bin_tokens.astype(jnp.float32), *params)
        grads = back(bin_cot.astype(jnp.float32))
        totals = tuple((total + grad for total, grad in zip(totals, grads[1:])))
        return (totals, (result.astype(jnp.bfloat16), grads[0]))
    zeros = tuple((jnp.zeros_like(param) for param in params))
    totals, (block_out, grad_tokens) = lax.scan(bin_step, zeros, (tokens, lengths, cotangent))
    return (block_out, grad_tokens, totals[0], totals[1], totals[2], totals[3], totals[4], totals[5], totals[6])
```

```python
import jax, jax.numpy as jnp
from jax import lax
from jax.experimental import pallas as pl
from jax.experimental.pallas import tpu as pltpu
from jax.sharding import PartitionSpec as P
BF=jnp.bfloat16; F32=jnp.float32
NT=(((1,),(1,)),((),()))
TN=(((0,),(0,)),((),()))
SB=256

def mm(a,b): return jnp.dot(a,b,preferred_element_type=F32)
def mm_nt(a,b): return lax.dot_general(a,b,NT,preferred_element_type=F32)
def mm_tn(a,b): return lax.dot_general(a,b,TN,preferred_element_type=F32)

def half_ones(width, size):
    r=lax.broadcasted_iota(jnp.int32,(width,width),0)//size
    c=lax.broadcasted_iota(jnp.int32,(width,width),1)//size
    return (r==c).astype(F32).astype(BF)

def first_half(shape, size):
    return lax.broadcasted_iota(jnp.int32,shape,1)%(2*size) < size

def half_sum(t, ones):
    hi=t.astype(BF); lo=(t-hi.astype(F32)).astype(BF)
    return mm(hi,ones)+mm(lo,ones)

def features(x, w2, ones, size):
    u=mm(x,w2)
    h0=first_half(u.shape,size)
    big=jnp.float32(3e38)
    def both(f, fill):
        return jnp.where(h0, f(jnp.where(h0,u,fill)), f(jnp.where(h0,fill,u)))
    top=both(lambda t: jnp.max(t,axis=1,keepdims=True), -big)
    low=both(lambda t: jnp.min(t,axis=1,keepdims=True), big)
    e=jnp.concatenate([jnp.exp(u-top),jnp.exp(low-u)],axis=1)
    s=mm(e.astype(BF),ones)
    return e/s

def halves(t, h0):
    z=jnp.zeros_like(t)
    return jnp.where(h0,t,z), jnp.where(h0,z,t)

def attend(fq, fk, v, size):
    n=fq.shape[0]
    h0=first_half(fq.shape,size)
    fqs=halves(fq,h0)
    hv=first_half(v.shape,size)
    one=jnp.ones(v.shape,BF)
    ve=halves(jnp.concatenate([v,one],axis=1),h0)
    outs=[]
    for r in range(0,n,SB):
        ext=r+SB
        keep=(lax.broadcasted_iota(jnp.int32,(SB,ext),0)+r)>=lax.broadcasted_iota(jnp.int32,(SB,ext),1)
        acc=None
        for s in range(2):
            sc=mm_nt(fqs[s][r:r+SB],fk[:ext])
            sc=jnp.where(keep,sc,0.0).astype(BF)
            t=mm(sc,ve[s][:ext])
            acc=t if acc is None else acc+t
        outs.append(acc)
    p=jnp.concatenate(outs,axis=0)
    w=v.shape[1]
    rden=1.0/p[:,w:]
    return p[:,:w]*rden, rden

def attend_back(fq,fk,v,mixed,rden,datt,ones,size):
    n,w=v.shape
    wide=(n,2*w)
    h0=first_half(wide,size)
    dn=(datt*rden).astype(BF)
    dd=-half_sum(datt*mixed.astype(F32),ones)*rden
    hi=dd.astype(BF); lo=(dd-hi.astype(F32)).astype(BF)
    lane=lax.broadcasted_iota(jnp.int32,(n,w),1)%size
    zero=jnp.zeros((n,w),BF)
    ext_=jnp.where(lane==0,hi,jnp.where(lane==1,lo,zero))
    nx=halves(jnp.concatenate([dn,ext_],axis=1),h0)
    vx=jnp.concatenate([v,jnp.ones((n,w),BF)],axis=1)
    fqs=halves(fq,h0); fks=halves(fk,h0)
    dfq=[];dfk=[];dv=[]
    for r in range(0,n,SB):
        ext=r+SB
        keep=(lax.broadcasted_iota(jnp.int32,(SB,ext),0)+r)>=lax.broadcasted_iota(jnp.int32,(SB,ext),1)
        acc=0.0
        for s in range(2):
            ds=jnp.where(keep,mm_nt(nx[s][r:r+SB],vx[:ext]),0.0).astype(BF)
            acc=acc+mm(ds,fks[s][:ext])
        dfq.append(acc)
        left=n-r
        keep=lax.broadcasted_iota(jnp.int32,(SB,left),0)<=lax.broadcasted_iota(jnp.int32,(SB,left),1)
        ak=0.0; av=0.0
        for s in range(2):
            ds=jnp.where(keep,mm_nt(vx[r:r+SB],nx[s][r:]),0.0).astype(BF)
            ak=ak+mm(ds,fqs[s][r:])
            sc=jnp.where(keep,mm_nt(fk[r:r+SB],fqs[s][r:]),0.0).astype(BF)
            av=av+mm(sc,nx[s][r:,:w])
        dfk.append(ak); dv.append(av)
    cat=lambda t: jnp.concatenate(t,axis=0)
    return cat(dfq),cat(dfk),cat(dv)

def feature_back(f, df, ones):
    w=f.shape[1]//2
    f=f.astype(F32)
    part=f*(df-half_sum(f*df,ones))
    return (part[:,:w]-part[:,w:]).astype(BF)

def pair_weights(wf_ref, w2_ref):
    hd=wf_ref.shape[-1]
    w2_ref[...]=jnp.zeros_like(w2_ref)
    for t in range(2):
        for p in range(w2_ref.shape[1]):
            w2_ref[t,p,:hd,:hd]=wf_ref[t,2*p]
            w2_ref[t,p,hd:,hd:]=wf_ref[t,2*p+1]

def fwd_kernel(len_ref, rows_ref, wqkv_ref, wf_ref, wout_ref, proj_ref, feat_ref, mixed_ref, rden_ref, branch_ref, w2_ref):
    hd=wf_ref.shape[-1]; w=2*hd; n=rows_ref.shape[0]; pairs=w2_ref.shape[1]
    pair_weights(wf_ref,w2_ref)
    for i in range(3):
        proj_ref[i]=mm(rows_ref[...],wqkv_ref[i]).astype(BF)
    ones=half_ones(2*w,hd)
    valid=lax.broadcasted_iota(jnp.int32,(n,2*w),0)<len_ref[0,0]
    def body(p,_):
        c=pl.ds(pl.multiple_of(p*w,w),w)
        fq=features(proj_ref[0,:,c],w2_ref[0,p],ones,hd).astype(BF)
        fk=jnp.where(valid,features(proj_ref[1,:,c],w2_ref[1,p],ones,hd),0.0).astype(BF)
        feat_ref[0,p]=fq; feat_ref[1,p]=fk
        m,rd=attend(fq,fk,proj_ref[2,:,c],hd)
        mixed_ref[:,c]=m.astype(BF); rden_ref[:,c]=rd
        return 0
    lax.fori_loop(0,pairs,body,0)
    branch_ref[...]=mm(mixed_ref[...],wout_ref[...]).astype(branch_ref.dtype)

def bwd_kernel(rows_ref,wqkv_ref,wf_ref,wout_ref,proj_ref,feat_ref,mixed_ref,rden_ref,dbr_ref,
               gq_ref,gf_ref,go_ref,dfirst_ref,w2_ref,datt_ref,dproj_ref):
    hd=wf_ref.shape[-1]; w=2*hd; n=rows_ref.shape[0]; pairs=w2_ref.shape[1]
    pair_weights(wf_ref,w2_ref)
    ones=half_ones(2*w,hd); ones1=half_ones(w,hd)
    datt_ref[...]=mm_nt(dbr_ref[...],wout_ref[...])
    go_ref[...]=mm_tn(mixed_ref[...],dbr_ref[...]).astype(go_ref.dtype)
    def body(p,_):
        c=pl.ds(pl.multiple_of(p*w,w),w)
        fq=feat_ref[0,p]; fk=feat_ref[1,p]
        dfq,dfk,dv=attend_back(fq,fk,proj_ref[2,:,c],mixed_ref[:,c],rden_ref[:,c],datt_ref[:,c],ones1,hd)
        for t,(f,df) in enumerate(((fq,dfq),(fk,dfk))):
            du=feature_back(f,df,ones)
            g=mm_tn(proj_ref[t,:,c],du)
            gf_ref[t,2*p]=g[:hd,:hd].astype(gf_ref.dtype); gf_ref[t,2*p+1]=g[hd:,hd:].astype(gf_ref.dtype)
            dproj_ref[t,:,c]=mm_nt(du,w2_ref[t,p]).astype(BF)
        dproj_ref[2,:,c]=dv.astype(BF)
        return 0
    lax.fori_loop(0,pairs,body,0)
    acc=None
    for i in range(3):
        gq_ref[i]=mm_tn(rows_ref[...],dproj_ref[i]).astype(gq_ref.dtype)
        t=mm_nt(dproj_ref[i],wqkv_ref[i])
        acc=t if acc is None else acc+t
    dfirst_ref[...]=acc.astype(dfirst_ref.dtype)
VM=pl.BlockSpec(memory_space=pltpu.VMEM)
SM=pl.BlockSpec(memory_space=pltpu.SMEM)
S=jax.ShapeDtypeStruct
def fwd(length,rows,wqkv,wf,wout):
    n,d=rows.shape; c=wout.shape[0]; h=wf.shape[1]; hd=wf.shape[-1]
    return pl.pallas_call(fwd_kernel,
      out_shape=(S((3,n,c),BF),S((2,h//2,n,4*hd),BF),S((n,c),BF),S((n,c),F32),S((n,d),BF)),
      in_specs=[SM,VM,VM,VM,VM],out_specs=[VM]*5,
      scratch_shapes=[pltpu.VMEM((2,h//2,2*hd,2*hd),BF)],
      compiler_params=pltpu.CompilerParams(vmem_limit_bytes=56*2**20))(length,rows,wqkv,wf,wout)
def bwd(rows,wqkv,wf,wout,proj,feat,mixed,rden,dbr):
    n,d=rows.shape; c=wout.shape[0]; h=wf.shape[1]; hd=wf.shape[-1]
    return pl.pallas_call(bwd_kernel,
      out_shape=(S((3,d,c),BF),S((2,h,hd,hd),F32),S((c,d),BF),S((n,d),BF)),
      in_specs=[VM]*9,out_specs=[VM]*4,
      scratch_shapes=[pltpu.VMEM((2,h//2,2*hd,2*hd),BF),pltpu.VMEM((n,c),F32),pltpu.VMEM((3,n,c),BF)],
      compiler_params=pltpu.CompilerParams(vmem_limit_bytes=56*2**20))(rows,wqkv,wf,wout,proj,feat,mixed,rden,dbr)

EPS=1e-05

def normalize(values, gain):
    average = jnp.mean(values, axis=-1, keepdims=True)
    centred = values - average
    spread = jnp.mean(centred * centred, axis=-1, keepdims=True)
    return centred * lax.rsqrt(spread + EPS) * gain

def smooth_gate(values):
    return jax.nn.gelu(values, approximate=True)

def per_device(
    tokens, lengths, norm_first, w_qkv, w_feature, w_out, norm_second, w_up, w_down, cotangent
):
    wqkv=jnp.transpose(w_qkv,(1,0,2))
    residual_in = tokens[0].astype(jnp.float32)
    normed_first, first_back = jax.vjp(normalize, residual_in, norm_first)
    first_low = normed_first.astype(jnp.bfloat16)
    first_rows = lax.all_gather(first_low, "head", axis=0, tiled=True)
    cot_low = cotangent[0]
    cot_rows = lax.all_gather(cot_low, "hidden", axis=0, tiled=True)
    proj,feat,mixed,rden,part=fwd(lengths,first_rows,wqkv,w_feature,w_out)
    branch = lax.psum_scatter(part, "head", scatter_dimension=0, tiled=True).astype(jnp.float32)
    middle = residual_in + branch
    normed_second, second_back = jax.vjp(normalize, middle, norm_second)
    second_low = normed_second.astype(jnp.bfloat16)
    second_rows = lax.all_gather(second_low, "hidden", axis=0, tiled=True)
    hidden_pre = jnp.dot(second_rows, w_up, preferred_element_type=jnp.float32)
    active = smooth_gate(hidden_pre).astype(jnp.bfloat16)
    gate_grad = jax.vjp(smooth_gate, hidden_pre)[1]
    d_active = jnp.einsum("nd,fd->nf", cot_rows, w_down, preferred_element_type=jnp.float32)
    d_pre = gate_grad(d_active)[0].astype(jnp.bfloat16)
    d_second = lax.psum_scatter(
        jnp.einsum("nf,df->nd", d_pre, w_up, preferred_element_type=jnp.float32).astype(jnp.bfloat16),
        "hidden",
        scatter_dimension=0,
        tiled=True,
    ).astype(jnp.float32)
    mlp_result = lax.psum_scatter(
        jnp.dot(active, w_down, preferred_element_type=jnp.float32).astype(jnp.bfloat16),
        "hidden",
        scatter_dimension=0,
        tiled=True,
    ).astype(jnp.float32)
    block_out = (middle + mlp_result).astype(jnp.bfloat16)
    grad_down = jnp.einsum("nf,nd->fd", active, cot_rows, preferred_element_type=jnp.float32)
    grad_up = jnp.einsum("nd,nf->df", second_rows, d_pre, preferred_element_type=jnp.float32)
    d_middle_norm, grad_norm_second = second_back(d_second)
    d_middle = cot_low.astype(jnp.float32) + d_middle_norm
    d_branch_rows = lax.all_gather(d_middle.astype(jnp.bfloat16), "head", axis=0, tiled=True)
    gq,grad_feature,go,dfirst=bwd(first_rows,wqkv,w_feature,w_out,proj,feat,mixed,rden,d_branch_rows)
    d_first = lax.psum_scatter(dfirst, "head", scatter_dimension=0, tiled=True).astype(jnp.float32)
    d_input_norm, grad_norm_first = first_back(d_first)
    grad_tokens = d_middle + d_input_norm
    grad_up, grad_down = (
        lax.psum(grad_up.astype(jnp.bfloat16), ("dp", "head")).astype(jnp.float32),
        lax.psum(grad_down.astype(jnp.bfloat16), ("dp", "head")).astype(jnp.float32),
    )
    gq, grad_feature, go = (
        lax.psum(gq, ("dp", "hidden")).astype(jnp.float32),
        lax.psum(grad_feature.astype(jnp.bfloat16), ("dp", "hidden")).astype(jnp.float32),
        lax.psum(go, ("dp", "hidden")).astype(jnp.float32),
    )
    grad_norm_first, grad_norm_second = lax.psum(
        (grad_norm_first, grad_norm_second), ("dp", "head", "hidden")
    )
    return (
        block_out[None],
        grad_tokens[None],
        grad_norm_first,
        jnp.transpose(gq,(1,0,2)),
        grad_feature,
        go,
        grad_norm_second,
        grad_up,
        grad_down,
    )


def solution(mesh):
    in_specs = (
        P(("dp", "hidden"), "head", None),
        P(("dp", "hidden"), None),
        P(),
        P(None, None, "head"),
        P(None, "head", None, None),
        P("head", None),
        P(),
        P(None, "hidden"),
        P("hidden", None),
        P(("dp", "hidden"), "head", None),
    )
    out_specs = (
        P(("dp", "hidden"), "head", None),
        P(("dp", "hidden"), "head", None),
        P(),
        P(None, None, "head"),
        P(None, "head", None, None),
        P("head", None),
        P(),
        P(None, "hidden"),
        P("hidden", None),
    )
    return jax.shard_map(
        per_device, mesh=mesh, in_specs=in_specs, out_specs=out_specs, check_vma=False
    )
```

```python
import jax, jax.numpy as jnp
from jax import lax
from jax.experimental import pallas as pl
from jax.experimental.pallas import tpu as pltpu
from jax.sharding import PartitionSpec as P
BF=jnp.bfloat16; F32=jnp.float32
NT=(((1,),(1,)),((),()))
TN=(((0,),(0,)),((),()))
SB=256

def mm(a,b): return jnp.dot(a,b,preferred_element_type=F32)
def mm_nt(a,b): return lax.dot_general(a,b,NT,preferred_element_type=F32)
def mm_tn(a,b): return lax.dot_general(a,b,TN,preferred_element_type=F32)

def half_ones(width, size):
    r=lax.broadcasted_iota(jnp.int32,(width,width),0)//size
    c=lax.broadcasted_iota(jnp.int32,(width,width),1)//size
    return (r==c).astype(F32).astype(BF)

def first_half(shape, size):
    return lax.broadcasted_iota(jnp.int32,shape,1)%(2*size) < size

def half_sum(t, ones):
    hi=t.astype(BF); lo=(t-hi.astype(F32)).astype(BF)
    return mm(hi,ones)+mm(lo,ones)

def features(x, w2, ones, size):
    u=mm(x,w2)
    h0=first_half(u.shape,size)
    big=jnp.float32(3e38)
    def both(f, fill):
        return jnp.where(h0, f(jnp.where(h0,u,fill)), f(jnp.where(h0,fill,u)))
    top=both(lambda t: jnp.max(t,axis=1,keepdims=True), -big)
    low=both(lambda t: jnp.min(t,axis=1,keepdims=True), big)
    e=jnp.concatenate([jnp.exp(u-top),jnp.exp(low-u)],axis=1)
    s=mm(e.astype(BF),ones)
    return e/s

def halves(t, h0):
    z=jnp.zeros_like(t)
    return jnp.where(h0,t,z), jnp.where(h0,z,t)

def attend(fq, fk, v, size):
    n=fq.shape[0]
    h0=first_half(fq.shape,size)
    fqs=halves(fq,h0)
    hv=first_half(v.shape,size)
    one=jnp.ones(v.shape,BF)
    ve=halves(jnp.concatenate([v,one],axis=1),h0)
    outs=[]
    for r in range(0,n,SB):
        ext=r+SB
        keep=(lax.broadcasted_iota(jnp.int32,(SB,ext),0)+r)>=lax.broadcasted_iota(jnp.int32,(SB,ext),1)
        acc=None
        for s in range(2):
            sc=mm_nt(fqs[s][r:r+SB],fk[:ext])
            sc=jnp.where(keep,sc,0.0).astype(BF)
            t=mm(sc,ve[s][:ext])
            acc=t if acc is None else acc+t
        outs.append(acc)
    p=jnp.concatenate(outs,axis=0)
    w=v.shape[1]
    rden=1.0/p[:,w:]
    return p[:,:w]*rden, rden

def attend_back(fq,fk,v,mixed,rden,datt,ones,size):
    n,w=v.shape
    wide=(n,2*w)
    h0=first_half(wide,size)
    dn=(datt*rden).astype(BF)
    dd=-half_sum(datt*mixed.astype(F32),ones)*rden
    hi=dd.astype(BF); lo=(dd-hi.astype(F32)).astype(BF)
    lane=lax.broadcasted_iota(jnp.int32,(n,w),1)%size
    zero=jnp.zeros((n,w),BF)
    ext_=jnp.where(lane==0,hi,jnp.where(lane==1,lo,zero))
    nx=halves(jnp.concatenate([dn,ext_],axis=1),h0)
    vx=jnp.concatenate([v,jnp.ones((n,w),BF)],axis=1)
    fqs=halves(fq,h0); fks=halves(fk,h0)
    dfq=[];dfk=[];dv=[]
    for r in range(0,n,SB):
        ext=r+SB
        keep=(lax.broadcasted_iota(jnp.int32,(SB,ext),0)+r)>=lax.broadcasted_iota(jnp.int32,(SB,ext),1)
        acc=0.0
        for s in range(2):
            ds=jnp.where(keep,mm_nt(nx[s][r:r+SB],vx[:ext]),0.0).astype(BF)
            acc=acc+mm(ds,fks[s][:ext])
        dfq.append(acc)
        left=n-r
        keep=lax.broadcasted_iota(jnp.int32,(SB,left),0)<=lax.broadcasted_iota(jnp.int32,(SB,left),1)
        ak=0.0; av=0.0
        for s in range(2):
            ds=jnp.where(keep,mm_nt(vx[r:r+SB],nx[s][r:]),0.0).astype(BF)
            ak=ak+mm(ds,fqs[s][r:])
            sc=jnp.where(keep,mm_nt(fk[r:r+SB],fqs[s][r:]),0.0).astype(BF)
            av=av+mm(sc,nx[s][r:,:w])
        dfk.append(ak); dv.append(av)
    cat=lambda t: jnp.concatenate(t,axis=0)
    return cat(dfq),cat(dfk),cat(dv)

def feature_back(f, df, ones):
    w=f.shape[1]//2
    f=f.astype(F32)
    part=f*(df-half_sum(f*df,ones))
    return (part[:,:w]-part[:,w:]).astype(BF)

def pair_weights(wf_ref, w2_ref):
    hd=wf_ref.shape[-1]
    w2_ref[...]=jnp.zeros_like(w2_ref)
    for t in range(2):
        for p in range(w2_ref.shape[1]):
            w2_ref[t,p,:hd,:hd]=wf_ref[t,2*p]
            w2_ref[t,p,hd:,hd:]=wf_ref[t,2*p+1]

def fwd_kernel(len_ref, rows_ref, wqkv_ref, wf_ref, wout_ref, proj_ref, feat_ref, mixed_ref, rden_ref, branch_ref, w2_ref):
    hd=wf_ref.shape[-1]; w=2*hd; n=rows_ref.shape[0]; pairs=w2_ref.shape[1]
    pair_weights(wf_ref,w2_ref)
    for i in range(3):
        proj_ref[i]=mm(rows_ref[...],wqkv_ref[i]).astype(BF)
    ones=half_ones(2*w,hd)
    valid=lax.broadcasted_iota(jnp.int32,(n,2*w),0)<len_ref[0,0]
    def body(p,_):
        c=pl.ds(pl.multiple_of(p*w,w),w)
        fq=features(proj_ref[0,:,c],w2_ref[0,p],ones,hd).astype(BF)
        fk=jnp.where(valid,features(proj_ref[1,:,c],w2_ref[1,p],ones,hd),0.0).astype(BF)
        feat_ref[0,p]=fq; feat_ref[1,p]=fk
        m,rd=attend(fq,fk,proj_ref[2,:,c],hd)
        mixed_ref[:,c]=m.astype(BF); rden_ref[:,c]=rd
        return 0
    lax.fori_loop(0,pairs,body,0)
    branch_ref[...]=mm(mixed_ref[...],wout_ref[...]).astype(branch_ref.dtype)

def bwd_kernel(rows_ref,wqkv_ref,wf_ref,wout_ref,proj_ref,feat_ref,mixed_ref,rden_ref,dbr_ref,
               gq_ref,gf_ref,go_ref,dfirst_ref,w2_ref,datt_ref,dproj_ref):
    hd=wf_ref.shape[-1]; w=2*hd; n=rows_ref.shape[0]; pairs=w2_ref.shape[1]
    pair_weights(wf_ref,w2_ref)
    ones=half_ones(2*w,hd); ones1=half_ones(w,hd)
    datt_ref[...]=mm_nt(dbr_ref[...],wout_ref[...])
    go_ref[...]=mm_tn(mixed_ref[...],dbr_ref[...]).astype(go_ref.dtype)
    def body(p,_):
        c=pl.ds(pl.multiple_of(p*w,w),w)
        fq=feat_ref[0,p]; fk=feat_ref[1,p]
        dfq,dfk,dv=attend_back(fq,fk,proj_ref[2,:,c],mixed_ref[:,c],rden_ref[:,c],datt_ref[:,c],ones1,hd)
        for t,(f,df) in enumerate(((fq,dfq),(fk,dfk))):
            du=feature_back(f,df,ones)
            g=mm_tn(proj_ref[t,:,c],du)
            gf_ref[t,2*p]=g[:hd,:hd].astype(gf_ref.dtype); gf_ref[t,2*p+1]=g[hd:,hd:].astype(gf_ref.dtype)
            dproj_ref[t,:,c]=mm_nt(du,w2_ref[t,p]).astype(BF)
        dproj_ref[2,:,c]=dv.astype(BF)
        return 0
    lax.fori_loop(0,pairs,body,0)
    acc=None
    for i in range(3):
        gq_ref[i]=mm_tn(rows_ref[...],dproj_ref[i]).astype(gq_ref.dtype)
        t=mm_nt(dproj_ref[i],wqkv_ref[i])
        acc=t if acc is None else acc+t
    dfirst_ref[...]=acc.astype(dfirst_ref.dtype)
VM=pl.BlockSpec(memory_space=pltpu.VMEM)
SM=pl.BlockSpec(memory_space=pltpu.SMEM)
S=jax.ShapeDtypeStruct
def fwd(length,rows,wqkv,wf,wout):
    n,d=rows.shape; c=wout.shape[0]; h=wf.shape[1]; hd=wf.shape[-1]
    return pl.pallas_call(fwd_kernel,
      out_shape=(S((3,n,c),BF),S((2,h//2,n,4*hd),BF),S((n,c),BF),S((n,c),F32),S((n,d),BF)),
      in_specs=[SM,VM,VM,VM,VM],out_specs=[VM]*5,
      scratch_shapes=[pltpu.VMEM((2,h//2,2*hd,2*hd),BF)],
      compiler_params=pltpu.CompilerParams(vmem_limit_bytes=56*2**20))(length,rows,wqkv,wf,wout)
def bwd(rows,wqkv,wf,wout,proj,feat,mixed,rden,dbr):
    n,d=rows.shape; c=wout.shape[0]; h=wf.shape[1]; hd=wf.shape[-1]
    return pl.pallas_call(bwd_kernel,
      out_shape=(S((3,d,c),BF),S((2,h,hd,hd),F32),S((c,d),BF),S((n,d),BF)),
      in_specs=[VM]*9,out_specs=[VM]*4,
      scratch_shapes=[pltpu.VMEM((2,h//2,2*hd,2*hd),BF),pltpu.VMEM((n,c),F32),pltpu.VMEM((3,n,c),BF)],
      compiler_params=pltpu.CompilerParams(vmem_limit_bytes=56*2**20))(rows,wqkv,wf,wout,proj,feat,mixed,rden,dbr)

EPS=1e-05

def normalize(values, gain):
    average = jnp.mean(values, axis=-1, keepdims=True)
    centred = values - average
    spread = jnp.mean(centred * centred, axis=-1, keepdims=True)
    return centred * lax.rsqrt(spread + EPS) * gain

def smooth_gate(values):
    return jax.nn.gelu(values, approximate=True)

def per_device(
    tokens, lengths, norm_first, w_qkv, w_feature, w_out, norm_second, w_up, w_down, cotangent
):
    wqkv=jnp.transpose(w_qkv,(1,0,2))
    residual_in = tokens[0].astype(jnp.float32)
    normed_first, first_back = jax.vjp(normalize, residual_in, norm_first)
    first_low = normed_first.astype(jnp.bfloat16)
    first_rows = lax.all_gather(first_low, "head", axis=0, tiled=True)
    cot_low = cotangent[0]
    cot_rows = lax.all_gather(cot_low, "hidden", axis=0, tiled=True)
    proj,feat,mixed,rden,part=fwd(lengths,first_rows,wqkv,w_feature,w_out)
    branch = lax.psum_scatter(part, "head", scatter_dimension=0, tiled=True).astype(jnp.float32)
    middle = residual_in + branch
    normed_second, second_back = jax.vjp(normalize, middle, norm_second)
    second_low = normed_second.astype(jnp.bfloat16)
    second_rows = lax.all_gather(second_low, "hidden", axis=0, tiled=True)
    hidden_pre = jnp.dot(second_rows, w_up, preferred_element_type=jnp.float32)
    active = smooth_gate(hidden_pre).astype(jnp.bfloat16)
    gate_grad = jax.vjp(smooth_gate, hidden_pre)[1]
    d_active = jnp.einsum("nd,fd->nf", cot_rows, w_down, preferred_element_type=jnp.float32)
    d_pre = gate_grad(d_active)[0].astype(jnp.bfloat16)
    d_second = lax.psum_scatter(
        jnp.einsum("nf,df->nd", d_pre, w_up, preferred_element_type=jnp.float32).astype(jnp.bfloat16),
        "hidden",
        scatter_dimension=0,
        tiled=True,
    ).astype(jnp.float32)
    mlp_result = lax.psum_scatter(
        jnp.dot(active, w_down, preferred_element_type=jnp.float32).astype(jnp.bfloat16),
        "hidden",
        scatter_dimension=0,
        tiled=True,
    ).astype(jnp.float32)
    block_out = (middle + mlp_result).astype(jnp.bfloat16)
    grad_down = jnp.einsum("nf,nd->fd", active, cot_rows, preferred_element_type=jnp.float32)
    grad_up = jnp.einsum("nd,nf->df", second_rows, d_pre, preferred_element_type=jnp.float32)
    d_middle_norm, grad_norm_second = second_back(d_second)
    d_middle = cot_low.astype(jnp.float32) + d_middle_norm
    d_branch_rows = lax.all_gather(d_middle.astype(jnp.bfloat16), "head", axis=0, tiled=True)
    gq,grad_feature,go,dfirst=bwd(first_rows,wqkv,w_feature,w_out,proj,feat,mixed,rden,d_branch_rows)
    d_first = lax.psum_scatter(dfirst, "head", scatter_dimension=0, tiled=True).astype(jnp.float32)
    d_input_norm, grad_norm_first = first_back(d_first)
    grad_tokens = d_middle + d_input_norm
    grad_up, grad_down = (
        lax.psum(grad_up.astype(jnp.bfloat16), ("dp", "head")).astype(jnp.float32),
        lax.psum(grad_down.astype(jnp.bfloat16), ("dp", "head")).astype(jnp.float32),
    )
    gq, grad_feature, go = (
        lax.psum(gq, ("dp", "hidden")).astype(jnp.float32),
        lax.psum(grad_feature.astype(jnp.bfloat16), ("dp", "hidden")).astype(jnp.float32),
        lax.psum(go, ("dp", "hidden")).astype(jnp.float32),
    )
    grad_norm_first, grad_norm_second = lax.psum(
        (grad_norm_first, grad_norm_second), ("dp", "head", "hidden")
    )
    return (
        block_out[None],
        grad_tokens[None],
        grad_norm_first,
        jnp.transpose(gq,(1,0,2)),
        grad_feature,
        go,
        grad_norm_second,
        grad_up,
        grad_down,
    )


MESH=pl.DeviceIdType.MESH
ANY=pl.BlockSpec(memory_space=pl.ANY)
EPS=1e-05

def place():
    dp=lax.axis_index("dp")
    return dp//2, dp%2, lax.axis_index("head"), lax.axis_index("hidden")

def around():
    x,c,y,z=place()
    return ((1-x)*2+c,y,z), (x*2+c,1-y,z), (x*2+1-c,y,z)

def along(step):
    x,c,y,z=place()
    return (x*2+c,y,z+step)

def remote(src,dst,sems,i,dev):
    return pltpu.make_async_remote_copy(src_ref=src,dst_ref=dst,send_sem=sems.at[0,i],recv_sem=sems.at[1,i],device_id=dev,device_id_type=MESH)

def greet(peers, line):
    _,_,_,z=place()
    last=lax.axis_size("hidden")-1
    bar=pltpu.get_barrier_semaphore()
    for d in peers:
        pl.semaphore_signal(bar,inc=1,device_id=d,device_id_type=MESH)
    count=len(peers)
    if line:
        for step in (1,-1):
            @pl.when((z<last) if step==1 else (z>0))
            def _():
                pl.semaphore_signal(bar,inc=1,device_id=along(step),device_id_type=MESH)
        count=count+jnp.where(z<last,1,0)+jnp.where(z>0,1,0)
    pl.semaphore_wait(bar,count)

def unit(values):
    centred=values-jnp.mean(values,axis=-1,keepdims=True)
    r=lax.rsqrt(jnp.mean(centred*centred,axis=-1,keepdims=True)+EPS)
    return centred*r, r

def k1_kernel(len_ref,tok,g1,wqkv,wf,wout,g2,wup,wdn,cot,
              tok_o,rows_o,proj_o,feat_o,mixed_o,rden_o,mid_o,sec_o,wu_o,wd_o,cot_o,
              T,rows,wq,wo,proj,feat,mixed,rden,own,snd,rcv,mid,sec,w2,loc,rem,zr,zl,dd):
    x,c,y,z=place()
    last=lax.axis_size("hidden")-1
    nx,ny,nc=around()
    R=tok.shape[0]; n=2*R; d=tok.shape[1]
    hd=wf.shape[-1]; w=2*hd; pairs=w2.shape[1]
    q=x*2+y
    lc=lambda s,t,i: pltpu.make_async_copy(s,t,loc.at[i])
    mine=pl.ds(pl.multiple_of(y*R,R),R); other=pl.ds(pl.multiple_of((1-y)*R,R),R)
    fs=wup.shape[1]//4
    cols=pl.ds(pl.multiple_of(q*fs,fs),fs)
    hu=wup.shape[0]//2; hw=fs//2
    uh=pl.ds(pl.multiple_of(c*hu,hu),hu); dh=pl.ds(pl.multiple_of(c*hw,hw),hw)
    l_tok=lc(tok,T.at[mine],0); l_wq=[lc(wqkv.at[i],wq.at[i],1+i) for i in range(3)]; l_wo=lc(wout,wo,4)
    l_wu=lc(wup.at[:,cols],wu_o.at[z],5); l_wd=lc(wdn.at[cols],wd_o.at[z],6); l_cot=lc(cot,cot_o.at[q],7)
    l_tok.start()
    for k in l_wq: k.start()
    greet((nx,ny,nc),True)
    r_tok=remote(tok,T.at[mine],rem,0,ny)
    r_tok.start()
    def z_copies(s,right):
        j=(z-s+1) if right else (z+s-1)
        sems,dev=(zr,along(1)) if right else (zl,along(-1))
        if s==1:
            su=wup.at[uh,cols]
            sd=wdn.at[pl.ds(pl.multiple_of(q*fs+c*hw,hw),hw)]
        else:
            su=wu_o.at[j,uh]; sd=wd_o.at[j,dh]
        return [remote(su,wu_o.at[j,uh],sems,2*(s-1),dev),remote(sd,wd_o.at[j,dh],sems,2*(s-1)+1,dev)]
    def z_send(s):
        for right in (True,False):
            ok=((z<last)&(z-s+1>=0)) if right else ((z>0)&(z+s-1<=last))
            @pl.when(ok)
            def _():
                for k in z_copies(s,right): k.start()
    def z_recv(s):
        for right in (True,False):
            ok=(z-s>=0) if right else (z+s<=last)
            j=(z-s) if right else (z+s)
            @pl.when(ok)
            def _():
                jj=jnp.clip(j,0,last)
                sems=zr if right else zl
                remote(wu_o.at[jj,uh],wu_o.at[jj,uh],sems,2*(s-1),nc).wait_recv()
                remote(wd_o.at[jj,dh],wd_o.at[jj,dh],sems,2*(s-1)+1,nc).wait_recv()
                i=2*(s-1)+(0 if right else 2*last)
                remote(wu_o.at[jj,uh],wu_o.at[jj,uh],dd,i,nc).start()
                remote(wd_o.at[jj,dh],wd_o.at[jj,dh],dd,i+1,nc).start()
    def z_end():
        for s in range(1,last+1):
            for right in (True,False):
                ok=((z<last)&(z-s+1>=0)) if right else ((z>0)&(z+s-1<=last))
                @pl.when(ok)
                def _():
                    for k in z_copies(s,right): k.wait_send()
                got=(z-s>=0) if right else (z+s<=last)
                j=(z-s) if right else (z+s)
                @pl.when(got)
                def _():
                    jj=jnp.clip(j,0,last)
                    i=2*(s-1)+(0 if right else 2*last)
                    co=1-c
                    ou=pl.ds(pl.multiple_of(co*hu,hu),hu); od=pl.ds(pl.multiple_of(co*hw,hw),hw)
                    remote(wu_o.at[jj,uh],wu_o.at[jj,ou],dd,i,nc).wait()
                    remote(wd_o.at[jj,dh],wd_o.at[jj,od],dd,i+1,nc).wait()
    z_send(1)
    r_cx=remote(cot,cot_o.at[q],rem,1,nx)
    r_cx.start()
    for k in (l_wo,l_wu,l_wd,l_cot): k.start()
    pair_weights(wf,w2)
    ones=half_ones(2*w,hd)
    def first(at):
        xh,_=unit(T[at].astype(F32))
        rows[at]=(xh*g1[...]).astype(BF)
    def project(at):
        for i in range(3): proj[i,at]=mm(rows[at],wq[i]).astype(BF)
    l_tok.wait()
    first(mine)
    for k in l_wq: k.wait()
    project(mine)
    r_tok.wait_recv()
    r_cy=remote(cot,cot_o.at[q],rem,2,ny)
    r_cy.start()
    l_tok_o=lc(T,tok_o,8); l_tok_o.start()
    first(other)
    l_rows=lc(rows,rows_o,9); l_rows.start()
    project(other)
    l_proj=lc(proj,proj_o,10); l_proj.start()
    valid=lax.broadcasted_iota(jnp.int32,(n,2*w),0)<len_ref[0,0]
    def body(p,_):
        cc=pl.ds(pl.multiple_of(p*w,w),w)
        fq=features(proj[0,:,cc],w2[0,p],ones,hd).astype(BF)
        fk=jnp.where(valid,features(proj[1,:,cc],w2[1,p],ones,hd),0.0).astype(BF)
        feat[0,p]=fq; feat[1,p]=fk
        m,rd=attend(fq,fk,proj[2,:,cc],hd)
        mixed[:,cc]=m.astype(BF); rden[:,cc]=rd
        return 0
    lax.fori_loop(0,pairs//2,body,0)
    z_recv(1)
    z_send(2)
    lax.fori_loop(pairs//2,pairs,body,0)
    l_wo.wait()
    snd[...]=mm(mixed[other],wo[...]).astype(BF)
    r_part=remote(snd,rcv,rem,3,ny)
    r_part.start()
    own[...]=mm(mixed[mine],wo[...])
    l_feat=lc(feat,feat_o,11); l_mixed=lc(mixed,mixed_o,12); l_rden=lc(rden,rden_o,13)
    for k in (l_feat,l_mixed,l_rden): k.start()
    z_recv(2)
    z_send(3)
    r_cy.wait_recv()
    yq=x*2+1-y
    r_cf=remote(cot_o.at[yq],cot_o.at[yq],rem,4,nx)
    r_cf.start()
    r_part.wait_recv()
    middle=T[mine].astype(F32)+(own[...]+rcv[...].astype(F32))
    mid[...]=middle
    xh,_=unit(middle)
    sec[...]=(xh*g2[...]).astype(BF)
    l_mid=lc(mid,mid_o,14); l_sec=lc(sec,sec_o,15)
    l_mid.start(); l_sec.start()
    z_recv(3)
    r_cx.wait_recv(); r_cf.wait_recv()
    for k in (r_tok,r_cx,r_cy,r_part,r_cf): k.wait_send()
    z_end()
    for k in (l_wu,l_wd,l_cot,l_tok_o,l_rows,l_proj,l_feat,l_mixed,l_rden,l_mid,l_sec): k.wait()

def k1(length,tok,g1,wqkv,wf,wout,g2,wup,wdn,cot):
    R,d=tok.shape; n=2*R; c=wout.shape[0]; h=wf.shape[1]; hd=wf.shape[-1]; f=wup.shape[1]
    last=lax.axis_size("hidden")-1
    big=[S((n,d),BF),S((n,d),BF),S((3,n,c),BF),S((2,h//2,n,4*hd),BF),S((n,c),BF),S((n,c),F32),S((R,d),F32),S((R,d),BF)]
    vm=[pltpu.VMEM(s.shape,s.dtype) for s in big]
    T,rows,proj,feat,mixed,rden,mid,sec=vm
    D=pltpu.SemaphoreType.DMA
    return pl.pallas_call(k1_kernel,
      out_shape=tuple(big+[S((last+1,d,f//4),BF),S((last+1,f//4,d),BF),S((4,R,d),BF)]),
      in_specs=[SM,ANY,VM,ANY,VM,ANY,VM,ANY,ANY,ANY],out_specs=[ANY]*11,
      scratch_shapes=[T,rows,pltpu.VMEM((3,d,c),BF),pltpu.VMEM((c,d),BF),proj,feat,mixed,rden,
        pltpu.VMEM((R,d),F32),pltpu.VMEM((R,d),BF),pltpu.VMEM((R,d),BF),mid,sec,
        pltpu.VMEM((2,h//2,2*hd,2*hd),BF),D((16,)),D((2,5)),D((2,2*last)),D((2,2*last)),D((2,4*last))],
      compiler_params=pltpu.CompilerParams(vmem_limit_bytes=48*2**20,collective_id=1,has_side_effects=True),
      cost_estimate=pl.CostEstimate(flops=4*10**9,bytes_accessed=30*10**6,transcendentals=10**6))(
      length,tok,g1,wqkv,wf,wout,g2,wup,wdn,cot)

def per_device_k1(
    tokens, lengths, norm_first, w_qkv, w_feature, w_out, norm_second, w_up, w_down, cotangent
):
    wqkv=jnp.transpose(w_qkv,(1,0,2))
    tok,first_rows,proj,feat,mixed,rden,middle,second_low,wu,wd,cot_all=k1(lengths,tokens[0],norm_first[None],wqkv,w_feature,w_out,norm_second[None],w_up,w_down,cotangent[0])
    residual_in = tokens[0].astype(jnp.float32)
    _, first_back = jax.vjp(normalize, residual_in, norm_first)
    cot_low = cotangent[0]
    _, second_back = jax.vjp(normalize, middle, norm_second)
    g=[[0,2],[1,3]]
    sx=lax.all_gather(second_low,"dp",axis_index_groups=g)
    sxy=lax.all_gather(sx,"head",axis=1).reshape(4*256,1024)
    cot_rows=cot_all.reshape(1024,1024)
    up=jnp.transpose(wu,(1,0,2)).reshape(1024,1024)
    dn=wd.reshape(1024,1024)
    hidden_pre = jnp.dot(sxy, up, preferred_element_type=jnp.float32)
    active = smooth_gate(hidden_pre).astype(jnp.bfloat16)
    gate_grad = jax.vjp(smooth_gate, hidden_pre)[1]
    d_active = jnp.einsum("nd,fd->nf", cot_rows, dn, preferred_element_type=jnp.float32)
    d_pre = gate_grad(d_active)[0].astype(jnp.bfloat16)
    def scat(v):
        v=v.astype(jnp.bfloat16).reshape(2,2,256,1024)
        v=lax.psum_scatter(v,"head",scatter_dimension=1)
        return lax.psum_scatter(v,"dp",scatter_dimension=0,axis_index_groups=g).astype(jnp.float32)
    d_second=scat(jnp.einsum("nf,df->nd", d_pre, up, preferred_element_type=jnp.float32))
    mlp_result=scat(jnp.dot(active, dn, preferred_element_type=jnp.float32))
    block_out = (middle + mlp_result).astype(jnp.bfloat16)
    gd = jnp.einsum("nf,nd->fd", active, cot_rows, preferred_element_type=jnp.float32).astype(BF).reshape(4,256,1024)
    gu = jnp.einsum("nd,nf->df", sxy, d_pre, preferred_element_type=jnp.float32).astype(BF).reshape(1024,4,256)
    gd=lax.psum_scatter(gd,"hidden",scatter_dimension=0)
    gu=lax.psum_scatter(gu,"hidden",scatter_dimension=1)
    gd=lax.psum(gd,"dp",axis_index_groups=[[0,1],[2,3]]); gu=lax.psum(gu,"dp",axis_index_groups=[[0,1],[2,3]])
    grad_down=lax.all_gather(lax.all_gather(gd,"head"),"dp",axis_index_groups=g).reshape(1024,1024).astype(F32)
    grad_up=lax.all_gather(lax.all_gather(gu,"head",axis=1),"dp",axis=1,axis_index_groups=g).reshape(1024,1024).astype(F32)
    d_middle_norm, grad_norm_second = second_back(d_second)
    d_middle = cot_low.astype(jnp.float32) + d_middle_norm
    d_branch_rows = lax.all_gather(d_middle.astype(jnp.bfloat16), "head", axis=0, tiled=True)
    gq,grad_feature,go,dfirst=bwd(first_rows,wqkv,w_feature,w_out,proj,feat,mixed,rden,d_branch_rows)
    d_first = lax.psum_scatter(dfirst, "head", scatter_dimension=0, tiled=True).astype(jnp.float32)
    d_input_norm, grad_norm_first = first_back(d_first)
    grad_tokens = d_middle + d_input_norm
    gq, grad_feature, go = (
        lax.psum(gq, ("dp", "hidden")).astype(jnp.float32),
        lax.psum(grad_feature.astype(jnp.bfloat16), ("dp", "hidden")).astype(jnp.float32),
        lax.psum(go, ("dp", "hidden")).astype(jnp.float32),
    )
    grad_norm_first, grad_norm_second = lax.psum(
        (grad_norm_first, grad_norm_second), ("dp", "head", "hidden")
    )
    return (
        block_out[None],
        grad_tokens[None],
        grad_norm_first,
        jnp.transpose(gq,(1,0,2)),
        grad_feature,
        go,
        grad_norm_second,
        grad_up,
        grad_down,
    )


def solution(mesh):
    in_specs = (
        P(("dp", "hidden"), "head", None),
        P(("dp", "hidden"), None),
        P(),
        P(None, None, "head"),
        P(None, "head", None, None),
        P("head", None),
        P(),
        P(None, "hidden"),
        P("hidden", None),
        P(("dp", "hidden"), "head", None),
    )
    out_specs = (
        P(("dp", "hidden"), "head", None),
        P(("dp", "hidden"), "head", None),
        P(),
        P(None, None, "head"),
        P(None, "head", None, None),
        P("head", None),
        P(),
        P(None, "hidden"),
        P("hidden", None),
    )
    near=dict(mesh.shape)=={"dp":4,"head":2,"hidden":4}
    return jax.shard_map(
        per_device_k1 if near else per_device, mesh=mesh, in_specs=in_specs, out_specs=out_specs, check_vma=False
    )
```

```python
import jax, jax.numpy as jnp
from jax import lax
from jax.experimental import pallas as pl
from jax.experimental.pallas import tpu as pltpu
from jax.sharding import PartitionSpec as P
BF=jnp.bfloat16; F32=jnp.float32
NT=(((1,),(1,)),((),()))
TN=(((0,),(0,)),((),()))
SB=256

def mm(a,b): return jnp.dot(a,b,preferred_element_type=F32)
def mm_nt(a,b): return lax.dot_general(a,b,NT,preferred_element_type=F32)
def mm_tn(a,b): return lax.dot_general(a,b,TN,preferred_element_type=F32)

def half_ones(width, size):
    r=lax.broadcasted_iota(jnp.int32,(width,width),0)//size
    c=lax.broadcasted_iota(jnp.int32,(width,width),1)//size
    return (r==c).astype(F32).astype(BF)

def first_half(shape, size):
    return lax.broadcasted_iota(jnp.int32,shape,1)%(2*size) < size

def half_sum(t, ones):
    hi=t.astype(BF); lo=(t-hi.astype(F32)).astype(BF)
    return mm(hi,ones)+mm(lo,ones)

def features(x, w2, ones, size):
    u=mm(x,w2)
    h0=first_half(u.shape,size)
    big=jnp.float32(3e38)
    def both(f, fill):
        return jnp.where(h0, f(jnp.where(h0,u,fill)), f(jnp.where(h0,fill,u)))
    top=both(lambda t: jnp.max(t,axis=1,keepdims=True), -big)
    low=both(lambda t: jnp.min(t,axis=1,keepdims=True), big)
    e=jnp.concatenate([jnp.exp(u-top),jnp.exp(low-u)],axis=1)
    s=mm(e.astype(BF),ones)
    return e/s

def halves(t, h0):
    z=jnp.zeros_like(t)
    return jnp.where(h0,t,z), jnp.where(h0,z,t)

def attend(fq, fk, v, size):
    n=fq.shape[0]
    h0=first_half(fq.shape,size)
    fqs=halves(fq,h0)
    hv=first_half(v.shape,size)
    one=jnp.ones(v.shape,BF)
    ve=halves(jnp.concatenate([v,one],axis=1),h0)
    outs=[]
    for r in range(0,n,SB):
        ext=r+SB
        keep=(lax.broadcasted_iota(jnp.int32,(SB,ext),0)+r)>=lax.broadcasted_iota(jnp.int32,(SB,ext),1)
        acc=None
        for s in range(2):
            sc=mm_nt(fqs[s][r:r+SB],fk[:ext])
            sc=jnp.where(keep,sc,0.0).astype(BF)
            t=mm(sc,ve[s][:ext])
            acc=t if acc is None else acc+t
        outs.append(acc)
    p=jnp.concatenate(outs,axis=0)
    w=v.shape[1]
    rden=1.0/p[:,w:]
    return p[:,:w]*rden, rden

def attend_back(fq,fk,v,mixed,rden,datt,ones,size):
    n,w=v.shape
    wide=(n,2*w)
    h0=first_half(wide,size)
    dn=(datt*rden).astype(BF)
    dd=-half_sum(datt*mixed.astype(F32),ones)*rden
    hi=dd.astype(BF); lo=(dd-hi.astype(F32)).astype(BF)
    lane=lax.broadcasted_iota(jnp.int32,(n,w),1)%size
    zero=jnp.zeros((n,w),BF)
    ext_=jnp.where(lane==0,hi,jnp.where(lane==1,lo,zero))
    nx=halves(jnp.concatenate([dn,ext_],axis=1),h0)
    vx=jnp.concatenate([v,jnp.ones((n,w),BF)],axis=1)
    fqs=halves(fq,h0); fks=halves(fk,h0)
    dfq=[];dfk=[];dv=[]
    for r in range(0,n,SB):
        ext=r+SB
        keep=(lax.broadcasted_iota(jnp.int32,(SB,ext),0)+r)>=lax.broadcasted_iota(jnp.int32,(SB,ext),1)
        acc=0.0
        for s in range(2):
            ds=jnp.where(keep,mm_nt(nx[s][r:r+SB],vx[:ext]),0.0).astype(BF)
            acc=acc+mm(ds,fks[s][:ext])
        dfq.append(acc)
        left=n-r
        keep=lax.broadcasted_iota(jnp.int32,(SB,left),0)<=lax.broadcasted_iota(jnp.int32,(SB,left),1)
        ak=0.0; av=0.0
        for s in range(2):
            ds=jnp.where(keep,mm_nt(vx[r:r+SB],nx[s][r:]),0.0).astype(BF)
            ak=ak+mm(ds,fqs[s][r:])
            sc=jnp.where(keep,mm_nt(fk[r:r+SB],fqs[s][r:]),0.0).astype(BF)
            av=av+mm(sc,nx[s][r:,:w])
        dfk.append(ak); dv.append(av)
    cat=lambda t: jnp.concatenate(t,axis=0)
    return cat(dfq),cat(dfk),cat(dv)

def feature_back(f, df, ones):
    w=f.shape[1]//2
    f=f.astype(F32)
    part=f*(df-half_sum(f*df,ones))
    return (part[:,:w]-part[:,w:]).astype(BF)

def pair_weights(wf_ref, w2_ref):
    hd=wf_ref.shape[-1]
    w2_ref[...]=jnp.zeros_like(w2_ref)
    for t in range(2):
        for p in range(w2_ref.shape[1]):
            w2_ref[t,p,:hd,:hd]=wf_ref[t,2*p]
            w2_ref[t,p,hd:,hd:]=wf_ref[t,2*p+1]

def fwd_kernel(len_ref, rows_ref, wqkv_ref, wf_ref, wout_ref, proj_ref, feat_ref, mixed_ref, rden_ref, branch_ref, w2_ref):
    hd=wf_ref.shape[-1]; w=2*hd; n=rows_ref.shape[0]; pairs=w2_ref.shape[1]
    pair_weights(wf_ref,w2_ref)
    for i in range(3):
        proj_ref[i]=mm(rows_ref[...],wqkv_ref[i]).astype(BF)
    ones=half_ones(2*w,hd)
    valid=lax.broadcasted_iota(jnp.int32,(n,2*w),0)<len_ref[0,0]
    def body(p,_):
        c=pl.ds(pl.multiple_of(p*w,w),w)
        fq=features(proj_ref[0,:,c],w2_ref[0,p],ones,hd).astype(BF)
        fk=jnp.where(valid,features(proj_ref[1,:,c],w2_ref[1,p],ones,hd),0.0).astype(BF)
        feat_ref[0,p]=fq; feat_ref[1,p]=fk
        m,rd=attend(fq,fk,proj_ref[2,:,c],hd)
        mixed_ref[:,c]=m.astype(BF); rden_ref[:,c]=rd
        return 0
    lax.fori_loop(0,pairs,body,0)
    branch_ref[...]=mm(mixed_ref[...],wout_ref[...]).astype(branch_ref.dtype)

def bwd_kernel(rows_ref,wqkv_ref,wf_ref,wout_ref,proj_ref,feat_ref,mixed_ref,rden_ref,dbr_ref,
               gq_ref,gf_ref,go_ref,dfirst_ref,w2_ref,datt_ref,dproj_ref):
    hd=wf_ref.shape[-1]; w=2*hd; n=rows_ref.shape[0]; pairs=w2_ref.shape[1]
    pair_weights(wf_ref,w2_ref)
    ones=half_ones(2*w,hd); ones1=half_ones(w,hd)
    datt_ref[...]=mm_nt(dbr_ref[...],wout_ref[...])
    go_ref[...]=mm_tn(mixed_ref[...],dbr_ref[...]).astype(go_ref.dtype)
    def body(p,_):
        c=pl.ds(pl.multiple_of(p*w,w),w)
        fq=feat_ref[0,p]; fk=feat_ref[1,p]
        dfq,dfk,dv=attend_back(fq,fk,proj_ref[2,:,c],mixed_ref[:,c],rden_ref[:,c],datt_ref[:,c],ones1,hd)
        for t,(f,df) in enumerate(((fq,dfq),(fk,dfk))):
            du=feature_back(f,df,ones)
            g=mm_tn(proj_ref[t,:,c],du)
            gf_ref[t,2*p]=g[:hd,:hd].astype(gf_ref.dtype); gf_ref[t,2*p+1]=g[hd:,hd:].astype(gf_ref.dtype)
            dproj_ref[t,:,c]=mm_nt(du,w2_ref[t,p]).astype(BF)
        dproj_ref[2,:,c]=dv.astype(BF)
        return 0
    lax.fori_loop(0,pairs,body,0)
    acc=None
    for i in range(3):
        gq_ref[i]=mm_tn(rows_ref[...],dproj_ref[i]).astype(gq_ref.dtype)
        t=mm_nt(dproj_ref[i],wqkv_ref[i])
        acc=t if acc is None else acc+t
    dfirst_ref[...]=acc.astype(dfirst_ref.dtype)
VM=pl.BlockSpec(memory_space=pltpu.VMEM)
SM=pl.BlockSpec(memory_space=pltpu.SMEM)
S=jax.ShapeDtypeStruct
def fwd(length,rows,wqkv,wf,wout):
    n,d=rows.shape; c=wout.shape[0]; h=wf.shape[1]; hd=wf.shape[-1]
    return pl.pallas_call(fwd_kernel,
      out_shape=(S((3,n,c),BF),S((2,h//2,n,4*hd),BF),S((n,c),BF),S((n,c),F32),S((n,d),BF)),
      in_specs=[SM,VM,VM,VM,VM],out_specs=[VM]*5,
      scratch_shapes=[pltpu.VMEM((2,h//2,2*hd,2*hd),BF)],
      compiler_params=pltpu.CompilerParams(vmem_limit_bytes=56*2**20))(length,rows,wqkv,wf,wout)
def bwd(rows,wqkv,wf,wout,proj,feat,mixed,rden,dbr):
    n,d=rows.shape; c=wout.shape[0]; h=wf.shape[1]; hd=wf.shape[-1]
    return pl.pallas_call(bwd_kernel,
      out_shape=(S((3,d,c),BF),S((2,h,hd,hd),F32),S((c,d),BF),S((n,d),BF)),
      in_specs=[VM]*9,out_specs=[VM]*4,
      scratch_shapes=[pltpu.VMEM((2,h//2,2*hd,2*hd),BF),pltpu.VMEM((n,c),F32),pltpu.VMEM((3,n,c),BF)],
      compiler_params=pltpu.CompilerParams(vmem_limit_bytes=56*2**20))(rows,wqkv,wf,wout,proj,feat,mixed,rden,dbr)

EPS=1e-05

def normalize(values, gain):
    average = jnp.mean(values, axis=-1, keepdims=True)
    centred = values - average
    spread = jnp.mean(centred * centred, axis=-1, keepdims=True)
    return centred * lax.rsqrt(spread + EPS) * gain

def smooth_gate(values):
    return jax.nn.gelu(values, approximate=True)

def per_device(
    tokens, lengths, norm_first, w_qkv, w_feature, w_out, norm_second, w_up, w_down, cotangent
):
    wqkv=jnp.transpose(w_qkv,(1,0,2))
    residual_in = tokens[0].astype(jnp.float32)
    normed_first, first_back = jax.vjp(normalize, residual_in, norm_first)
    first_low = normed_first.astype(jnp.bfloat16)
    first_rows = lax.all_gather(first_low, "head", axis=0, tiled=True)
    cot_low = cotangent[0]
    cot_rows = lax.all_gather(cot_low, "hidden", axis=0, tiled=True)
    proj,feat,mixed,rden,part=fwd(lengths,first_rows,wqkv,w_feature,w_out)
    branch = lax.psum_scatter(part, "head", scatter_dimension=0, tiled=True).astype(jnp.float32)
    middle = residual_in + branch
    normed_second, second_back = jax.vjp(normalize, middle, norm_second)
    second_low = normed_second.astype(jnp.bfloat16)
    second_rows = lax.all_gather(second_low, "hidden", axis=0, tiled=True)
    hidden_pre = jnp.dot(second_rows, w_up, preferred_element_type=jnp.float32)
    active = smooth_gate(hidden_pre).astype(jnp.bfloat16)
    gate_grad = jax.vjp(smooth_gate, hidden_pre)[1]
    d_active = jnp.einsum("nd,fd->nf", cot_rows, w_down, preferred_element_type=jnp.float32)
    d_pre = gate_grad(d_active)[0].astype(jnp.bfloat16)
    d_second = lax.psum_scatter(
        jnp.einsum("nf,df->nd", d_pre, w_up, preferred_element_type=jnp.float32).astype(jnp.bfloat16),
        "hidden",
        scatter_dimension=0,
        tiled=True,
    ).astype(jnp.float32)
    mlp_result = lax.psum_scatter(
        jnp.dot(active, w_down, preferred_element_type=jnp.float32).astype(jnp.bfloat16),
        "hidden",
        scatter_dimension=0,
        tiled=True,
    ).astype(jnp.float32)
    block_out = (middle + mlp_result).astype(jnp.bfloat16)
    grad_down = jnp.einsum("nf,nd->fd", active, cot_rows, preferred_element_type=jnp.float32)
    grad_up = jnp.einsum("nd,nf->df", second_rows, d_pre, preferred_element_type=jnp.float32)
    d_middle_norm, grad_norm_second = second_back(d_second)
    d_middle = cot_low.astype(jnp.float32) + d_middle_norm
    d_branch_rows = lax.all_gather(d_middle.astype(jnp.bfloat16), "head", axis=0, tiled=True)
    gq,grad_feature,go,dfirst=bwd(first_rows,wqkv,w_feature,w_out,proj,feat,mixed,rden,d_branch_rows)
    d_first = lax.psum_scatter(dfirst, "head", scatter_dimension=0, tiled=True).astype(jnp.float32)
    d_input_norm, grad_norm_first = first_back(d_first)
    grad_tokens = d_middle + d_input_norm
    grad_up, grad_down = (
        lax.psum(grad_up.astype(jnp.bfloat16), ("dp", "head")).astype(jnp.float32),
        lax.psum(grad_down.astype(jnp.bfloat16), ("dp", "head")).astype(jnp.float32),
    )
    gq, grad_feature, go = (
        lax.psum(gq, ("dp", "hidden")).astype(jnp.float32),
        lax.psum(grad_feature.astype(jnp.bfloat16), ("dp", "hidden")).astype(jnp.float32),
        lax.psum(go, ("dp", "hidden")).astype(jnp.float32),
    )
    grad_norm_first, grad_norm_second = lax.psum(
        (grad_norm_first, grad_norm_second), ("dp", "head", "hidden")
    )
    return (
        block_out[None],
        grad_tokens[None],
        grad_norm_first,
        jnp.transpose(gq,(1,0,2)),
        grad_feature,
        go,
        grad_norm_second,
        grad_up,
        grad_down,
    )


MESH=pl.DeviceIdType.MESH
ANY=pl.BlockSpec(memory_space=pl.ANY)
EPS=1e-05

def place():
    dp=lax.axis_index("dp")
    return dp//2, dp%2, lax.axis_index("head"), lax.axis_index("hidden")

def around():
    x,c,y,z=place()
    return ((1-x)*2+c,y,z), (x*2+c,1-y,z), (x*2+1-c,y,z)

def along(step):
    x,c,y,z=place()
    return (x*2+c,y,z+step)

def remote(src,dst,sems,i,dev):
    return pltpu.make_async_remote_copy(src_ref=src,dst_ref=dst,send_sem=sems.at[0,i],recv_sem=sems.at[1,i],device_id=dev,device_id_type=MESH)

def greet(peers, line):
    _,_,_,z=place()
    last=lax.axis_size("hidden")-1
    bar=pltpu.get_barrier_semaphore()
    for d in peers:
        pl.semaphore_signal(bar,inc=1,device_id=d,device_id_type=MESH)
    count=len(peers)
    if line:
        for step in (1,-1):
            @pl.when((z<last) if step==1 else (z>0))
            def _():
                pl.semaphore_signal(bar,inc=1,device_id=along(step),device_id_type=MESH)
        count=count+jnp.where(z<last,1,0)+jnp.where(z>0,1,0)
    pl.semaphore_wait(bar,count)

def unit(values):
    centred=values-jnp.mean(values,axis=-1,keepdims=True)
    r=lax.rsqrt(jnp.mean(centred*centred,axis=-1,keepdims=True)+EPS)
    return centred*r, r

def k1_kernel(len_ref,tok,g1,wqkv,wf,wout,g2,wup,wdn,cot,
              tok_o,rows_o,proj_o,feat_o,mixed_o,rden_o,mid_o,sec_o,wu_o,wd_o,cot_o,
              T,rows,wq,wo,proj,feat,mixed,rden,own,snd,rcv,mid,sec,w2,loc,rem,zr,zl,dd):
    x,c,y,z=place()
    last=lax.axis_size("hidden")-1
    nx,ny,nc=around()
    R=tok.shape[0]; n=2*R; d=tok.shape[1]
    hd=wf.shape[-1]; w=2*hd; pairs=w2.shape[1]
    q=x*2+y
    lc=lambda s,t,i: pltpu.make_async_copy(s,t,loc.at[i])
    mine=pl.ds(pl.multiple_of(y*R,R),R); other=pl.ds(pl.multiple_of((1-y)*R,R),R)
    fs=wup.shape[1]//4
    cols=pl.ds(pl.multiple_of(q*fs,fs),fs)
    hu=wup.shape[0]//2; hw=fs//2
    uh=pl.ds(pl.multiple_of(c*hu,hu),hu); dh=pl.ds(pl.multiple_of(c*hw,hw),hw)
    l_tok=lc(tok,T.at[mine],0); l_wq=[lc(wqkv.at[i],wq.at[i],1+i) for i in range(3)]; l_wo=lc(wout,wo,4)
    l_wu=lc(wup.at[:,cols],wu_o.at[z],5); l_wd=lc(wdn.at[cols],wd_o.at[z],6); l_cot=lc(cot,cot_o.at[q],7)
    l_tok.start()
    for k in l_wq: k.start()
    greet((nx,ny,nc),True)
    r_tok=remote(tok,T.at[mine],rem,0,ny)
    r_tok.start()
    def z_copies(s,right):
        j=(z-s+1) if right else (z+s-1)
        sems,dev=(zr,along(1)) if right else (zl,along(-1))
        if s==1:
            su=wup.at[uh,cols]
            sd=wdn.at[pl.ds(pl.multiple_of(q*fs+c*hw,hw),hw)]
        else:
            su=wu_o.at[j,uh]; sd=wd_o.at[j,dh]
        return [remote(su,wu_o.at[j,uh],sems,2*(s-1),dev),remote(sd,wd_o.at[j,dh],sems,2*(s-1)+1,dev)]
    def z_send(s):
        for right in (True,False):
            ok=((z<last)&(z-s+1>=0)) if right else ((z>0)&(z+s-1<=last))
            @pl.when(ok)
            def _():
                for k in z_copies(s,right): k.start()
    def z_recv(s):
        for right in (True,False):
            ok=(z-s>=0) if right else (z+s<=last)
            j=(z-s) if right else (z+s)
            @pl.when(ok)
            def _():
                jj=jnp.clip(j,0,last)
                sems=zr if right else zl
                remote(wu_o.at[jj,uh],wu_o.at[jj,uh],sems,2*(s-1),nc).wait_recv()
                remote(wd_o.at[jj,dh],wd_o.at[jj,dh],sems,2*(s-1)+1,nc).wait_recv()
                i=2*(s-1)+(0 if right else 2*last)
                remote(wu_o.at[jj,uh],wu_o.at[jj,uh],dd,i,nc).start()
                remote(wd_o.at[jj,dh],wd_o.at[jj,dh],dd,i+1,nc).start()
    def z_end():
        for s in range(1,last+1):
            for right in (True,False):
                ok=((z<last)&(z-s+1>=0)) if right else ((z>0)&(z+s-1<=last))
                @pl.when(ok)
                def _():
                    for k in z_copies(s,right): k.wait_send()
                got=(z-s>=0) if right else (z+s<=last)
                j=(z-s) if right else (z+s)
                @pl.when(got)
                def _():
                    jj=jnp.clip(j,0,last)
                    i=2*(s-1)+(0 if right else 2*last)
                    co=1-c
                    ou=pl.ds(pl.multiple_of(co*hu,hu),hu); od=pl.ds(pl.multiple_of(co*hw,hw),hw)
                    remote(wu_o.at[jj,uh],wu_o.at[jj,ou],dd,i,nc).wait()
                    remote(wd_o.at[jj,dh],wd_o.at[jj,od],dd,i+1,nc).wait()
    z_send(1)
    r_cx=remote(cot,cot_o.at[q],rem,1,nx)
    r_cx.start()
    for k in (l_wo,l_wu,l_wd,l_cot): k.start()
    pair_weights(wf,w2)
    ones=half_ones(2*w,hd)
    def first(at):
        xh,_=unit(T[at].astype(F32))
        rows[at]=(xh*g1[...]).astype(BF)
    def project(at):
        for i in range(3): proj[i,at]=mm(rows[at],wq[i]).astype(BF)
    l_tok.wait()
    first(mine)
    for k in l_wq: k.wait()
    project(mine)
    r_tok.wait_recv()
    r_cy=remote(cot,cot_o.at[q],rem,2,ny)
    r_cy.start()
    l_tok_o=lc(T,tok_o,8); l_tok_o.start()
    first(other)
    l_rows=lc(rows,rows_o,9); l_rows.start()
    project(other)
    l_proj=lc(proj,proj_o,10); l_proj.start()
    valid=lax.broadcasted_iota(jnp.int32,(n,2*w),0)<len_ref[0,0]
    def body(p,_):
        cc=pl.ds(pl.multiple_of(p*w,w),w)
        fq=features(proj[0,:,cc],w2[0,p],ones,hd).astype(BF)
        fk=jnp.where(valid,features(proj[1,:,cc],w2[1,p],ones,hd),0.0).astype(BF)
        feat[0,p]=fq; feat[1,p]=fk
        m,rd=attend(fq,fk,proj[2,:,cc],hd)
        mixed[:,cc]=m.astype(BF); rden[:,cc]=rd
        return 0
    lax.fori_loop(0,pairs//2,body,0)
    z_recv(1)
    z_send(2)
    lax.fori_loop(pairs//2,pairs,body,0)
    l_wo.wait()
    snd[...]=mm(mixed[other],wo[...]).astype(BF)
    r_part=remote(snd,rcv,rem,3,ny)
    r_part.start()
    own[...]=mm(mixed[mine],wo[...])
    l_feat=lc(feat,feat_o,11); l_mixed=lc(mixed,mixed_o,12); l_rden=lc(rden,rden_o,13)
    for k in (l_feat,l_mixed,l_rden): k.start()
    z_recv(2)
    z_send(3)
    r_cy.wait_recv()
    yq=x*2+1-y
    r_cf=remote(cot_o.at[yq],cot_o.at[yq],rem,4,nx)
    r_cf.start()
    r_part.wait_recv()
    middle=T[mine].astype(F32)+(own[...]+rcv[...].astype(F32))
    mid[...]=middle
    xh,_=unit(middle)
    sec[...]=(xh*g2[...]).astype(BF)
    l_mid=lc(mid,mid_o,14); l_sec=lc(sec,sec_o,15)
    l_mid.start(); l_sec.start()
    z_recv(3)
    r_cx.wait_recv(); r_cf.wait_recv()
    for k in (r_tok,r_cx,r_cy,r_part,r_cf): k.wait_send()
    z_end()
    for k in (l_wu,l_wd,l_cot,l_tok_o,l_rows,l_proj,l_feat,l_mixed,l_rden,l_mid,l_sec): k.wait()

def k1(length,tok,g1,wqkv,wf,wout,g2,wup,wdn,cot):
    R,d=tok.shape; n=2*R; c=wout.shape[0]; h=wf.shape[1]; hd=wf.shape[-1]; f=wup.shape[1]
    last=lax.axis_size("hidden")-1
    big=[S((n,d),BF),S((n,d),BF),S((3,n,c),BF),S((2,h//2,n,4*hd),BF),S((n,c),BF),S((n,c),F32),S((R,d),F32),S((R,d),BF)]
    vm=[pltpu.VMEM(s.shape,s.dtype) for s in big]
    T,rows,proj,feat,mixed,rden,mid,sec=vm
    D=pltpu.SemaphoreType.DMA
    return pl.pallas_call(k1_kernel,
      out_shape=tuple(big+[S((last+1,d,f//4),BF),S((last+1,f//4,d),BF),S((4,R,d),BF)]),
      in_specs=[SM,ANY,VM,ANY,VM,ANY,VM,ANY,ANY,ANY],out_specs=[ANY]*11,
      scratch_shapes=[T,rows,pltpu.VMEM((3,d,c),BF),pltpu.VMEM((c,d),BF),proj,feat,mixed,rden,
        pltpu.VMEM((R,d),F32),pltpu.VMEM((R,d),BF),pltpu.VMEM((R,d),BF),mid,sec,
        pltpu.VMEM((2,h//2,2*hd,2*hd),BF),D((16,)),D((2,5)),D((2,2*last)),D((2,2*last)),D((2,4*last))],
      compiler_params=pltpu.CompilerParams(vmem_limit_bytes=48*2**20,collective_id=1,has_side_effects=True),
      cost_estimate=pl.CostEstimate(flops=4*10**9,bytes_accessed=30*10**6,transcendentals=10**6))(
      length,tok,g1,wqkv,wf,wout,g2,wup,wdn,cot)

def gate(v):
    k=0.7978845608; a=0.044715
    sq=v*v
    t=jnp.tanh(k*v*(1.0+a*sq))
    half=0.5*(1.0+t)
    return v*half, half+0.5*v*(1.0-t*t)*(k+(3.0*a*k)*sq)

def norm_back(values,grad,gain):
    xh,r=unit(values)
    e=grad*gain
    inner=e-jnp.mean(e,axis=-1,keepdims=True)-xh*jnp.mean(e*xh,axis=-1,keepdims=True)
    return r*inner, jnp.sum(grad*xh,axis=0,keepdims=True)

def k2_kernel(sec,mid,cots,wu,wd,g2,
              dmid_o,dbr_o,gn_o,mlp_o,gu_o,gd_o,
              SA,CA,Wu,Wd,act,dpre,P,mlp,gu,gd,midv,dmid,dbr,own,rx,ry,rdx,rdy,loc,ag,rs):
    x,c,y,z=place()
    nx,ny,nc=around()
    R=sec.shape[0]; H=R//2; fs=wu.shape[2]; nz=wu.shape[0]
    qo,qx,qy,qd=x*2+y,(1-x)*2+y,x*2+1-y,(1-x)*2+1-y
    lc=lambda s,t,i: pltpu.make_async_copy(s,t,loc.at[i])
    l_sec=lc(sec,SA.at[qo],0)
    l_cot=lc(cots,CA,1)
    l_wu=[lc(wu.at[j],Wu.at[:,pl.ds(j*fs,fs)],2+j) for j in range(nz)]
    l_wd=lc(wd,Wd,2+nz); l_mid=lc(mid,midv,3+nz)
    l_sec.start()
    for k in l_wu: k.start()
    greet((nx,ny),False)
    A=pl.ds(0,H); B=pl.ds(H,H)
    xa=remote(sec.at[A],SA.at[qo,A],ag,0,nx); xb=remote(sec.at[B],SA.at[qo,B],ag,1,nx)
    yb=remote(sec.at[B],SA.at[qo,B],ag,2,ny); ya=remote(sec.at[A],SA.at[qo,A],ag,3,ny)
    for k in (xa,yb,xb,ya): k.start()
    l_cot.start(); l_wd.start(); l_mid.start()
    def block(qi,keep):
        hp=mm(SA[qi],Wu[...])
        a,ga=gate(hp)
        act[qi]=a.astype(BF)
        dp=(mm_nt(CA[qi],Wd[...])*ga).astype(BF)
        dpre[qi]=dp
        d2=mm_nt(dp,Wu[...])
        if keep: own[...]=d2
        else: P[qi]=d2.astype(BF)
    def down(qi): mlp[qi]=mm(act[qi],Wd[...]).astype(BF)
    l_sec.wait()
    for k in l_wu: k.wait()
    l_cot.wait(); l_wd.wait()
    block(qo,True)
    xa.wait_recv()
    fa=remote(SA.at[qx,A],SA.at[qx,A],ag,4,ny); fa.start()
    yb.wait_recv()
    fb=remote(SA.at[qy,B],SA.at[qy,B],ag,5,nx); fb.start()
    down(qo)
    xb.wait_recv()
    block(qx,False)
    p_xa=remote(P.at[qx,A],rx.at[A],rs,0,nx);
    ya.wait_recv()
    block(qy,False)
    p_yb=remote(P.at[qy,B],ry.at[B],rs,1,ny);
    fa.wait_recv(); fb.wait_recv()
    block(qd,False)
    p_da=remote(P.at[qd,A],rdx,rs,2,nx); p_da.start()
    p_db=remote(P.at[qd,B],rdy,rs,3,ny); p_db.start()
    p_xa.start(); p_yb.start()
    down(qx); down(qy); down(qd)
    l_mlp=lc(mlp,mlp_o,4+nz); l_mlp.start()
    p_da.wait_recv()
    P[qy,A]=(P[qy,A].astype(F32)+rdx[...].astype(F32)).astype(BF)
    p_ya=remote(P.at[qy,A],ry.at[A],rs,4,ny); p_ya.start()
    p_db.wait_recv()
    P[qx,B]=(P[qx,B].astype(F32)+rdy[...].astype(F32)).astype(BF)
    p_xb=remote(P.at[qx,B],rx.at[B],rs,5,nx); p_xb.start()
    rows=4*R
    sa=SA[...].reshape(rows,-1); ca=CA[...].reshape(rows,-1)
    for j in range(nz//2):
        cc=pl.ds(2*j*fs,2*fs)
        t=mm_tn(sa,dpre[:,:,cc].reshape(rows,-1)).astype(BF)
        gu[2*j]=t[:,:fs]; gu[2*j+1]=t[:,fs:]
    l_gu=lc(gu,gu_o,5+nz); l_gu.start()
    for j in range(nz):
        gd[j]=mm_tn(act[:,:,pl.ds(j*fs,fs)].reshape(rows,-1),ca).astype(BF)
    l_gd=lc(gd,gd_o,6+nz); l_gd.start()
    l_mid.wait()
    for k in (p_xa,p_xb,p_ya,p_yb): k.wait_recv()
    ds=own[...]+(rx[...].astype(F32)+ry[...].astype(F32))
    dx,gn=norm_back(midv[...],ds,g2[...])
    gn_o[...]=gn
    dm=CA[qo].astype(F32)+dx
    dmid[...]=dm; dbr[...]=dm.astype(BF)
    l_dm=lc(dmid,dmid_o,7+nz); l_db=lc(dbr,dbr_o,8+nz)
    l_dm.start(); l_db.start()
    for k in (xa,xb,ya,yb,fa,fb,p_xa,p_xb,p_ya,p_yb,p_da,p_db): k.wait_send()
    for k in (l_mlp,l_gu,l_gd,l_dm,l_db): k.wait()

def k2(sec,mid,cots,wu,wd,g2):
    R,d=sec.shape; nz,_,fs=wu.shape; f=nz*fs
    V=pltpu.VMEM; D=pltpu.SemaphoreType.DMA
    return pl.pallas_call(k2_kernel,
      out_shape=(S((R,d),F32),S((R,d),BF),S((1,d),F32),S((4,R,d),BF),S((nz,d,fs),BF),S((nz,fs,d),BF)),
      in_specs=[ANY]*5+[VM],out_specs=[ANY,ANY,VM,ANY,ANY,ANY],
      scratch_shapes=[V((4,R,d),BF),V((4,R,d),BF),V((d,f),BF),V((nz*fs,d),BF),V((4,R,f),BF),V((4,R,f),BF),V((4,R,d),BF),V((4,R,d),BF),
        V((nz,d,fs),BF),V((nz,fs,d),BF),V((R,d),F32),V((R,d),F32),V((R,d),BF),V((R,d),F32),V((R,d),BF),V((R,d),BF),V((R//2,d),BF),V((R//2,d),BF),
        D((9+nz,)),D((2,6)),D((2,6))],
      compiler_params=pltpu.CompilerParams(vmem_limit_bytes=56*2**20,collective_id=2,has_side_effects=True),
      cost_estimate=pl.CostEstimate(flops=13*10**9,bytes_accessed=30*10**6,transcendentals=10**6))(
      sec,mid,cots,wu,wd.reshape(f,d),g2)

class Wires:
    def __init__(self,sems):
        self.sems=sems; self.count=0; self.all=[]
    def send(self,src,dst,dev):
        k=remote(src,dst,self.sems,self.count,dev)
        self.count+=1
        k.start()
        self.all.append(k)
        return k

def add_into(dst,src,step):
    rows=dst.shape[0]
    def body(i,_):
        r=pl.ds(pl.multiple_of(i*step,step),step)
        dst[r]=(dst[r].astype(F32)+src[r].astype(F32)).astype(dst.dtype)
        return 0
    lax.fori_loop(0,rows//step,body,0)

def k3_kernel(dbr,tok,rows_i,wqkv,wf,wout,proj_i,feat_i,mixed_i,rden_i,g1,dmid_i,mid_i,mlp_i,gu_i,gd_i,gn2,
              bo_o,gt_o,go_o,gp_o,gu_o,gd_o,gn_o,
              db,T,rows,rowsT,wq,wo,proj,feat,mixed,rden,datt,dproj,dmid,mid,
              G0,GP,C0,CP,X0,XP,U0,UP,W0,WP,
              GU,GD,cu,cd,zu,zd,yu,yd,ML,ma,mb,na,nb,bo,dfo,dfs,dfr,gt,gn,gr,w2,loc,sems):
    x,c,y,z=place()
    nx,ny,nc=around()
    nh=lax.axis_size("hidden")
    z1,z2=z+1-2*(z%2),(z+2)%nh
    n1=(x*2+c,y,z1); n2=(x*2+c,y,z2)
    R=dbr.shape[0]; n=2*R; d=dbr.shape[1]; H=R//2
    hd=wf.shape[-1]; w=2*hd; pairs=w2.shape[1]; nz=gu_i.shape[0]; fs=gu_i.shape[2]
    qo,qx,qy,qd=x*2+y,(1-x)*2+y,x*2+1-y,(1-x)*2+1-y
    mine=pl.ds(pl.multiple_of(y*R,R),R); other=pl.ds(pl.multiple_of((1-y)*R,R),R)
    A=pl.ds(0,H); B=pl.ds(H,H)
    half=lambda size,b: pl.ds(pl.multiple_of(b*size,size),size)
    nloc=[0]; pend=[]
    def lc(s,t,out=False):
        k=pltpu.make_async_copy(s,t,loc.at[nloc[0]]); nloc[0]+=1
        k.start()
        if out: pend.append(k)
        return k
    wires=Wires(sems)
    send=wires.send
    hu,hw=d//2,fs//2
    l_db=lc(dbr,db.at[mine]); l_wo=lc(wout,wo); l_rows=lc(rows_i,rows)
    greet((nx,ny,nc,n1,n2),False)
    r_db=send(dbr,db.at[mine],ny)
    r_cu=send(gu_i.at[:,half(hu,1-c)],cu,nc); r_cd=send(gd_i.at[:,half(hw,1-c)],cd,nc)
    r_a1=[send(mlp_i.at[qx,A],ma.at[0],nx),send(mlp_i.at[qd,A],ma.at[1],nx)]
    l_gu=lc(gu_i.at[:,half(hu,c)],GU); l_gd=lc(gd_i.at[:,half(hw,c)],GD)
    l_feat=lc(feat_i,feat); l_proj=lc(proj_i,proj); l_mixed=lc(mixed_i,mixed); l_rden=lc(rden_i,rden)
    l_wq=lc(wqkv,wq); l_ml=lc(mlp_i,ML); l_T=lc(tok,T); l_dm=lc(dmid_i,dmid); l_mid=lc(mid_i,mid)
    pair_weights(wf,w2)
    ones=half_ones(2*w,hd); ones1=half_ones(w,hd)

    class Grads:
        def __init__(self,G,bufs,O):
            self.G,self.bufs,self.O=G,bufs,O
            self.size=G.shape[0]; self.base=0; self.k=0
            self.steps=[(nc,c),(nx,x),(n1,z%2),(n2,z//2)]
        def start(self): self._send()
        def _send(self):
            dev,bit=self.steps[self.k]
            self.size//=2
            s=self.size
            away=pl.multiple_of(self.base+(1-bit)*s,16)
            self.base=pl.multiple_of(self.base+bit*s,16)
            self.cur=send(self.G.at[pl.ds(away,s)],self.bufs[self.k],dev)
        def advance(self):
            if self.k<4:
                self.cur.wait_recv()
                here=self.G.at[pl.ds(self.base,self.size)]
                add_into(here,self.bufs[self.k],self.size//2 if self.size%32==0 and self.size>=64 else self.size)
                self.k+=1
                if self.k<4: self._send(); return
                self.own=lc(here,self.O.at[pl.ds(self.base,self.size)])
                self.k=4
                self.cur=send(here,self.O.at[pl.ds(self.base,self.size)],n2)
                self.got=[self.cur]
            else:
                self.cur.wait_recv()
                if self.k==4: self.own.wait()
                dev,bit=self.steps[7-self.k]
                self.base=pl.multiple_of(self.base-bit*self.size,16)
                self.size*=2
                self.k+=1
                if self.k<8:
                    r=self.O.at[pl.ds(self.base,self.size)]
                    self.cur=send(r,r,self.steps[7-self.k][0])
    chunks=[Grads(G0,(C0,X0,U0,W0),go_o)]+[Grads(GP.at[p],(CP.at[p],XP.at[p],UP.at[p],WP.at[p]),gp_o.at[p]) for p in range(pairs)]

    l_rows.wait()
    rowsT[...]=rows[...].T
    l_db.wait(); l_wo.wait()
    datt[mine]=mm_nt(db[mine],wo[...])
    l_gu.wait(); l_gd.wait()
    r_cu.wait_recv(); r_cd.wait_recv()
    for j in range(nz):
        add_into(GU.at[j],cu.at[j],64); add_into(GD.at[j],cd.at[j],16)
    zz1=(z1+2)%nh; zz=z2
    r_z1=[send(GU.at[z1],zu.at[0],n1),send(GD.at[z1],zd.at[0],n1),send(GU.at[zz1],zu.at[1],n1),send(GD.at[zz1],zd.at[1],n1)]
    r_db.wait_recv()
    r_b1=[send(mlp_i.at[qy,B],mb.at[0],ny),send(mlp_i.at[qd,B],mb.at[1],ny)]
    datt[other]=mm_nt(db[other],wo[...])
    l_mixed.wait()
    G0[...]=mm_tn(mixed[...],db[...]).astype(BF)
    chunks[0].start()
    for k in (l_feat,l_proj,l_rden): k.wait()

    def pair(p):
        cc=slice(p*w,(p+1)*w)
        fq=feat[0,p]; fk=feat[1,p]
        dfq,dfk,dv=attend_back(fq,fk,proj[2,:,cc],mixed[:,cc],rden[:,cc],datt[:,cc],ones1,hd)
        parts=[]
        for t,(f,df) in enumerate(((fq,dfq),(fk,dfk))):
            du=feature_back(f,df,ones)
            GP[p,pl.ds(3*d+t*w,w)]=mm_tn(proj[t,:,cc],du).astype(BF)
            parts.append(mm_nt(du,w2[t,p]).astype(BF))
        parts.append(dv.astype(BF))
        for t in range(3): dproj[t,:,cc]=parts[t]
        g=mm(rowsT[...],jnp.concatenate(parts,axis=1)).astype(BF)
        for t in range(3): GP[p,pl.ds(t*d,d)]=g[:,t*w:(t+1)*w]
        chunks[1+p].start()

    def a_mid():
        for k in r_a1: k.wait_recv()
        add_into(ML.at[qo,A],ma.at[0],H); add_into(ML.at[qy,A],ma.at[1],H)
        return send(ML.at[qy,A],na,ny)
    def b_mid():
        for k in r_b1: k.wait_recv()
        add_into(ML.at[qo,B],mb.at[0],H); add_into(ML.at[qx,B],mb.at[1],H)
        return send(ML.at[qx,B],nb,nx)
    def z_mid():
        for k in r_z1: k.wait_recv()
        add_into(GU.at[zz],zu.at[1],64); add_into(GD.at[zz],zd.at[1],16)
        r=[send(GU.at[zz],yu,n2),send(GD.at[zz],yd,n2)]
        add_into(GU.at[z],zu.at[0],64); add_into(GD.at[z],zd.at[0],16)
        return r

    pair(0)
    chunks[0].advance()
    l_ml.wait()
    r_a2=a_mid()
    pair(1)
    chunks[1].advance(); chunks[0].advance()
    pair(2)
    chunks[2].advance(); chunks[1].advance(); chunks[0].advance()
    pair(3)
    chunks[3].advance(); chunks[2].advance(); chunks[1].advance()
    l_wq.wait()
    def first_grad(at):
        t=mm_nt(dproj[0,at],wq[0])+mm_nt(dproj[1,at],wq[1])
        return t+mm_nt(dproj[2,at],wq[2])
    t=first_grad(other)
    dfs[...]=t.astype(BF)
    r_df=send(dfs,dfr,ny)
    l_T.wait()
    xo,_=unit(T[other].astype(F32))
    gsum=jnp.sum(t*xo,axis=0,keepdims=True)
    t=first_grad(mine)
    dfo[...]=t
    xm,_=unit(T[mine].astype(F32))
    gsum=gsum+jnp.sum(t*xm,axis=0,keepdims=True)
    gn[...]=jnp.zeros_like(gn)
    gn[0,0:1]=gsum
    gn[0,1:2]=gn2[...]
    gains=[nc,nx,ny,n1,n2]; gk=[0]
    def gain_step():
        k=gk[0]
        r=send(gn.at[k],gr.at[k],gains[k])
        r.wait_recv()
        r.wait_send()
        gn[k+1]=gn[k]+gr[k]
        gk[0]+=1
    chunks[4].advance(); chunks[3].advance(); chunks[2].advance()
    r_z2=z_mid()
    r_b2=b_mid()
    chunks[0].advance(); chunks[1].advance()
    return_pending=None
    for k in (4,3,2): chunks[k].advance()
    for k in r_z2: k.wait_recv()
    add_into(GU.at[z],yu,64); add_into(GD.at[z],yd,16)
    qc=lambda q: pl.ds(pl.multiple_of(q*fs,fs),fs)
    uh=half(hu,c)
    rd=lambda q: gd_o.at[q,half(hw,c)]
    ru=lambda q: gu_o.at[uh,qc(q)]
    l_u=lc(GU.at[z],ru(qo)); l_d=lc(GD.at[z],rd(qo))
    r_x=[send(GU.at[z],ru(qo),nx),send(GD.at[z],rd(qo),nx)]
    r_y=[send(GU.at[z],ru(qo),ny),send(GD.at[z],rd(qo),ny)]
    for s in range(3,9):
        for k in range(5):
            if chunks[k].k<min(s,8): chunks[k].advance()
        if s==4:
            for k in r_x: k.wait_recv()
            r_y+=[send(ru(qx),ru(qx),ny),send(rd(qx),rd(qx),ny)]
        if s==6:
            for k in r_y: k.wait_recv()
            l_u.wait(); l_d.wait()
            r_c=[send(gu_o.at[uh],gu_o.at[uh],nc),send(gd_o.at[:,half(hw,c)],gd_o.at[:,half(hw,c)],nc)]
    for k in range(5):
        while chunks[k].k<8: chunks[k].advance()
    r_a2.wait_recv(); r_b2.wait_recv()
    l_mid.wait()
    for at,buf in ((A,na),(B,nb)):
        bo[at]=(mid[at]+(ML[qo,at].astype(F32)+buf[...].astype(F32))).astype(BF)
    lc(bo,bo_o,True)
    r_df.wait_recv()
    l_dm.wait()
    dx,_=norm_back(T[mine].astype(F32),dfo[...]+dfr[...].astype(F32),g1[...])
    gt[...]=dmid[...]+dx
    lc(gt,gt_o,True)
    for _ in gains: gain_step()
    gn_o[...]=gn[len(gains)]
    for k in r_c: k.wait_recv()
    for k in wires.all[:len(wires.all)-len(gains)]: k.wait_send()
    for k in pend: k.wait()

def k3(dbr,tok,rows,wqkv,wf,wout,proj,feat,mixed,rden,g1,dmid,mid,mlp,gu,gd,gn2):
    R,d=dbr.shape; n=2*R; c=wout.shape[0]; h=wf.shape[1]; hd=wf.shape[-1]; pairs=h//2
    nz,_,fs=gu.shape; f=nz*fs; w=2*hd; q=3*d+2*w
    V=pltpu.VMEM; D=pltpu.SemaphoreType.DMA
    like=lambda a: V(a.shape,a.dtype)
    return pl.pallas_call(k3_kernel,
      out_shape=(S((R,d),BF),S((R,d),F32),S((c,d),BF),S((pairs,q,w),BF),S((d,f),BF),S((4,fs,d),BF),S((8,d),F32)),
      in_specs=[ANY,ANY,ANY,ANY,VM,ANY,ANY,ANY,ANY,ANY,VM,ANY,ANY,ANY,ANY,ANY,VM],
      out_specs=[ANY]*6+[VM],
      scratch_shapes=[V((n,d),BF),like(tok),like(rows),V((d,n),BF),like(wqkv),like(wout),like(proj),like(feat),like(mixed),like(rden),
        V((n,c),F32),like(proj),like(dmid),like(mid),
        V((c,d),BF),V((pairs,q,w),BF),V((c//2,d),BF),V((pairs,q//2,w),BF),V((c//4,d),BF),V((pairs,q//4,w),BF),
        V((c//8,d),BF),V((pairs,q//8,w),BF),V((c//16,d),BF),V((pairs,q//16,w),BF),
        V((nz,d//2,fs),BF),V((nz,fs//2,d),BF),V((nz,d//2,fs),BF),V((nz,fs//2,d),BF),V((2,d//2,fs),BF),V((2,fs//2,d),BF),
        V((d//2,fs),BF),V((fs//2,d),BF),
        like(mlp),V((2,R//2,d),BF),V((2,R//2,d),BF),V((R//2,d),BF),V((R//2,d),BF),V((R,d),BF),
        V((R,d),F32),V((R,d),BF),V((R,d),BF),V((R,d),F32),V((6,8,d),F32),V((5,8,d),F32),
        V((2,pairs,w,w),BF),D((40,)),D((2,80))],
      compiler_params=pltpu.CompilerParams(vmem_limit_bytes=60*2**20,collective_id=3,has_side_effects=True),
      cost_estimate=pl.CostEstimate(flops=8*10**9,bytes_accessed=40*10**6,transcendentals=10**6))(
      dbr,tok,rows,wqkv,wf,wout,proj,feat,mixed,rden,g1,dmid,mid,mlp,gu,gd,gn2)

def per_device_k1(
    tokens, lengths, norm_first, w_qkv, w_feature, w_out, norm_second, w_up, w_down, cotangent
):
    wqkv=jnp.transpose(w_qkv,(1,0,2))
    tok,first_rows,proj,feat,mixed,rden,middle,second_low,wu,wd,cot_all=k1(lengths,tokens[0],norm_first[None],wqkv,w_feature,w_out,norm_second[None],w_up,w_down,cotangent[0])
    d_middle,d_branch_low,gn2,mlp,gu,gd=k2(second_low,middle,cot_all,wu,wd,norm_second[None])
    block_out,grad_tokens,go,gp,gu,gd,gn=k3(d_branch_low,tok,first_rows,wqkv,w_feature,w_out,proj,feat,mixed,rden,norm_first[None],d_middle,middle,mlp,gu,gd,gn2)
    d=tokens.shape[2]; h=w_feature.shape[1]; hd=w_feature.shape[3]; w=2*hd
    gq=jnp.transpose(gp[:,:3*d].reshape(h//2,3,d,w),(2,1,0,3)).reshape(d,3,h*hd).astype(F32)
    t=gp[:,3*d:].reshape(h//2,2,2,hd,2,hd)
    gf=jnp.stack([t[:,:,0,:,0],t[:,:,1,:,1]],axis=2)
    gf=jnp.transpose(gf,(1,0,2,3,4)).reshape(2,h,hd,hd).astype(F32)
    return (
        block_out[None],
        grad_tokens[None],
        gn[0],
        gq,
        gf,
        go.astype(F32),
        gn[1],
        gu.astype(F32),
        gd.reshape(gd.shape[0]*gd.shape[1],-1).astype(F32),
    )


def solution(mesh):
    in_specs = (
        P(("dp", "hidden"), "head", None),
        P(("dp", "hidden"), None),
        P(),
        P(None, None, "head"),
        P(None, "head", None, None),
        P("head", None),
        P(),
        P(None, "hidden"),
        P("hidden", None),
        P(("dp", "hidden"), "head", None),
    )
    out_specs = (
        P(("dp", "hidden"), "head", None),
        P(("dp", "hidden"), "head", None),
        P(),
        P(None, None, "head"),
        P(None, "head", None, None),
        P("head", None),
        P(),
        P(None, "hidden"),
        P("hidden", None),
    )
    near=dict(mesh.shape)=={"dp":4,"head":2,"hidden":4}
    return jax.shard_map(
        per_device_k1 if near else per_device, mesh=mesh, in_specs=in_specs, out_specs=out_specs, check_vma=False
    )
```

```python
import jax, jax.numpy as jnp
from jax import lax
from jax.experimental import pallas as pl
from jax.experimental.pallas import tpu as pltpu
from jax.sharding import PartitionSpec as P
BF=jnp.bfloat16; F32=jnp.float32
NT=(((1,),(1,)),((),()))
TN=(((0,),(0,)),((),()))
SB=256

def mm(a,b): return jnp.dot(a,b,preferred_element_type=F32)
def mm_nt(a,b): return lax.dot_general(a,b,NT,preferred_element_type=F32)
def mm_tn(a,b): return lax.dot_general(a,b,TN,preferred_element_type=F32)

def half_ones(width, size):
    r=lax.broadcasted_iota(jnp.int32,(width,width),0)//size
    c=lax.broadcasted_iota(jnp.int32,(width,width),1)//size
    return (r==c).astype(F32).astype(BF)

def first_half(shape, size):
    return lax.broadcasted_iota(jnp.int32,shape,1)%(2*size) < size

def half_sum(t, ones):
    hi=t.astype(BF); lo=(t-hi.astype(F32)).astype(BF)
    return mm(hi,ones)+mm(lo,ones)

def features(x, w2, ones, size):
    u=mm(x,w2)
    h0=first_half(u.shape,size)
    big=jnp.float32(3e38)
    def both(f, fill):
        return jnp.where(h0, f(jnp.where(h0,u,fill)), f(jnp.where(h0,fill,u)))
    top=both(lambda t: jnp.max(t,axis=1,keepdims=True), -big)
    low=both(lambda t: jnp.min(t,axis=1,keepdims=True), big)
    e=jnp.concatenate([jnp.exp(u-top),jnp.exp(low-u)],axis=1)
    s=mm(e.astype(BF),ones)
    return e/s

def halves(t, h0):
    z=jnp.zeros_like(t)
    return jnp.where(h0,t,z), jnp.where(h0,z,t)

def attend(fq, fk, v, size):
    n=fq.shape[0]
    h0=first_half(fq.shape,size)
    fqs=halves(fq,h0)
    hv=first_half(v.shape,size)
    one=jnp.ones(v.shape,BF)
    ve=halves(jnp.concatenate([v,one],axis=1),h0)
    outs=[]
    for r in range(0,n,SB):
        ext=r+SB
        keep=(lax.broadcasted_iota(jnp.int32,(SB,ext),0)+r)>=lax.broadcasted_iota(jnp.int32,(SB,ext),1)
        acc=None
        for s in range(2):
            sc=mm_nt(fqs[s][r:r+SB],fk[:ext])
            sc=jnp.where(keep,sc,0.0).astype(BF)
            t=mm(sc,ve[s][:ext])
            acc=t if acc is None else acc+t
        outs.append(acc)
    p=jnp.concatenate(outs,axis=0)
    w=v.shape[1]
    rden=1.0/p[:,w:]
    return p[:,:w]*rden, rden

def attend_back(fq,fk,v,mixed,rden,datt,ones,size):
    n,w=v.shape
    wide=(n,2*w)
    h0=first_half(wide,size)
    dn=(datt*rden).astype(BF)
    dd=-half_sum(datt*mixed.astype(F32),ones)*rden
    hi=dd.astype(BF); lo=(dd-hi.astype(F32)).astype(BF)
    lane=lax.broadcasted_iota(jnp.int32,(n,w),1)%size
    zero=jnp.zeros((n,w),BF)
    ext_=jnp.where(lane==0,hi,jnp.where(lane==1,lo,zero))
    nx=halves(jnp.concatenate([dn,ext_],axis=1),h0)
    vx=jnp.concatenate([v,jnp.ones((n,w),BF)],axis=1)
    fqs=halves(fq,h0); fks=halves(fk,h0)
    dfq=[];dfk=[];dv=[]
    for r in range(0,n,SB):
        ext=r+SB
        keep=(lax.broadcasted_iota(jnp.int32,(SB,ext),0)+r)>=lax.broadcasted_iota(jnp.int32,(SB,ext),1)
        acc=0.0
        for s in range(2):
            ds=jnp.where(keep,mm_nt(nx[s][r:r+SB],vx[:ext]),0.0).astype(BF)
            acc=acc+mm(ds,fks[s][:ext])
        dfq.append(acc)
        left=n-r
        keep=lax.broadcasted_iota(jnp.int32,(SB,left),0)<=lax.broadcasted_iota(jnp.int32,(SB,left),1)
        ak=0.0; av=0.0
        for s in range(2):
            ds=jnp.where(keep,mm_nt(vx[r:r+SB],nx[s][r:]),0.0).astype(BF)
            ak=ak+mm(ds,fqs[s][r:])
            sc=jnp.where(keep,mm_nt(fk[r:r+SB],fqs[s][r:]),0.0).astype(BF)
            av=av+mm(sc,nx[s][r:,:w])
        dfk.append(ak); dv.append(av)
    cat=lambda t: jnp.concatenate(t,axis=0)
    return cat(dfq),cat(dfk),cat(dv)

def feature_back(f, df, ones):
    w=f.shape[1]//2
    f=f.astype(F32)
    part=f*(df-half_sum(f*df,ones))
    return (part[:,:w]-part[:,w:]).astype(BF)

def pair_weights(wf_ref, w2_ref):
    hd=wf_ref.shape[-1]
    w2_ref[...]=jnp.zeros_like(w2_ref)
    for t in range(2):
        for p in range(w2_ref.shape[1]):
            w2_ref[t,p,:hd,:hd]=wf_ref[t,2*p]
            w2_ref[t,p,hd:,hd:]=wf_ref[t,2*p+1]

def fwd_kernel(len_ref, rows_ref, wqkv_ref, wf_ref, wout_ref, proj_ref, feat_ref, mixed_ref, rden_ref, branch_ref, w2_ref):
    hd=wf_ref.shape[-1]; w=2*hd; n=rows_ref.shape[0]; pairs=w2_ref.shape[1]
    pair_weights(wf_ref,w2_ref)
    for i in range(3):
        proj_ref[i]=mm(rows_ref[...],wqkv_ref[i]).astype(BF)
    ones=half_ones(2*w,hd)
    valid=lax.broadcasted_iota(jnp.int32,(n,2*w),0)<len_ref[0,0]
    def body(p,_):
        c=pl.ds(pl.multiple_of(p*w,w),w)
        fq=features(proj_ref[0,:,c],w2_ref[0,p],ones,hd).astype(BF)
        fk=jnp.where(valid,features(proj_ref[1,:,c],w2_ref[1,p],ones,hd),0.0).astype(BF)
        feat_ref[0,p]=fq; feat_ref[1,p]=fk
        m,rd=attend(fq,fk,proj_ref[2,:,c],hd)
        mixed_ref[:,c]=m.astype(BF); rden_ref[:,c]=rd
        return 0
    lax.fori_loop(0,pairs,body,0)
    branch_ref[...]=mm(mixed_ref[...],wout_ref[...]).astype(branch_ref.dtype)

def bwd_kernel(rows_ref,wqkv_ref,wf_ref,wout_ref,proj_ref,feat_ref,mixed_ref,rden_ref,dbr_ref,
               gq_ref,gf_ref,go_ref,dfirst_ref,w2_ref,datt_ref,dproj_ref):
    hd=wf_ref.shape[-1]; w=2*hd; n=rows_ref.shape[0]; pairs=w2_ref.shape[1]
    pair_weights(wf_ref,w2_ref)
    ones=half_ones(2*w,hd); ones1=half_ones(w,hd)
    datt_ref[...]=mm_nt(dbr_ref[...],wout_ref[...])
    go_ref[...]=mm_tn(mixed_ref[...],dbr_ref[...]).astype(go_ref.dtype)
    def body(p,_):
        c=pl.ds(pl.multiple_of(p*w,w),w)
        fq=feat_ref[0,p]; fk=feat_ref[1,p]
        dfq,dfk,dv=attend_back(fq,fk,proj_ref[2,:,c],mixed_ref[:,c],rden_ref[:,c],datt_ref[:,c],ones1,hd)
        for t,(f,df) in enumerate(((fq,dfq),(fk,dfk))):
            du=feature_back(f,df,ones)
            g=mm_tn(proj_ref[t,:,c],du)
            gf_ref[t,2*p]=g[:hd,:hd].astype(gf_ref.dtype); gf_ref[t,2*p+1]=g[hd:,hd:].astype(gf_ref.dtype)
            dproj_ref[t,:,c]=mm_nt(du,w2_ref[t,p]).astype(BF)
        dproj_ref[2,:,c]=dv.astype(BF)
        return 0
    lax.fori_loop(0,pairs,body,0)
    acc=None
    for i in range(3):
        gq_ref[i]=mm_tn(rows_ref[...],dproj_ref[i]).astype(gq_ref.dtype)
        t=mm_nt(dproj_ref[i],wqkv_ref[i])
        acc=t if acc is None else acc+t
    dfirst_ref[...]=acc.astype(dfirst_ref.dtype)
VM=pl.BlockSpec(memory_space=pltpu.VMEM)
SM=pl.BlockSpec(memory_space=pltpu.SMEM)
S=jax.ShapeDtypeStruct
def fwd(length,rows,wqkv,wf,wout):
    n,d=rows.shape; c=wout.shape[0]; h=wf.shape[1]; hd=wf.shape[-1]
    return pl.pallas_call(fwd_kernel,
      out_shape=(S((3,n,c),BF),S((2,h//2,n,4*hd),BF),S((n,c),BF),S((n,c),F32),S((n,d),BF)),
      in_specs=[SM,VM,VM,VM,VM],out_specs=[VM]*5,
      scratch_shapes=[pltpu.VMEM((2,h//2,2*hd,2*hd),BF)],
      compiler_params=pltpu.CompilerParams(vmem_limit_bytes=56*2**20))(length,rows,wqkv,wf,wout)
def bwd(rows,wqkv,wf,wout,proj,feat,mixed,rden,dbr):
    n,d=rows.shape; c=wout.shape[0]; h=wf.shape[1]; hd=wf.shape[-1]
    return pl.pallas_call(bwd_kernel,
      out_shape=(S((3,d,c),BF),S((2,h,hd,hd),F32),S((c,d),BF),S((n,d),BF)),
      in_specs=[VM]*9,out_specs=[VM]*4,
      scratch_shapes=[pltpu.VMEM((2,h//2,2*hd,2*hd),BF),pltpu.VMEM((n,c),F32),pltpu.VMEM((3,n,c),BF)],
      compiler_params=pltpu.CompilerParams(vmem_limit_bytes=56*2**20))(rows,wqkv,wf,wout,proj,feat,mixed,rden,dbr)

EPS=1e-05

def normalize(values, gain):
    average = jnp.mean(values, axis=-1, keepdims=True)
    centred = values - average
    spread = jnp.mean(centred * centred, axis=-1, keepdims=True)
    return centred * lax.rsqrt(spread + EPS) * gain

def smooth_gate(values):
    return jax.nn.gelu(values, approximate=True)

def per_device(
    tokens, lengths, norm_first, w_qkv, w_feature, w_out, norm_second, w_up, w_down, cotangent
):
    wqkv=jnp.transpose(w_qkv,(1,0,2))
    residual_in = tokens[0].astype(jnp.float32)
    normed_first, first_back = jax.vjp(normalize, residual_in, norm_first)
    first_low = normed_first.astype(jnp.bfloat16)
    first_rows = lax.all_gather(first_low, "head", axis=0, tiled=True)
    cot_low = cotangent[0]
    cot_rows = lax.all_gather(cot_low, "hidden", axis=0, tiled=True)
    proj,feat,mixed,rden,part=fwd(lengths,first_rows,wqkv,w_feature,w_out)
    branch = lax.psum_scatter(part, "head", scatter_dimension=0, tiled=True).astype(jnp.float32)
    middle = residual_in + branch
    normed_second, second_back = jax.vjp(normalize, middle, norm_second)
    second_low = normed_second.astype(jnp.bfloat16)
    second_rows = lax.all_gather(second_low, "hidden", axis=0, tiled=True)
    hidden_pre = jnp.dot(second_rows, w_up, preferred_element_type=jnp.float32)
    active = smooth_gate(hidden_pre).astype(jnp.bfloat16)
    gate_grad = jax.vjp(smooth_gate, hidden_pre)[1]
    d_active = jnp.einsum("nd,fd->nf", cot_rows, w_down, preferred_element_type=jnp.float32)
    d_pre = gate_grad(d_active)[0].astype(jnp.bfloat16)
    d_second = lax.psum_scatter(
        jnp.einsum("nf,df->nd", d_pre, w_up, preferred_element_type=jnp.float32).astype(jnp.bfloat16),
        "hidden",
        scatter_dimension=0,
        tiled=True,
    ).astype(jnp.float32)
    mlp_result = lax.psum_scatter(
        jnp.dot(active, w_down, preferred_element_type=jnp.float32).astype(jnp.bfloat16),
        "hidden",
        scatter_dimension=0,
        tiled=True,
    ).astype(jnp.float32)
    block_out = (middle + mlp_result).astype(jnp.bfloat16)
    grad_down = jnp.einsum("nf,nd->fd", active, cot_rows, preferred_element_type=jnp.float32)
    grad_up = jnp.einsum("nd,nf->df", second_rows, d_pre, preferred_element_type=jnp.float32)
    d_middle_norm, grad_norm_second = second_back(d_second)
    d_middle = cot_low.astype(jnp.float32) + d_middle_norm
    d_branch_rows = lax.all_gather(d_middle.astype(jnp.bfloat16), "head", axis=0, tiled=True)
    gq,grad_feature,go,dfirst=bwd(first_rows,wqkv,w_feature,w_out,proj,feat,mixed,rden,d_branch_rows)
    d_first = lax.psum_scatter(dfirst, "head", scatter_dimension=0, tiled=True).astype(jnp.float32)
    d_input_norm, grad_norm_first = first_back(d_first)
    grad_tokens = d_middle + d_input_norm
    grad_up, grad_down = (
        lax.psum(grad_up.astype(jnp.bfloat16), ("dp", "head")).astype(jnp.float32),
        lax.psum(grad_down.astype(jnp.bfloat16), ("dp", "head")).astype(jnp.float32),
    )
    gq, grad_feature, go = (
        lax.psum(gq, ("dp", "hidden")).astype(jnp.float32),
        lax.psum(grad_feature.astype(jnp.bfloat16), ("dp", "hidden")).astype(jnp.float32),
        lax.psum(go, ("dp", "hidden")).astype(jnp.float32),
    )
    grad_norm_first, grad_norm_second = lax.psum(
        (grad_norm_first, grad_norm_second), ("dp", "head", "hidden")
    )
    return (
        block_out[None],
        grad_tokens[None],
        grad_norm_first,
        jnp.transpose(gq,(1,0,2)),
        grad_feature,
        go,
        grad_norm_second,
        grad_up,
        grad_down,
    )


MESH=pl.DeviceIdType.MESH
ANY=pl.BlockSpec(memory_space=pl.ANY)
EPS=1e-05

def place():
    dp=lax.axis_index("dp")
    return dp//2, dp%2, lax.axis_index("head"), lax.axis_index("hidden")

def around():
    x,c,y,z=place()
    return ((1-x)*2+c,y,z), (x*2+c,1-y,z), (x*2+1-c,y,z)

def along(step):
    x,c,y,z=place()
    return (x*2+c,y,z+step)

def remote(src,dst,sems,i,dev):
    return pltpu.make_async_remote_copy(src_ref=src,dst_ref=dst,send_sem=sems.at[0,i],recv_sem=sems.at[1,i],device_id=dev,device_id_type=MESH)

def greet(peers, line):
    _,_,_,z=place()
    last=lax.axis_size("hidden")-1
    bar=pltpu.get_barrier_semaphore()
    for d in peers:
        pl.semaphore_signal(bar,inc=1,device_id=d,device_id_type=MESH)
    count=len(peers)
    if line:
        for step in (1,-1):
            @pl.when((z<last) if step==1 else (z>0))
            def _():
                pl.semaphore_signal(bar,inc=1,device_id=along(step),device_id_type=MESH)
        count=count+jnp.where(z<last,1,0)+jnp.where(z>0,1,0)
    pl.semaphore_wait(bar,count)

def unit(values):
    centred=values-jnp.mean(values,axis=-1,keepdims=True)
    r=lax.rsqrt(jnp.mean(centred*centred,axis=-1,keepdims=True)+EPS)
    return centred*r, r

def k1_kernel(len_ref,tok,g1,wqkv,wf,wout,g2,wup,wdn,cot,
              tok_o,rows_o,proj_o,feat_o,mixed_o,rden_o,mid_o,sec_o,wu_o,wd_o,cot_o,
              T,rows,wq,wo,proj,feat,mixed,rden,own,snd,rcv,mid,sec,w2,loc,rem,zr,zl,dd):
    x,c,y,z=place()
    last=lax.axis_size("hidden")-1
    nx,ny,nc=around()
    R=tok.shape[0]; n=2*R; d=tok.shape[1]
    hd=wf.shape[-1]; w=2*hd; pairs=w2.shape[1]
    q=x*2+y
    lc=lambda s,t,i: pltpu.make_async_copy(s,t,loc.at[i])
    mine=pl.ds(pl.multiple_of(y*R,R),R); other=pl.ds(pl.multiple_of((1-y)*R,R),R)
    fs=wup.shape[1]//4
    cols=pl.ds(pl.multiple_of(q*fs,fs),fs)
    hu=wup.shape[0]//2; hw=fs//2
    uh=pl.ds(pl.multiple_of(c*hu,hu),hu); dh=pl.ds(pl.multiple_of(c*hw,hw),hw)
    l_tok=lc(tok,T.at[mine],0); l_wq=[lc(wqkv.at[i],wq.at[i],1+i) for i in range(3)]; l_wo=lc(wout,wo,4)
    l_tok.start()
    for k in l_wq: k.start()
    greet((nx,ny,nc),True)
    r_tok=remote(tok,T.at[mine],rem,0,ny)
    r_tok.start()
    def z_copies(s,right):
        j=(z-s+1) if right else (z+s-1)
        sems,dev=(zr,along(1)) if right else (zl,along(-1))
        if s==1:
            su=wup.at[uh,cols]
            sd=wdn.at[pl.ds(pl.multiple_of(q*fs+c*hw,hw),hw)]
        else:
            su=wu_o.at[j,uh]; sd=wd_o.at[j,dh]
        return [remote(su,wu_o.at[j,uh],sems,2*(s-1),dev),remote(sd,wd_o.at[j,dh],sems,2*(s-1)+1,dev)]
    def z_send(s):
        for right in (True,False):
            ok=((z<last)&(z-s+1>=0)) if right else ((z>0)&(z+s-1<=last))
            @pl.when(ok)
            def _():
                for k in z_copies(s,right): k.start()
    def z_recv(s):
        for right in (True,False):
            ok=(z-s>=0) if right else (z+s<=last)
            j=(z-s) if right else (z+s)
            @pl.when(ok)
            def _():
                jj=jnp.clip(j,0,last)
                sems=zr if right else zl
                remote(wu_o.at[jj,uh],wu_o.at[jj,uh],sems,2*(s-1),nc).wait_recv()
                remote(wd_o.at[jj,dh],wd_o.at[jj,dh],sems,2*(s-1)+1,nc).wait_recv()
                i=2*(s-1)+(0 if right else 2*last)
                remote(wu_o.at[jj,uh],wu_o.at[jj,uh],dd,i,nc).start()
                remote(wd_o.at[jj,dh],wd_o.at[jj,dh],dd,i+1,nc).start()
    def z_end():
        for s in range(1,last+1):
            for right in (True,False):
                ok=((z<last)&(z-s+1>=0)) if right else ((z>0)&(z+s-1<=last))
                @pl.when(ok)
                def _():
                    for k in z_copies(s,right): k.wait_send()
                got=(z-s>=0) if right else (z+s<=last)
                j=(z-s) if right else (z+s)
                @pl.when(got)
                def _():
                    jj=jnp.clip(j,0,last)
                    i=2*(s-1)+(0 if right else 2*last)
                    co=1-c
                    ou=pl.ds(pl.multiple_of(co*hu,hu),hu); od=pl.ds(pl.multiple_of(co*hw,hw),hw)
                    remote(wu_o.at[jj,uh],wu_o.at[jj,ou],dd,i,nc).wait()
                    remote(wd_o.at[jj,dh],wd_o.at[jj,od],dd,i+1,nc).wait()
    z_send(1)
    r_cx=remote(cot,cot_o.at[q],rem,1,nx)
    r_cx.start()
    l_wo.start()
    pair_weights(wf,w2)
    ones=half_ones(2*w,hd)
    def first(at):
        xh,_=unit(T[at].astype(F32))
        rows[at]=(xh*g1[...]).astype(BF)
    def project(at):
        for i in range(3): proj[i,at]=mm(rows[at],wq[i]).astype(BF)
    l_tok.wait()
    first(mine)
    for k in l_wq: k.wait()
    project(mine)
    r_tok.wait_recv()
    z_recv(1)
    z_send(2)
    r_cy=remote(cot,cot_o.at[q],rem,2,ny)
    r_cy.start()
    l_tok_o=lc(T,tok_o,8); l_tok_o.start()
    first(other)
    l_rows=lc(rows,rows_o,9); l_rows.start()
    project(other)
    l_proj=lc(proj,proj_o,10); l_proj.start()
    valid=lax.broadcasted_iota(jnp.int32,(n,2*w),0)<len_ref[0,0]
    def body(p,_):
        cc=pl.ds(pl.multiple_of(p*w,w),w)
        fq=features(proj[0,:,cc],w2[0,p],ones,hd).astype(BF)
        fk=jnp.where(valid,features(proj[1,:,cc],w2[1,p],ones,hd),0.0).astype(BF)
        feat[0,p]=fq; feat[1,p]=fk
        m,rd=attend(fq,fk,proj[2,:,cc],hd)
        mixed[:,cc]=m.astype(BF); rden[:,cc]=rd
        return 0
    lax.fori_loop(0,pairs,body,0)
    l_wo.wait()
    snd[...]=mm(mixed[other],wo[...]).astype(BF)
    r_part=remote(snd,rcv,rem,3,ny)
    r_part.start()
    z_recv(2)
    z_send(3)
    own[...]=mm(mixed[mine],wo[...])
    l_feat=lc(feat,feat_o,11); l_mixed=lc(mixed,mixed_o,12); l_rden=lc(rden,rden_o,13)
    for k in (l_feat,l_mixed,l_rden): k.start()
    r_cy.wait_recv()
    yq=x*2+1-y
    r_cf=remote(cot_o.at[yq],cot_o.at[yq],rem,4,nx)
    r_cf.start()
    r_part.wait_recv()
    middle=T[mine].astype(F32)+(own[...]+rcv[...].astype(F32))
    mid[...]=middle
    xh,_=unit(middle)
    sec[...]=(xh*g2[...]).astype(BF)
    l_mid=lc(mid,mid_o,14); l_sec=lc(sec,sec_o,15)
    l_mid.start(); l_sec.start()
    z_recv(3)
    r_cx.wait_recv(); r_cf.wait_recv()
    for k in (r_tok,r_cx,r_cy,r_part,r_cf): k.wait_send()
    z_end()
    for k in (l_tok_o,l_rows,l_proj,l_feat,l_mixed,l_rden,l_mid,l_sec): k.wait()

def k1(length,tok,g1,wqkv,wf,wout,g2,wup,wdn,cot):
    R,d=tok.shape; n=2*R; c=wout.shape[0]; h=wf.shape[1]; hd=wf.shape[-1]; f=wup.shape[1]
    last=lax.axis_size("hidden")-1
    big=[S((n,d),BF),S((n,d),BF),S((3,n,c),BF),S((2,h//2,n,4*hd),BF),S((n,c),BF),S((n,c),F32),S((R,d),F32),S((R,d),BF)]
    vm=[pltpu.VMEM(s.shape,s.dtype) for s in big]
    T,rows,proj,feat,mixed,rden,mid,sec=vm
    D=pltpu.SemaphoreType.DMA
    return pl.pallas_call(k1_kernel,
      out_shape=tuple(big+[S((last+1,d,f//4),BF),S((last+1,f//4,d),BF),S((4,R,d),BF)]),
      in_specs=[SM,ANY,VM,ANY,VM,ANY,VM,ANY,ANY,ANY],out_specs=[ANY]*11,
      scratch_shapes=[T,rows,pltpu.VMEM((3,d,c),BF),pltpu.VMEM((c,d),BF),proj,feat,mixed,rden,
        pltpu.VMEM((R,d),F32),pltpu.VMEM((R,d),BF),pltpu.VMEM((R,d),BF),mid,sec,
        pltpu.VMEM((2,h//2,2*hd,2*hd),BF),D((16,)),D((2,5)),D((2,2*last)),D((2,2*last)),D((2,4*last))],
      compiler_params=pltpu.CompilerParams(vmem_limit_bytes=62*2**20,collective_id=1,has_side_effects=True),
      cost_estimate=pl.CostEstimate(flops=4*10**9,bytes_accessed=30*10**6,transcendentals=10**6))(
      length,tok,g1,wqkv,wf,wout,g2,wup,wdn,cot)

def add_into(dst,src,step):
    rows=dst.shape[0]
    def body(i,_):
        r=pl.ds(pl.multiple_of(i*step,step),step)
        dst[r]=(dst[r].astype(F32)+src[r].astype(F32)).astype(dst.dtype)
        return 0
    lax.fori_loop(0,rows//step,body,0)

def gate(v):
    k=0.7978845608; a=0.044715
    sq=v*v
    t=jnp.tanh(k*v*(1.0+a*sq))
    half=0.5*(1.0+t)
    return v*half, half+0.5*v*(1.0-t*t)*(k+(3.0*a*k)*sq)

def norm_back(values,grad,gain):
    xh,r=unit(values)
    e=grad*gain
    inner=e-jnp.mean(e,axis=-1,keepdims=True)-xh*jnp.mean(e*xh,axis=-1,keepdims=True)
    return r*inner, jnp.sum(grad*xh,axis=0,keepdims=True)

def k2_kernel(sec,mid,cots,cot,wu,wd,wup,wdn,g2,
              dmid_o,dbr_o,gn_o,mlp_o,gu_o,gd_o,
              SA,CA,Wu,Wd,act,dpre,P,mlp,gu,gd,midv,dmid,dbr,own,rx,ry,rdx,rdy,cu,cd,zu,loc,ag,rs):
    x,c,y,z=place()
    nx,ny,nc=around()
    nh=lax.axis_size("hidden")
    z1,z2=z+1-2*(z%2),(z+2)%nh
    n1=(x*2+c,y,z1)
    R,d=sec.shape; H=R//2; fs=wu.shape[2]; nz=wu.shape[0]
    qo,qx,qy,qd=x*2+y,(1-x)*2+y,x*2+1-y,(1-x)*2+1-y
    lc=lambda s,t,i: pltpu.make_async_copy(s,t,loc.at[i])
    l_sec=lc(sec,SA.at[qo],0)
    at=lambda j: pl.ds(pl.multiple_of(j*fs,fs),fs)
    l_wu=[lc(wup.at[:,at(qo)],Wu.at[:,at(z)],1)]; l_wd=[lc(wdn.at[at(qo)],Wd.at[at(z)],2)]
    for t in range(1,nz):
        j=(z+t)%nz
        l_wu.append(lc(wu.at[j],Wu.at[:,at(j)],2*t+1)); l_wd.append(lc(wd.at[j],Wd.at[at(j)],2*t+2))
    l_cot=[lc(cot,CA.at[qo],2*nz+1)]+[lc(cots.at[q],CA.at[q],2*nz+2+i) for i,q in enumerate((qx,qy,qd))]
    l_mid=lc(mid,midv,2*nz+5)
    l_sec.start()
    for k in l_wu: k.start()
    greet((nx,ny,nc,n1),False)
    A=pl.ds(0,H); B=pl.ds(H,H)
    xa=remote(sec.at[A],SA.at[qo,A],ag,0,nx); xb=remote(sec.at[B],SA.at[qo,B],ag,1,nx)
    yb=remote(sec.at[B],SA.at[qo,B],ag,2,ny); ya=remote(sec.at[A],SA.at[qo,A],ag,3,ny)
    for k in (xa,yb,xb,ya): k.start()
    for k in l_wd+l_cot: k.start()
    l_mid.start()
    def block(qi,keep):
        hp=mm(SA[qi],Wu[...])
        a,ga=gate(hp)
        act[qi]=a.astype(BF)
        dp=(mm_nt(CA[qi],Wd[...])*ga).astype(BF)
        dpre[qi]=dp
        d2=mm_nt(dp,Wu[...])
        if keep: own[...]=d2
        else: P[qi]=d2.astype(BF)
    def down(qi): mlp[qi]=mm(act[qi],Wd[...]).astype(BF)
    l_sec.wait()
    for k in l_wu: k.wait()
    for k in l_cot+l_wd: k.wait()
    block(qo,True)
    xa.wait_recv()
    fa=remote(SA.at[qx,A],SA.at[qx,A],ag,4,ny); fa.start()
    yb.wait_recv()
    fb=remote(SA.at[qy,B],SA.at[qy,B],ag,5,nx); fb.start()
    down(qo)
    xb.wait_recv()
    block(qx,False)
    p_xa=remote(P.at[qx,A],rx.at[A],rs,0,nx); p_xa.start()
    ya.wait_recv()
    block(qy,False)
    p_yb=remote(P.at[qy,B],ry.at[B],rs,1,ny); p_yb.start()
    fa.wait_recv(); fb.wait_recv()
    block(qd,False)
    p_da=remote(P.at[qd,A],rdx,rs,2,nx); p_da.start()
    p_db=remote(P.at[qd,B],rdy,rs,3,ny); p_db.start()
    rows=4*R
    hu,hw=d//2,fs//2
    half=lambda size,b: pl.ds(pl.multiple_of(b*size,size),size)
    uo,ua,do,da=half(hu,c),half(hu,1-c),half(hw,c),half(hw,1-c)
    sa=SA[...].reshape(rows,-1)
    for j in range(nz//2):
        cc=pl.ds(2*j*fs,2*fs)
        t=mm_tn(sa,dpre[:,:,cc].reshape(rows,-1)).astype(BF)
        gu[2*j]=t[:,:fs]; gu[2*j+1]=t[:,fs:]
    k_u=remote(gu.at[:,ua],cu,rs,6,nc); k_u.start()
    down(qx); down(qy); down(qd)
    l_mlp=lc(mlp,mlp_o,2*nz+6); l_mlp.start()
    k_u.wait_recv()
    for j in range(nz): add_into(gu.at[j,uo],cu.at[j],64)
    zz1=(z1+2)%nh
    k_z=[remote(gu.at[z1,uo],zu.at[0],rs,7,n1),remote(gu.at[zz1,uo],zu.at[1],rs,8,n1)]
    for k in k_z: k.start()
    p_da.wait_recv()
    P[qy,A]=(P[qy,A].astype(F32)+rdx[...].astype(F32)).astype(BF)
    p_ya=remote(P.at[qy,A],ry.at[A],rs,4,ny); p_ya.start()
    p_db.wait_recv()
    P[qx,B]=(P[qx,B].astype(F32)+rdy[...].astype(F32)).astype(BF)
    p_xb=remote(P.at[qx,B],rx.at[B],rs,5,nx); p_xb.start()
    ca=CA[...].reshape(rows,-1)
    for j in range(nz):
        gd[j]=mm_tn(act[:,:,pl.ds(j*fs,fs)].reshape(rows,-1),ca).astype(BF)
    k_d=remote(gd.at[:,da],cd,rs,9,nc); k_d.start()
    l_mid.wait()
    for k in (p_xa,p_xb,p_ya,p_yb): k.wait_recv()
    ds=own[...]+(rx[...].astype(F32)+ry[...].astype(F32))
    dx,gn=norm_back(midv[...],ds,g2[...])
    gn_o[...]=gn
    dm=CA[qo].astype(F32)+dx
    dmid[...]=dm; dbr[...]=dm.astype(BF)
    l_dm=lc(dmid,dmid_o,2*nz+9); l_db=lc(dbr,dbr_o,2*nz+10)
    l_dm.start(); l_db.start()
    k_d.wait_recv()
    for j in range(nz): add_into(gd.at[j,do],cd.at[j],16)
    l_gd=lc(gd.at[:,do],gd_o,2*nz+8); l_gd.start()
    for k in k_z: k.wait_recv()
    add_into(gu.at[z2,uo],zu.at[1],64)
    l_g1=lc(gu.at[z2,uo],gu_o.at[1],2*nz+7); l_g1.start()
    add_into(gu.at[z,uo],zu.at[0],64)
    l_g0=lc(gu.at[z,uo],gu_o.at[0],2*nz+11); l_g0.start()
    for k in (xa,xb,ya,yb,fa,fb,p_xa,p_xb,p_ya,p_yb,p_da,p_db,k_u,k_d,*k_z): k.wait_send()
    for k in (l_mlp,l_g0,l_g1,l_gd,l_dm,l_db): k.wait()

def k2(sec,mid,cots,cot,wu,wd,wup,wdn,g2):
    R,d=sec.shape; nz,_,fs=wu.shape; f=nz*fs
    V=pltpu.VMEM; D=pltpu.SemaphoreType.DMA
    return pl.pallas_call(k2_kernel,
      out_shape=(S((R,d),F32),S((R,d),BF),S((1,d),F32),S((4,R,d),BF),S((2,d//2,fs),BF),S((nz,fs//2,d),BF)),
      in_specs=[ANY]*8+[VM],out_specs=[ANY,ANY,VM,ANY,ANY,ANY],
      scratch_shapes=[V((4,R,d),BF),V((4,R,d),BF),V((d,f),BF),V((f,d),BF),V((4,R,f),BF),V((4,R,f),BF),V((4,R,d),BF),V((4,R,d),BF),
        V((nz,d,fs),BF),V((nz,fs,d),BF),V((R,d),F32),V((R,d),F32),V((R,d),BF),V((R,d),F32),V((R,d),BF),V((R,d),BF),V((R//2,d),BF),V((R//2,d),BF),
        V((nz,d//2,fs),BF),V((nz,fs//2,d),BF),V((2,d//2,fs),BF),
        D((2*nz+12,)),D((2,6)),D((2,10))],
      compiler_params=pltpu.CompilerParams(vmem_limit_bytes=62*2**20,collective_id=2,has_side_effects=True),
      cost_estimate=pl.CostEstimate(flops=13*10**9,bytes_accessed=30*10**6,transcendentals=10**6))(
      sec,mid,cots,cot,wu,wd,wup,wdn,g2)

ORDER=("tr","dm","do","u","A","go","p0","0","v","p1","u","1","p2","0","2","B","p3","0","3","1","4","v","fo","fm","2","n","0","1","A","B","2","0","u","3","1","u","4","0","2","3","4","1","v","3","n","2","f","4","0","3","1","0","v","2","v","n","4","3","n","1","4","1","2","2","3","4","3","4","n")
EARLY_X=(2,)

class Wires:
    def __init__(self,sems):
        self.sems=sems; self.count=0; self.all=[]
    def send(self,src,dst,dev):
        k=remote(src,dst,self.sems,self.count,dev)
        self.count+=1
        k.start()
        self.all.append(k)
        return k

def k3_kernel(dbr,tok,rows_i,wqkv,wf,wout,proj_i,feat_i,mixed_i,rden_i,g1,dmid_i,mid_i,mlp_i,gu_i,gd_i,gn2,
              bo_o,gt_o,go_o,gp_o,gu_o,gd_o,gn_o,
              db,T,rows,rowsT,gsum,wq,wo,proj,feat,mixed,rden,datt,dproj,dmid,mid,
              G0,GP,C0,CP,X0,XP,U0,UP,W0,WP,
              GU,GD,zd,yu,yd,ML,ma,mb,na,nb,bo,dfo,dfs,dfr,gt,gn,gr,w2,loc,sems):
    x,c,y,z=place()
    nx,ny,nc=around()
    nh=lax.axis_size("hidden")
    z1,z2=z+1-2*(z%2),(z+2)%nh
    n1=(x*2+c,y,z1); n2=(x*2+c,y,z2)
    R=dbr.shape[0]; n=2*R; d=dbr.shape[1]; H=R//2
    hd=wf.shape[-1]; w=2*hd; pairs=w2.shape[1]; nz=gd_i.shape[0]; fs=gu_i.shape[2]
    qo,qx,qy,qd=x*2+y,(1-x)*2+y,x*2+1-y,(1-x)*2+1-y
    mine=pl.ds(pl.multiple_of(y*R,R),R); other=pl.ds(pl.multiple_of((1-y)*R,R),R)
    A=pl.ds(0,H); B=pl.ds(H,H)
    half=lambda size,b: pl.ds(pl.multiple_of(b*size,size),size)
    nloc=[0]; pend=[]
    def lc(s,t,out=False):
        k=pltpu.make_async_copy(s,t,loc.at[nloc[0]]); nloc[0]+=1
        k.start()
        if out: pend.append(k)
        return k
    wires=Wires(sems)
    send=wires.send
    hu,hw=d//2,fs//2
    l_db=lc(dbr,db.at[mine]); l_wo=lc(wout,wo); l_rows=lc(rows_i,rows)
    greet((nx,ny,nc,n1,n2),False)
    r_db=send(dbr,db.at[mine],ny)
    l_gu=lc(gu_i,GU); l_gd=lc(gd_i,GD)
    l_feat=lc(feat_i,feat); l_proj=lc(proj_i,proj); l_mixed=lc(mixed_i,mixed); l_rden=lc(rden_i,rden)
    l_wq=lc(wqkv,wq); l_ml=lc(mlp_i,ML); l_T=lc(tok,T); l_dm=lc(dmid_i,dmid); l_mid=lc(mid_i,mid)
    pair_weights(wf,w2)
    ones=half_ones(2*w,hd); ones1=half_ones(w,hd)

    def grads(G,bufs,O,back=(3,2,1,0)):
        steps=[(nc,c),(nx,x),(n1,z%2),(n2,z//2)]
        size=G.shape[0]; base=0
        for (dev,bit),buf in zip(steps,bufs):
            size//=2
            away=pl.multiple_of(base+(1-bit)*size,16)
            base=pl.multiple_of(base+bit*size,16)
            k=send(G.at[pl.ds(away,size)],buf,dev)
            yield
            k.wait_recv()
            add_into(G.at[pl.ds(base,size)],buf,size//2 if size%32==0 else size)
        src=G.at[pl.ds(base,size)]
        own=lc(src,O.at[c,x,z%2,z//2])
        at=[c,x,z%2,z//2]
        for i in back:
            ref=lambda: O.at[tuple(at)]
            k=send(ref() if src is None else src,ref(),steps[i][0])
            src=None
            yield
            k.wait_recv()
            if own is not None: own.wait()
            own=None
            at[i]=slice(None)

    def mlp_grads(first,near,later,last,own,piece,rows):
        first.wait()
        if later is not None:
            k=[send(near(z1),later.at[0],n1),send(near((z1+2)%nh),later.at[1],n1)]
            yield
            for t in k: t.wait_recv()
            add_into(near(z2),later.at[1],rows)
        k=send(near(z2),last,n2)
        if later is not None: add_into(near(z),later.at[0],rows)
        yield
        k.wait_recv()
        mine_=near(z)
        add_into(mine_,last,rows)
        l=lc(mine_,piece(qo))
        k=send(mine_,piece(qo),nx)
        k2=send(mine_,piece(qo),ny)
        yield
        k.wait_recv()
        k=send(piece(qx),piece(qx),ny)
        yield
        k.wait_recv(); k2.wait_recv(); l.wait()
        k=send(own,own,nc)
        yield
        k.wait_recv()

    def mlp_rows(at,near,dev,q1,q2,buf,far,q3):
        k=[send(mlp_i.at[q1,at],buf.at[0],near),send(mlp_i.at[q2,at],buf.at[1],near)]
        yield
        l_ml.wait() if at is A else None
        for t in k: t.wait_recv()
        add_into(ML.at[qo,at],buf.at[0],H); add_into(ML.at[q3,at],buf.at[1],H)
        k=send(ML.at[q3,at],far,dev)
        yield
        k.wait_recv()
        if at is A: l_mid.wait()
        bo[at]=(mid[at]+(ML[qo,at].astype(F32)+far[...].astype(F32))).astype(BF)
        lc(bo.at[at],bo_o.at[at],True)

    def first_grad(at):
        t=mm_nt(dproj[0,at],wq[0])+mm_nt(dproj[1,at],wq[1])
        return t+mm_nt(dproj[2,at],wq[2])

    def first_rows():
        l_wq.wait()
        t=first_grad(other)
        dfs[...]=t.astype(BF)
        k=send(dfs,dfr,ny)
        l_T.wait()
        xo,_=unit(T[other].astype(F32))
        gsum[...]=jnp.sum(t*xo,axis=0,keepdims=True)
        yield
        k.wait_recv()
        l_dm.wait()
        dx,_=norm_back(T[mine].astype(F32),dfo[...]+dfr[...].astype(F32),g1[...])
        gt[...]=dmid[...]+dx
        lc(gt,gt_o,True)

    def gains():
        t=first_grad(mine)
        dfo[...]=t
        xm,_=unit(T[mine].astype(F32))
        gn[...]=jnp.zeros_like(gn)
        gn[0,0:1]=gsum[...]+jnp.sum(t*xm,axis=0,keepdims=True)
        gn[0,1:2]=gn2[...]
        order=[nc,nx,ny,n1,n2]
        for i,dev in enumerate(order):
            k=send(gn.at[i],gr.at[i],dev)
            yield
            k.wait_recv()
            gn[i+1]=gn[i]+gr[i]
        gn_o[...]=gn[len(order)]

    def pair(p):
        cc=slice(p*w,(p+1)*w)
        fq=feat[0,p]; fk=feat[1,p]
        dfq,dfk,dv=attend_back(fq,fk,proj[2,:,cc],mixed[:,cc],rden[:,cc],datt[:,cc],ones1,hd)
        parts=[]
        for t,(f,df) in enumerate(((fq,dfq),(fk,dfk))):
            du=feature_back(f,df,ones)
            GP[p,pl.ds(3*d+t*w,w)]=mm_tn(proj[t,:,cc],du).astype(BF)
            parts.append(mm_nt(du,w2[t,p]).astype(BF))
        parts.append(dv.astype(BF))
        for t in range(3): dproj[t,:,cc]=parts[t]
        g=mm(rowsT[...],jnp.concatenate(parts,axis=1)).astype(BF)
        for t in range(3): GP[p,pl.ds(t*d,d)]=g[:,t*w:(t+1)*w]

    uh=half(hu,c)
    qc=lambda q: pl.ds(pl.multiple_of(q*fs,fs),fs)
    chains={"0":grads(G0,(C0,X0,U0,W0),go_o),
        "u":mlp_grads(l_gu,lambda j: GU.at[(j+nh-z)%nh//2],None,yu,gu_o.at[uh],lambda q: gu_o.at[uh,qc(q)],64),
        "v":mlp_grads(l_gd,lambda j: GD.at[j],zd,yd,gd_o.at[:,half(hw,c)],lambda q: gd_o.at[q,half(hw,c)],16),
        "A":mlp_rows(A,nx,ny,qx,qd,ma,na,qy),"B":mlp_rows(B,ny,nx,qy,qd,mb,nb,qx),
        "f":first_rows(),"n":gains()}
    for p in range(pairs): chains[str(p+1)]=grads(GP.at[p],(CP.at[p],XP.at[p],UP.at[p],WP.at[p]),gp_o.at[p],(1,3,2,0) if p in EARLY_X else (3,2,1,0))
    def go(name): next(chains[name],None)
    def do(name):
        if name=="tr":
            l_rows.wait()
            rowsT[...]=rows[...].T
        elif name=="dm":
            l_db.wait(); l_wo.wait()
            datt[mine]=mm_nt(db[mine],wo[...])
        elif name=="do":
            r_db.wait_recv()
            go("B")
            datt[other]=mm_nt(db[other],wo[...])
        elif name=="go":
            l_mixed.wait()
            G0[...]=mm_tn(mixed[...],db[...]).astype(BF)
            go("0")
        elif name=="p0":
            for k in (l_feat,l_proj,l_rden): k.wait()
            pair(0); go("1")
        elif name[0]=="p":
            pair(int(name[1])); go(str(int(name[1])+1))
        elif name=="fo": go("f")
        elif name=="fm": go("n")
        else: go(name)
    for name in ("A","v","u"): go(name)
    for name in ORDER: do(name)
    for name in chains:
        for _ in chains[name]: pass
    for k in wires.all: k.wait_send()
    for k in pend: k.wait()

def k3(dbr,tok,rows,wqkv,wf,wout,proj,feat,mixed,rden,g1,dmid,mid,mlp,gu,gd,gn2):
    R,d=dbr.shape; n=2*R; c=wout.shape[0]; h=wf.shape[1]; hd=wf.shape[-1]; pairs=h//2
    nz=gd.shape[0]; fs=gu.shape[2]; f=nz*fs; w=2*hd; q=3*d+2*w
    V=pltpu.VMEM; D=pltpu.SemaphoreType.DMA
    like=lambda a: V(a.shape,a.dtype)
    return pl.pallas_call(k3_kernel,
      out_shape=(S((R,d),BF),S((R,d),F32),S((2,2,2,2,c//16,d),BF),S((pairs,2,2,2,2,q//16,w),BF),S((d,f),BF),S((4,fs,d),BF),S((8,d),F32)),
      in_specs=[ANY,ANY,ANY,ANY,VM,ANY,ANY,ANY,ANY,ANY,VM,ANY,ANY,ANY,ANY,ANY,VM],
      out_specs=[ANY]*6+[VM],
      scratch_shapes=[V((n,d),BF),like(tok),like(rows),V((d,n),BF),V((1,d),F32),like(wqkv),like(wout),like(proj),like(feat),like(mixed),like(rden),
        V((n,c),F32),like(proj),like(dmid),like(mid),
        V((c,d),BF),V((pairs,q,w),BF),V((c//2,d),BF),V((pairs,q//2,w),BF),V((c//4,d),BF),V((pairs,q//4,w),BF),
        V((c//8,d),BF),V((pairs,q//8,w),BF),V((c//16,d),BF),V((pairs,q//16,w),BF),
        V((2,d//2,fs),BF),V((nz,fs//2,d),BF),V((2,fs//2,d),BF),
        V((d//2,fs),BF),V((fs//2,d),BF),
        like(mlp),V((2,R//2,d),BF),V((2,R//2,d),BF),V((R//2,d),BF),V((R//2,d),BF),V((R,d),BF),
        V((R,d),F32),V((R,d),BF),V((R,d),BF),V((R,d),F32),V((6,8,d),F32),V((5,8,d),F32),
        V((2,pairs,w,w),BF),D((40,)),D((2,80))],
      compiler_params=pltpu.CompilerParams(vmem_limit_bytes=62*2**20,collective_id=3,has_side_effects=True),
      cost_estimate=pl.CostEstimate(flops=8*10**9,bytes_accessed=40*10**6,transcendentals=10**6))(
      dbr,tok,rows,wqkv,wf,wout,proj,feat,mixed,rden,g1,dmid,mid,mlp,gu,gd,gn2)

def finish_kernel(go,g0,g1,g2,gf,gu,gd,go_o,gq_o,gf_o,gu_o,gd_o):
    for a,b in ((go,go_o),(gu,gu_o),(gd,gd_o)): b[...]=a[...].astype(F32)
    pairs,_,w=g0.shape; hd=w//2
    for t,g in enumerate((g0,g1,g2)):
        for p in range(pairs): gq_o[t,:,p*w:(p+1)*w]=g[p].astype(F32)
    @pl.when(pl.program_id(0)==0)
    def _():
        for t in range(2):
            for p in range(pairs):
                for s in range(2):
                    gf_o[t,2*p+s]=gf[p,t*w+s*hd:t*w+(s+1)*hd,s*hd:(s+1)*hd].astype(F32)

def finish(go,gp,gu,gd,hd):
    c,d=go.shape; pairs,_,w=gp.shape; f=gu.shape[1]; N=8
    B=pl.BlockSpec
    row=lambda a: B((a.shape[0]//N,a.shape[1]),lambda i:(i,0))
    part=lambda t: B((pairs,d//N,w),lambda i:(0,i+N*t,0))
    return pl.pallas_call(finish_kernel,grid=(N,),
      out_shape=(S((c,d),F32),S((3,d,c),F32),S((2,2*pairs,hd,hd),F32),S((d,f),F32),S((f,d),F32)),
      in_specs=[row(go),part(0),part(1),part(2),B((pairs,2*w,w),lambda i:(0,3*d//(2*w),0)),row(gu),row(gd)],
      out_specs=[row(go),B((3,d//N,c),lambda i:(0,i,0)),B((2,2*pairs,hd,hd),lambda i:(0,0,0,0)),row(gu),row(gd)],
      compiler_params=pltpu.CompilerParams(vmem_limit_bytes=62*2**20))(go,gp,gp,gp,gp,gu,gd)

def per_device_k1(
    tokens, lengths, norm_first, w_qkv, w_feature, w_out, norm_second, w_up, w_down, cotangent
):
    wqkv=jnp.transpose(w_qkv,(1,0,2))
    tok,first_rows,proj,feat,mixed,rden,middle,second_low,wu,wd,cot_all=k1(lengths,tokens[0],norm_first[None],wqkv,w_feature,w_out,norm_second[None],w_up,w_down,cotangent[0])
    d_middle,d_branch_low,gn2,mlp,gu,gd=k2(second_low,middle,cot_all,cotangent[0],wu,wd,w_up,w_down,norm_second[None])
    block_out,grad_tokens,go,gp,gu,gd,gn=k3(d_branch_low,tok,first_rows,wqkv,w_feature,w_out,proj,feat,mixed,rden,norm_first[None],d_middle,middle,mlp,gu,gd,gn2)
    d=tokens.shape[2]; h=w_feature.shape[1]; hd=w_feature.shape[3]; w=2*hd
    go=go.reshape(w_out.shape); gp=gp.reshape(h//2,-1,w)
    go,gq,gf,gu,gd=finish(go,gp,gu,gd.reshape(gd.shape[0]*gd.shape[1],-1),hd)
    return (
        block_out[None],
        grad_tokens[None],
        gn[0],
        jnp.transpose(gq,(1,0,2)),
        gf,
        go,
        gn[1],
        gu,
        gd,
    )


def solution(mesh):
    in_specs = (
        P(("dp", "hidden"), "head", None),
        P(("dp", "hidden"), None),
        P(),
        P(None, None, "head"),
        P(None, "head", None, None),
        P("head", None),
        P(),
        P(None, "hidden"),
        P("hidden", None),
        P(("dp", "hidden"), "head", None),
    )
    out_specs = (
        P(("dp", "hidden"), "head", None),
        P(("dp", "hidden"), "head", None),
        P(),
        P(None, None, "head"),
        P(None, "head", None, None),
        P("head", None),
        P(),
        P(None, "hidden"),
        P("hidden", None),
    )
    near=dict(mesh.shape)=={"dp":4,"head":2,"hidden":4}
    return jax.shard_map(
        per_device_k1 if near else per_device, mesh=mesh, in_specs=in_specs, out_specs=out_specs, check_vma=False
    )
```

```python
import jax, jax.numpy as jnp
from jax import lax
from jax.experimental import pallas as pl
from jax.experimental.pallas import tpu as pltpu
from jax.sharding import PartitionSpec as P
BF=jnp.bfloat16; F32=jnp.float32
NT=(((1,),(1,)),((),()))
TN=(((0,),(0,)),((),()))
SB=256

def mm(a,b): return jnp.dot(a,b,preferred_element_type=F32)
def mm_nt(a,b): return lax.dot_general(a,b,NT,preferred_element_type=F32)
def mm_tn(a,b): return lax.dot_general(a,b,TN,preferred_element_type=F32)

def half_ones(width, size):
    r=lax.broadcasted_iota(jnp.int32,(width,width),0)//size
    c=lax.broadcasted_iota(jnp.int32,(width,width),1)//size
    return (r==c).astype(F32).astype(BF)

def first_half(shape, size):
    return lax.broadcasted_iota(jnp.int32,shape,1)%(2*size) < size

def half_sum(t, ones):
    hi=t.astype(BF); lo=(t-hi.astype(F32)).astype(BF)
    return mm(hi,ones)+mm(lo,ones)

def features(x, w2, ones, size):
    u=mm(x,w2)
    h0=first_half(u.shape,size)
    big=jnp.float32(3e38)
    def both(f, fill):
        return jnp.where(h0, f(jnp.where(h0,u,fill)), f(jnp.where(h0,fill,u)))
    top=both(lambda t: jnp.max(t,axis=1,keepdims=True), -big)
    low=both(lambda t: jnp.min(t,axis=1,keepdims=True), big)
    e=jnp.concatenate([jnp.exp(u-top),jnp.exp(low-u)],axis=1)
    s=mm(e.astype(BF),ones)
    return e/s

def halves(t, h0):
    z=jnp.zeros_like(t)
    return jnp.where(h0,t,z), jnp.where(h0,z,t)

def attend(fq, fk, v, size):
    n=fq.shape[0]
    h0=first_half(fq.shape,size)
    fqs=halves(fq,h0)
    hv=first_half(v.shape,size)
    one=jnp.ones(v.shape,BF)
    ve=halves(jnp.concatenate([v,one],axis=1),h0)
    outs=[]
    for r in range(0,n,SB):
        ext=r+SB
        keep=(lax.broadcasted_iota(jnp.int32,(SB,ext),0)+r)>=lax.broadcasted_iota(jnp.int32,(SB,ext),1)
        acc=None
        for s in range(2):
            sc=mm_nt(fqs[s][r:r+SB],fk[:ext])
            sc=jnp.where(keep,sc,0.0).astype(BF)
            t=mm(sc,ve[s][:ext])
            acc=t if acc is None else acc+t
        outs.append(acc)
    p=jnp.concatenate(outs,axis=0)
    w=v.shape[1]
    rden=1.0/p[:,w:]
    return p[:,:w]*rden, rden

def attend_back(fq,fk,v,mixed,rden,datt,ones,size):
    n,w=v.shape
    wide=(n,2*w)
    h0=first_half(wide,size)
    dn=(datt*rden).astype(BF)
    dd=-half_sum(datt*mixed.astype(F32),ones)*rden
    hi=dd.astype(BF); lo=(dd-hi.astype(F32)).astype(BF)
    lane=lax.broadcasted_iota(jnp.int32,(n,w),1)%size
    zero=jnp.zeros((n,w),BF)
    ext_=jnp.where(lane==0,hi,jnp.where(lane==1,lo,zero))
    nx=halves(jnp.concatenate([dn,ext_],axis=1),h0)
    vx=jnp.concatenate([v,jnp.ones((n,w),BF)],axis=1)
    fqs=halves(fq,h0); fks=halves(fk,h0)
    dfq=[];dfk=[];dv=[]
    for r in range(0,n,SB):
        ext=r+SB
        keep=(lax.broadcasted_iota(jnp.int32,(SB,ext),0)+r)>=lax.broadcasted_iota(jnp.int32,(SB,ext),1)
        acc=0.0
        for s in range(2):
            ds=jnp.where(keep,mm_nt(nx[s][r:r+SB],vx[:ext]),0.0).astype(BF)
            acc=acc+mm(ds,fks[s][:ext])
        dfq.append(acc)
        left=n-r
        keep=lax.broadcasted_iota(jnp.int32,(SB,left),0)<=lax.broadcasted_iota(jnp.int32,(SB,left),1)
        ak=0.0; av=0.0
        for s in range(2):
            ds=jnp.where(keep,mm_nt(vx[r:r+SB],nx[s][r:]),0.0).astype(BF)
            ak=ak+mm(ds,fqs[s][r:])
            sc=jnp.where(keep,mm_nt(fk[r:r+SB],fqs[s][r:]),0.0).astype(BF)
            av=av+mm(sc,nx[s][r:,:w])
        dfk.append(ak); dv.append(av)
    cat=lambda t: jnp.concatenate(t,axis=0)
    return cat(dfq),cat(dfk),cat(dv)

def feature_back(f, df, ones):
    w=f.shape[1]//2
    f=f.astype(F32)
    part=f*(df-half_sum(f*df,ones))
    return (part[:,:w]-part[:,w:]).astype(BF)

def pair_weights(wf_ref, w2_ref):
    hd=wf_ref.shape[-1]
    w2_ref[...]=jnp.zeros_like(w2_ref)
    for t in range(2):
        for p in range(w2_ref.shape[1]):
            w2_ref[t,p,:hd,:hd]=wf_ref[t,2*p]
            w2_ref[t,p,hd:,hd:]=wf_ref[t,2*p+1]

def fwd_kernel(len_ref, rows_ref, wqkv_ref, wf_ref, wout_ref, proj_ref, feat_ref, mixed_ref, rden_ref, branch_ref, w2_ref):
    hd=wf_ref.shape[-1]; w=2*hd; n=rows_ref.shape[0]; pairs=w2_ref.shape[1]
    pair_weights(wf_ref,w2_ref)
    for i in range(3):
        proj_ref[i]=mm(rows_ref[...],wqkv_ref[i]).astype(BF)
    ones=half_ones(2*w,hd)
    valid=lax.broadcasted_iota(jnp.int32,(n,2*w),0)<len_ref[0,0]
    def body(p,_):
        c=pl.ds(pl.multiple_of(p*w,w),w)
        fq=features(proj_ref[0,:,c],w2_ref[0,p],ones,hd).astype(BF)
        fk=jnp.where(valid,features(proj_ref[1,:,c],w2_ref[1,p],ones,hd),0.0).astype(BF)
        feat_ref[0,p]=fq; feat_ref[1,p]=fk
        m,rd=attend(fq,fk,proj_ref[2,:,c],hd)
        mixed_ref[:,c]=m.astype(BF); rden_ref[:,c]=rd
        return 0
    lax.fori_loop(0,pairs,body,0)
    branch_ref[...]=mm(mixed_ref[...],wout_ref[...]).astype(branch_ref.dtype)

def bwd_kernel(rows_ref,wqkv_ref,wf_ref,wout_ref,proj_ref,feat_ref,mixed_ref,rden_ref,dbr_ref,
               gq_ref,gf_ref,go_ref,dfirst_ref,w2_ref,datt_ref,dproj_ref):
    hd=wf_ref.shape[-1]; w=2*hd; n=rows_ref.shape[0]; pairs=w2_ref.shape[1]
    pair_weights(wf_ref,w2_ref)
    ones=half_ones(2*w,hd); ones1=half_ones(w,hd)
    datt_ref[...]=mm_nt(dbr_ref[...],wout_ref[...])
    go_ref[...]=mm_tn(mixed_ref[...],dbr_ref[...]).astype(go_ref.dtype)
    def body(p,_):
        c=pl.ds(pl.multiple_of(p*w,w),w)
        fq=feat_ref[0,p]; fk=feat_ref[1,p]
        dfq,dfk,dv=attend_back(fq,fk,proj_ref[2,:,c],mixed_ref[:,c],rden_ref[:,c],datt_ref[:,c],ones1,hd)
        for t,(f,df) in enumerate(((fq,dfq),(fk,dfk))):
            du=feature_back(f,df,ones)
            g=mm_tn(proj_ref[t,:,c],du)
            gf_ref[t,2*p]=g[:hd,:hd].astype(gf_ref.dtype); gf_ref[t,2*p+1]=g[hd:,hd:].astype(gf_ref.dtype)
            dproj_ref[t,:,c]=mm_nt(du,w2_ref[t,p]).astype(BF)
        dproj_ref[2,:,c]=dv.astype(BF)
        return 0
    lax.fori_loop(0,pairs,body,0)
    acc=None
    for i in range(3):
        gq_ref[i]=mm_tn(rows_ref[...],dproj_ref[i]).astype(gq_ref.dtype)
        t=mm_nt(dproj_ref[i],wqkv_ref[i])
        acc=t if acc is None else acc+t
    dfirst_ref[...]=acc.astype(dfirst_ref.dtype)
VM=pl.BlockSpec(memory_space=pltpu.VMEM)
SM=pl.BlockSpec(memory_space=pltpu.SMEM)
S=jax.ShapeDtypeStruct
def fwd(length,rows,wqkv,wf,wout):
    n,d=rows.shape; c=wout.shape[0]; h=wf.shape[1]; hd=wf.shape[-1]
    return pl.pallas_call(fwd_kernel,
      out_shape=(S((3,n,c),BF),S((2,h//2,n,4*hd),BF),S((n,c),BF),S((n,c),F32),S((n,d),BF)),
      in_specs=[SM,VM,VM,VM,VM],out_specs=[VM]*5,
      scratch_shapes=[pltpu.VMEM((2,h//2,2*hd,2*hd),BF)],
      compiler_params=pltpu.CompilerParams(vmem_limit_bytes=56*2**20))(length,rows,wqkv,wf,wout)
def bwd(rows,wqkv,wf,wout,proj,feat,mixed,rden,dbr):
    n,d=rows.shape; c=wout.shape[0]; h=wf.shape[1]; hd=wf.shape[-1]
    return pl.pallas_call(bwd_kernel,
      out_shape=(S((3,d,c),BF),S((2,h,hd,hd),F32),S((c,d),BF),S((n,d),BF)),
      in_specs=[VM]*9,out_specs=[VM]*4,
      scratch_shapes=[pltpu.VMEM((2,h//2,2*hd,2*hd),BF),pltpu.VMEM((n,c),F32),pltpu.VMEM((3,n,c),BF)],
      compiler_params=pltpu.CompilerParams(vmem_limit_bytes=56*2**20))(rows,wqkv,wf,wout,proj,feat,mixed,rden,dbr)

EPS=1e-05

def normalize(values, gain):
    average = jnp.mean(values, axis=-1, keepdims=True)
    centred = values - average
    spread = jnp.mean(centred * centred, axis=-1, keepdims=True)
    return centred * lax.rsqrt(spread + EPS) * gain

def smooth_gate(values):
    return jax.nn.gelu(values, approximate=True)

def per_device(
    tokens, lengths, norm_first, w_qkv, w_feature, w_out, norm_second, w_up, w_down, cotangent
):
    wqkv=jnp.transpose(w_qkv,(1,0,2))
    residual_in = tokens[0].astype(jnp.float32)
    normed_first, first_back = jax.vjp(normalize, residual_in, norm_first)
    first_low = normed_first.astype(jnp.bfloat16)
    first_rows = lax.all_gather(first_low, "head", axis=0, tiled=True)
    cot_low = cotangent[0]
    cot_rows = lax.all_gather(cot_low, "hidden", axis=0, tiled=True)
    proj,feat,mixed,rden,part=fwd(lengths,first_rows,wqkv,w_feature,w_out)
    branch = lax.psum_scatter(part, "head", scatter_dimension=0, tiled=True).astype(jnp.float32)
    middle = residual_in + branch
    normed_second, second_back = jax.vjp(normalize, middle, norm_second)
    second_low = normed_second.astype(jnp.bfloat16)
    second_rows = lax.all_gather(second_low, "hidden", axis=0, tiled=True)
    hidden_pre = jnp.dot(second_rows, w_up, preferred_element_type=jnp.float32)
    active = smooth_gate(hidden_pre).astype(jnp.bfloat16)
    gate_grad = jax.vjp(smooth_gate, hidden_pre)[1]
    d_active = jnp.einsum("nd,fd->nf", cot_rows, w_down, preferred_element_type=jnp.float32)
    d_pre = gate_grad(d_active)[0].astype(jnp.bfloat16)
    d_second = lax.psum_scatter(
        jnp.einsum("nf,df->nd", d_pre, w_up, preferred_element_type=jnp.float32).astype(jnp.bfloat16),
        "hidden",
        scatter_dimension=0,
        tiled=True,
    ).astype(jnp.float32)
    mlp_result = lax.psum_scatter(
        jnp.dot(active, w_down, preferred_element_type=jnp.float32).astype(jnp.bfloat16),
        "hidden",
        scatter_dimension=0,
        tiled=True,
    ).astype(jnp.float32)
    block_out = (middle + mlp_result).astype(jnp.bfloat16)
    grad_down = jnp.einsum("nf,nd->fd", active, cot_rows, preferred_element_type=jnp.float32)
    grad_up = jnp.einsum("nd,nf->df", second_rows, d_pre, preferred_element_type=jnp.float32)
    d_middle_norm, grad_norm_second = second_back(d_second)
    d_middle = cot_low.astype(jnp.float32) + d_middle_norm
    d_branch_rows = lax.all_gather(d_middle.astype(jnp.bfloat16), "head", axis=0, tiled=True)
    gq,grad_feature,go,dfirst=bwd(first_rows,wqkv,w_feature,w_out,proj,feat,mixed,rden,d_branch_rows)
    d_first = lax.psum_scatter(dfirst, "head", scatter_dimension=0, tiled=True).astype(jnp.float32)
    d_input_norm, grad_norm_first = first_back(d_first)
    grad_tokens = d_middle + d_input_norm
    grad_up, grad_down = (
        lax.psum(grad_up.astype(jnp.bfloat16), ("dp", "head")).astype(jnp.float32),
        lax.psum(grad_down.astype(jnp.bfloat16), ("dp", "head")).astype(jnp.float32),
    )
    gq, grad_feature, go = (
        lax.psum(gq, ("dp", "hidden")).astype(jnp.float32),
        lax.psum(grad_feature.astype(jnp.bfloat16), ("dp", "hidden")).astype(jnp.float32),
        lax.psum(go, ("dp", "hidden")).astype(jnp.float32),
    )
    grad_norm_first, grad_norm_second = lax.psum(
        (grad_norm_first, grad_norm_second), ("dp", "head", "hidden")
    )
    return (
        block_out[None],
        grad_tokens[None],
        grad_norm_first,
        jnp.transpose(gq,(1,0,2)),
        grad_feature,
        go,
        grad_norm_second,
        grad_up,
        grad_down,
    )


ORDER=("n0","t","cx","w","n1","a","pt","po","tr","cy","w","p","sec","cy","w","w","bo","yb","xa","dno","xb","ya","bx","by","yb","xa","bd","gu","Xa","dn","u","Yb","gd","Da","Db","ab","v","Da","Db","fin","u","dm","A","v","b","do","go","p0","0","A","p1","1","u","p2","0","2","p3","1","B","3","4","fo","0","v","fm","1","u","n","0","2","1","0","2","B","f","1","0","3","2","1","4","3","4","u","v","n","3","u","4","3","0","v","2","0","4","n","3","v","1","1","2","4","n","3","3","2","4","2","n","4")
EARLY_X=(1,)

MESH=pl.DeviceIdType.MESH
ANY=pl.BlockSpec(memory_space=pl.ANY)
EPS=1e-05

def place():
    dp=lax.axis_index("dp")
    return dp//2, dp%2, lax.axis_index("head"), lax.axis_index("hidden")

def only(when,act):
    if when is None: act()
    else: pl.when(when)(act)

class Wires:
    def __init__(self,sems):
        self.sems=sems; self.count=0; self.all=[]
    def send(self,src,dst,dev,when=None):
        i=self.count
        self.count+=1
        k=pltpu.make_async_remote_copy(src_ref=src,dst_ref=dst,send_sem=self.sems.at[0,i],recv_sem=self.sems.at[1,i],device_id=dev,device_id_type=MESH)
        only(when,k.start)
        self.all.append((k,when))
        return k

def greet(peers,maybe):
    bar=pltpu.get_barrier_semaphore()
    count=len(peers)
    for d in peers: pl.semaphore_signal(bar,inc=1,device_id=d,device_id_type=MESH)
    for when,d in maybe:
        @pl.when(when)
        def _():
            pl.semaphore_signal(bar,inc=1,device_id=d,device_id_type=MESH)
        count=count+jnp.where(when,1,0)
    pl.semaphore_wait(bar,count)

def unit(values):
    centred=values-jnp.mean(values,axis=-1,keepdims=True)
    r=lax.rsqrt(jnp.mean(centred*centred,axis=-1,keepdims=True)+EPS)
    return centred*r, r

def norm_back(values,grad,gain):
    xh,r=unit(values)
    e=grad*gain
    inner=e-jnp.mean(e,axis=-1,keepdims=True)-xh*jnp.mean(e*xh,axis=-1,keepdims=True)
    return r*inner, jnp.sum(grad*xh,axis=0,keepdims=True)

def gate(v):
    k=0.7978845608; a=0.044715
    sq=v*v
    t=jnp.tanh(k*v*(1.0+a*sq))
    half=0.5*(1.0+t)
    return v*half, half+0.5*v*(1.0-t*t)*(k+(3.0*a*k)*sq)

def add_into(dst,src,step):
    rows=dst.shape[0]
    def body(i,_):
        r=pl.ds(pl.multiple_of(i*step,step),step)
        dst[r]=(dst[r].astype(F32)+src[r].astype(F32)).astype(dst.dtype)
        return 0
    lax.fori_loop(0,rows//step,body,0)

def layer_kernel(len_ref,tok,cot,g1,g2,wqkv,wf,wout,wup,wdn,
                 bo_o,gt_o,go_o,gp_o,gu_o,gd_o,gn_o,
                 T,rows,rowsT,wq,wo,proj,feat,mixed,rden,own,snd,rcv,mid,
                 SA,CA,Wu,Wd,act,dpre,P,ML,gu,gd,cu,cd,zu,zd,yu,yd,rx,ry,rdx,rdy,
                 dmid,db,datt,dproj,G0,GP,C0,CP,X0,XP,U0,UP,W0,WP,
                 ma,mb,na,nb,bo,dfs,dfr,gn2,gsum,gn,gr,w2,loc,sems):
    x,c,y,z=place()
    nh=lax.axis_size("hidden"); last=nh-1
    nx,ny,nc=((1-x)*2+c,y,z),(x*2+c,1-y,z),(x*2+1-c,y,z)
    low,side=z%2,z//2
    z1,z2=z+1-2*low,(z+2)%nh
    zz1=(z1+2)%nh
    n1,n2=(x*2+c,y,z1),(x*2+c,y,z2)
    R,d=tok.shape; n=2*R; H=R//2
    hd=wf.shape[-1]; w=2*hd; pairs=w2.shape[1]; f=wup.shape[1]; fs=f//4
    qo,qx,qy,qd=x*2+y,(1-x)*2+y,x*2+1-y,(1-x)*2+1-y
    mine=pl.ds(pl.multiple_of(y*R,R),R); other=pl.ds(pl.multiple_of((1-y)*R,R),R)
    A=pl.ds(0,H); B=pl.ds(H,H)
    half=lambda size,b: pl.ds(pl.multiple_of(b*size,size),size)
    hu,hw=d//2,fs//2
    uo,ua,vo,va=half(hu,c),half(hu,1-c),half(hw,c),half(hw,1-c)
    at=lambda q: pl.ds(pl.multiple_of(q*fs,fs),fs)
    nloc=[0]; pend=[]
    def lc(s,t,out=False):
        k=pltpu.make_async_copy(s,t,loc.at[nloc[0]]); nloc[0]+=1
        k.start()
        if out: pend.append(k)
        return k
    wires=Wires(sems)
    send=wires.send
    l_tok=lc(tok,T.at[mine])
    l_wq=[lc(wqkv.at[i],wq.at[i]) for i in range(3)]
    greet((nx,ny,nc,n2),((z<last,(x*2+c,y,z+1)),(z>0,(x*2+c,y,z-1))))

    def simple(src,dst,dev):
        k=send(src,dst,dev)
        yield
        k.wait_recv()

    def onward(src,dst,dev,src2,dst2,dev2,between=None):
        k=send(src,dst,dev)
        yield
        k.wait_recv()
        if between is not None: between()
        k=send(src2,dst2,dev2)
        yield
        k.wait_recv()

    def weights():
        wdh=lambda q: pl.ds(pl.multiple_of(q*fs+c*hw,hw),hw)
        wdo=lambda q: pl.ds(pl.multiple_of(q*fs+(1-c)*hw,hw),hw)
        for s in range(1,nh):
            now=[]
            for right in (True,False):
                j=(z-s+1) if right else (z+s-1)
                when=((z<last)&(j>=0)) if right else ((z>0)&(j<=last))
                jj=jnp.clip(j,0,last)
                dev=(x*2+c,y,jnp.clip(z+1 if right else z-1,0,last))
                if s==1: su,sd=wup.at[uo,at(qo)],wdn.at[wdh(qo)]
                else: su,sd=Wu.at[uo,at(jj)],Wd.at[wdh(jj)]
                got=(z-s>=0) if right else (z+s<=last)
                now.append((send(su,Wu.at[uo,at(jj)],dev,when),send(sd,Wd.at[wdh(jj)],dev,when),got))
            yield
            for a,b,got in now: only(got,a.wait_recv); only(got,b.wait_recv)
            for right,(_,_,got) in zip((True,False),now):
                jj=jnp.clip((z-s) if right else (z+s),0,last)
                shared.append((send(Wu.at[uo,at(jj)],Wu.at[uo,at(jj)],nc,got),got))
                shared.append((send(Wd.at[wdh(jj)],Wd.at[wdh(jj)],nc,got),got))
        yield
        for k,got in shared: only(got,k.wait_recv)
    shared=[]

    def grads(G,bufs,O,early=False):
        steps=[(nc,c),(nx,x),(n1,low),(n2,side)]
        size=G.shape[0]; base=0
        for (dev,bit),buf in zip(steps,bufs):
            size//=2
            away=pl.multiple_of(base+(1-bit)*size,16)
            base=pl.multiple_of(base+bit*size,16)
            k=send(G.at[pl.ds(away,size)],buf,dev)
            yield
            k.wait_recv()
            add_into(G.at[pl.ds(base,size)],buf,size//2 if size%32==0 else size)
        src=G.at[pl.ds(base,size)]
        place_=[c,x,low,side]
        copy=lc(src,O.at[tuple(place_)])
        for i in ((1,3,2,0) if early else (3,2,1,0)):
            k=send(O.at[tuple(place_)] if src is None else src,O.at[tuple(place_)],steps[i][0])
            src=None
            yield
            k.wait_recv()
            if copy is not None: copy.wait()
            copy=None
            place_[i]=slice(None)

    def mlp_grads(W,kept,away,core,far,final,whole,piece,step):
        k=send(W.at[:,away],core,nc)
        yield
        k.wait_recv()
        for j in range(nh): add_into(W.at[j,kept],core.at[j],step)
        k=[send(W.at[z1,kept],far.at[0],n1),send(W.at[zz1,kept],far.at[1],n1)]
        yield
        for t in k: t.wait_recv()
        add_into(W.at[z2,kept],far.at[1],step)
        k=send(W.at[z2,kept],final,n2)
        add_into(W.at[z,kept],far.at[0],step)
        yield
        k.wait_recv()
        add_into(W.at[z,kept],final,step)
        l=lc(W.at[z,kept],piece(qo))
        k=send(W.at[z,kept],piece(qo),nx)
        k2=send(W.at[z,kept],piece(qo),ny)
        yield
        k.wait_recv()
        k=send(piece(qx),piece(qx),ny)
        yield
        k.wait_recv(); k2.wait_recv(); l.wait()
        k=send(whole,whole,nc)
        yield
        k.wait_recv()

    def mlp_rows(r,near,dev,q1,q2,buf,far,q3):
        k=[send(ML.at[q1,r],buf.at[0],near),send(ML.at[q2,r],buf.at[1],near)]
        yield
        for t in k: t.wait_recv()
        add_into(ML.at[qo,r],buf.at[0],H); add_into(ML.at[q3,r],buf.at[1],H)
        k=send(ML.at[q3,r],far,dev)
        yield
        k.wait_recv()
        bo[r]=(mid[r]+(ML[qo,r].astype(F32)+far[...].astype(F32))).astype(BF)
        lc(bo.at[r],bo_o.at[r],True)

    def first_grad(r):
        t=mm_nt(dproj[0,r],wq[0])+mm_nt(dproj[1,r],wq[1])
        return t+mm_nt(dproj[2,r],wq[2])

    def first_rows():
        t=first_grad(other)
        dfs[...]=t.astype(BF)
        k=send(dfs,dfr,ny)
        xo,_=unit(T[other].astype(F32))
        gsum[...]=jnp.sum(t*xo,axis=0,keepdims=True)
        yield
        k.wait_recv()
        dx,_=norm_back(T[mine].astype(F32),own[...]+dfr[...].astype(F32),g1[...])
        dmid[...]=dmid[...]+dx
        lc(dmid,gt_o,True)

    def gains():
        t=first_grad(mine)
        own[...]=t
        xm,_=unit(T[mine].astype(F32))
        gn[...]=jnp.zeros_like(gn)
        gn[0,0:1]=gsum[...]+jnp.sum(t*xm,axis=0,keepdims=True)
        gn[0,1:2]=gn2[...]
        order=[nc,nx,ny,n1,n2]
        for i,dev in enumerate(order):
            k=send(gn.at[i],gr.at[i],dev)
            yield
            k.wait_recv()
            gn[i+1]=gn[i]+gr[i]
        gn_o[...]=gn[len(order)]

    def sum_a(): P[qy,A]=(P[qy,A].astype(F32)+rdx[...].astype(F32)).astype(BF)
    def sum_b(): P[qx,B]=(P[qx,B].astype(F32)+rdy[...].astype(F32)).astype(BF)
    S_=lambda q,r: SA.at[q,r]
    chains={
        "t":simple(tok,T.at[mine],ny),
        "w":weights(),
        "cx":simple(cot,CA.at[qo],nx),
        "cy":onward(cot,CA.at[qo],ny,CA.at[qy],CA.at[qy],nx),
        "p":simple(snd,rcv,ny),
        "xa":onward(S_(qo,A),S_(qo,A),nx,S_(qx,A),S_(qx,A),ny),
        "yb":onward(S_(qo,B),S_(qo,B),ny,S_(qy,B),S_(qy,B),nx),
        "xb":simple(S_(qo,B),S_(qo,B),nx),
        "ya":simple(S_(qo,A),S_(qo,A),ny),
        "Xa":simple(P.at[qx,A],rx.at[A],nx),
        "Yb":simple(P.at[qy,B],ry.at[B],ny),
        "Da":onward(P.at[qd,A],rdx,nx,P.at[qy,A],ry.at[A],ny,sum_a),
        "Db":onward(P.at[qd,B],rdy,ny,P.at[qx,B],rx.at[B],nx,sum_b),
        "b":simple(db.at[mine],db.at[mine],ny),
        "u":mlp_grads(gu,uo,ua,cu,zu,yu,gu_o.at[uo],lambda q: gu_o.at[uo,at(q)],64),
        "v":mlp_grads(gd,vo,va,cd,zd,yd,gd_o.at[:,vo],lambda q: gd_o.at[q,vo],16),
        "A":mlp_rows(A,nx,ny,qx,qd,ma,na,qy),"B":mlp_rows(B,ny,nx,qy,qd,mb,nb,qx),
        "f":first_rows(),"n":gains(),
        "0":grads(G0,(C0,X0,U0,W0),go_o)}
    for p in range(pairs): chains[str(p+1)]=grads(GP.at[p],(CP.at[p],XP.at[p],UP.at[p],WP.at[p]),gp_o.at[p],p in EARLY_X)
    turns={name:-1 for name in chains}
    def go(*names):
        for name in names:
            next(chains[name],None)
            turns[name]+=1
    def need(**steps):
        for name,count in steps.items():
            while turns[name]<count: go(name)

    ones=half_ones(2*w,hd); ones1=half_ones(w,hd)
    valid=lax.broadcasted_iota(jnp.int32,(n,2*w),0)<len_ref[0,0]
    def first(r):
        xh,_=unit(T[r].astype(F32))
        rows[r]=(xh*g1[...]).astype(BF)
    def project(r):
        for i in range(3): proj[i,r]=mm(rows[r],wq[i]).astype(BF)
    def heads(p,_):
        cc=pl.ds(pl.multiple_of(p*w,w),w)
        fq=features(proj[0,:,cc],w2[0,p],ones,hd).astype(BF)
        fk=jnp.where(valid,features(proj[1,:,cc],w2[1,p],ones,hd),0.0).astype(BF)
        feat[0,p]=fq; feat[1,p]=fk
        m,rd=attend(fq,fk,proj[2,:,cc],hd)
        mixed[:,cc]=m.astype(BF); rden[:,cc]=rd
        return 0
    def block(qi,keep):
        a,ga=gate(mm(SA[qi],Wu[...]))
        act[qi]=a.astype(BF)
        dp=(mm_nt(CA[qi],Wd[...])*ga).astype(BF)
        dpre[qi]=dp
        d2=mm_nt(dp,Wu[...])
        if keep: own[...]=d2
        else: P[qi]=d2.astype(BF)
    def down(qi): ML[qi]=mm(act[qi],Wd[...]).astype(BF)
    def pair(p):
        cc=slice(p*w,(p+1)*w)
        fq=feat[0,p]; fk=feat[1,p]
        dfq,dfk,dv=attend_back(fq,fk,proj[2,:,cc],mixed[:,cc],rden[:,cc],datt[:,cc],ones1,hd)
        parts=[]
        for t,(ft,df) in enumerate(((fq,dfq),(fk,dfk))):
            du=feature_back(ft,df,ones)
            GP[p,pl.ds(3*d+t*w,w)]=mm_tn(proj[t,:,cc],du).astype(BF)
            parts.append(mm_nt(du,w2[t,p]).astype(BF))
        parts.append(dv.astype(BF))
        for t in range(3): dproj[t,:,cc]=parts[t]
        g=mm(rowsT[...],jnp.concatenate(parts,axis=1)).astype(BF)
        for t in range(3): GP[p,pl.ds(t*d,d)]=g[:,t*w:(t+1)*w]
    def do(name):
        if name=="n0":
            pair_weights(wf,w2)
            l_tok.wait()
            first(mine)
            for k in l_wq: k.wait()
            project(mine)
        elif name=="n1":
            need(t=1)
            first(other); project(other)
        elif name=="a": lax.fori_loop(0,pairs,heads,0)
        elif name=="pt":
            l_wo.wait()
            snd[...]=mm(mixed[other],wo[...]).astype(BF)
            go("p")
        elif name=="po": own[...]=mm(mixed[mine],wo[...])
        elif name=="tr": rowsT[...]=rows[...].T
        elif name=="sec":
            need(p=1)
            middle=T[mine].astype(F32)+(own[...]+rcv[...].astype(F32))
            mid[...]=middle
            xh,_=unit(middle)
            SA[qo]=(xh*g2[...]).astype(BF)
            go("xa","yb","xb","ya")
        elif name=="bo":
            need(w=nh)
            for k in l_own: k.wait()
            block(qo,True)
        elif name=="dno": down(qo)
        elif name=="bx":
            need(xa=1,xb=1,cx=1)
            block(qx,False); go("Xa")
        elif name=="by":
            need(ya=1,yb=1,cy=1)
            block(qy,False); go("Yb")
        elif name=="bd":
            need(xa=2,yb=2,cy=2)
            block(qd,False); go("Da","Db")
        elif name=="gu":
            sa=SA[...].reshape(4*R,d)
            for j in range(nh//2):
                t=mm_tn(sa,dpre[:,:,pl.ds(2*j*fs,2*fs)].reshape(4*R,2*fs)).astype(BF)
                gu[2*j]=t[:,:fs]; gu[2*j+1]=t[:,fs:]
            go("u")
        elif name=="dn":
            for q in (qx,qy,qd): down(q)
        elif name=="gd":
            ca=CA[...].reshape(4*R,d)
            for j in range(nh): gd[j]=mm_tn(act[:,:,pl.ds(j*fs,fs)].reshape(4*R,fs),ca).astype(BF)
            go("v")
        elif name=="ab": go("A")
        elif name=="fin":
            need(Da=2,Db=2,Xa=1,Yb=1)
            dx,g=norm_back(mid[...],own[...]+(rx[...].astype(F32)+ry[...].astype(F32)),g2[...])
            gn2[...]=g
            dm=CA[qo].astype(F32)+dx
            dmid[...]=dm
            db[mine]=dm.astype(BF)
            go("b")
        elif name=="dm": datt[mine]=mm_nt(db[mine],wo[...])
        elif name=="do":
            need(b=1)
            go("B")
            datt[other]=mm_nt(db[other],wo[...])
        elif name=="go":
            G0[...]=mm_tn(mixed[...],db[...]).astype(BF)
            go("0")
        elif name[0]=="p" and len(name)==2 and name[1].isdigit():
            p=int(name[1])
            if p<pairs: pair(p); go(str(p+1))
        elif name=="fo": go("f")
        elif name=="fm": go("n")
        elif name in chains: go(name)
    go("t","cy","cx","w")
    l_wo=lc(wout,wo)
    l_own=[lc(wup.at[:,at(qo)],Wu.at[:,at(z)]),lc(wdn.at[at(qo)],Wd.at[at(z)]),lc(cot,CA.at[qo])]
    for name in ORDER: do(name)
    for name in chains:
        for _ in chains[name]: pass
    for k,when in wires.all: only(when,k.wait_send)
    for k in pend: k.wait()

def layer(length,tok,cot,g1,g2,wqkv,wf,wout,wup,wdn):
    R,d=tok.shape; n=2*R; H=R//2; c=wout.shape[0]; h=wf.shape[1]; hd=wf.shape[-1]; pairs=h//2; w=2*hd; q=3*d+2*w
    f=wup.shape[1]; fs=f//4; nz=lax.axis_size("hidden")
    D=pltpu.SemaphoreType.DMA
    b=lambda *s: pltpu.VMEM(s,BF)
    e=lambda *s: pltpu.VMEM(s,F32)
    return pl.pallas_call(layer_kernel,
      out_shape=(S((R,d),BF),S((R,d),F32),S((2,2,2,2,c//16,d),BF),S((pairs,2,2,2,2,q//16,w),BF),S((d,f),BF),S((4,fs,d),BF),S((8,d),F32)),
      in_specs=[SM,ANY,ANY,VM,VM,ANY,VM,ANY,ANY,ANY],
      out_specs=[ANY]*6+[VM],
      scratch_shapes=[b(n,d),b(n,d),b(d,n),b(3,d,c),b(c,d),b(3,n,c),b(2,pairs,n,2*w),b(n,c),e(n,c),e(R,d),b(R,d),b(R,d),e(R,d),
        b(4,R,d),b(4,R,d),b(d,f),b(f,d),b(4,R,f),b(4,R,f),b(4,R,d),b(4,R,d),b(nz,d,fs),b(nz,fs,d),b(nz,d//2,fs),b(nz,fs//2,d),
        b(2,d//2,fs),b(2,fs//2,d),b(d//2,fs),b(fs//2,d),b(R,d),b(R,d),b(H,d),b(H,d),
        e(R,d),b(n,d),e(n,c),b(3,n,c),b(c,d),b(pairs,q,w),b(c//2,d),b(pairs,q//2,w),b(c//4,d),b(pairs,q//4,w),
        b(c//8,d),b(pairs,q//8,w),b(c//16,d),b(pairs,q//16,w),
        b(2,H,d),b(2,H,d),b(H,d),b(H,d),b(R,d),b(R,d),b(R,d),e(1,d),e(1,d),e(6,8,d),e(5,8,d),
        b(2,pairs,w,w),D((24,)),D((2,128))],
      compiler_params=pltpu.CompilerParams(vmem_limit_bytes=63*2**20,collective_id=1,has_side_effects=True),
      cost_estimate=pl.CostEstimate(flops=24*10**9,bytes_accessed=40*10**6,transcendentals=2*10**6))(
      length,tok,cot,g1,g2,wqkv,wf,wout,wup,wdn)

def per_device_k1(
    tokens, lengths, norm_first, w_qkv, w_feature, w_out, norm_second, w_up, w_down, cotangent
):
    h,hd=w_feature.shape[1],w_feature.shape[3]; w=2*hd
    block_out,grad_tokens,go,gp,gu,gd,gn=layer(lengths,tokens[0],cotangent[0],norm_first[None],norm_second[None],jnp.transpose(w_qkv,(1,0,2)),w_feature,w_out,w_up,w_down)
    go=go.reshape(w_out.shape); gp=gp.reshape(h//2,-1,w)
    go,gq,gf,gu,gd,block_out,grad_tokens,n1,n2=finish(go,gp,gu,gd.reshape(gd.shape[0]*gd.shape[1],-1),block_out,grad_tokens,gn,hd)
    return (
        block_out[None],
        grad_tokens[None],
        n1[0],
        jnp.transpose(gq,(1,0,2)),
        gf,
        go,
        n2[0],
        gu,
        gd,
    )

def finish_kernel(go,g0,g1,g2,gf,gu,gd,bo,gt,gn,go_o,gq_o,gf_o,gu_o,gd_o,bo_o,gt_o,n1_o,n2_o):
    for a,b in ((go,go_o),(gu,gu_o),(gd,gd_o)): b[...]=a[...].astype(F32)
    bo_o[...]=bo[...]
    gt_o[...]=gt[...]
    pairs,_,w=g0.shape; hd=w//2
    for t,g in enumerate((g0,g1,g2)):
        for p in range(pairs): gq_o[t,:,p*w:(p+1)*w]=g[p].astype(F32)
    @pl.when(pl.program_id(0)==0)
    def _():
        n1_o[...]=gn[0:1]; n2_o[...]=gn[1:2]
        for t in range(2):
            for p in range(pairs):
                for s in range(2):
                    gf_o[t,2*p+s]=gf[p,t*w+s*hd:t*w+(s+1)*hd,s*hd:(s+1)*hd].astype(F32)

def finish(go,gp,gu,gd,bo,gt,gn,hd,N=2):
    c,d=go.shape; pairs,_,w=gp.shape; f=gu.shape[1]
    B=pl.BlockSpec
    row=lambda a: B((a.shape[0]//N,a.shape[1]),lambda i:(i,0))
    all_=lambda a: B(a.shape,lambda i:(0,)*len(a.shape))
    part=lambda t: B((pairs,d//N,w),lambda i:(0,i+N*t,0))
    gf=S((2,2*pairs,hd,hd),F32); n=S((1,d),F32)
    return pl.pallas_call(finish_kernel,grid=(N,),
      out_shape=(S((c,d),F32),S((3,d,c),F32),gf,S((d,f),F32),S((f,d),F32),S(bo.shape,BF),S(gt.shape,F32),n,n),
      in_specs=[row(go),part(0),part(1),part(2),B((pairs,2*w,w),lambda i:(0,3*d//(2*w),0)),row(gu),row(gd),row(bo),row(gt),all_(gn)],
      out_specs=[row(go),B((3,d//N,c),lambda i:(0,i,0)),all_(gf),row(gu),row(gd),row(bo),row(gt),all_(n),all_(n)],
      compiler_params=pltpu.CompilerParams(vmem_limit_bytes=62*2**20))(go,gp,gp,gp,gp,gu,gd,bo,gt,gn)


def solution(mesh):
    in_specs = (
        P(("dp", "hidden"), "head", None),
        P(("dp", "hidden"), None),
        P(),
        P(None, None, "head"),
        P(None, "head", None, None),
        P("head", None),
        P(),
        P(None, "hidden"),
        P("hidden", None),
        P(("dp", "hidden"), "head", None),
    )
    out_specs = (
        P(("dp", "hidden"), "head", None),
        P(("dp", "hidden"), "head", None),
        P(),
        P(None, None, "head"),
        P(None, "head", None, None),
        P("head", None),
        P(),
        P(None, "hidden"),
        P("hidden", None),
    )
    near=dict(mesh.shape)=={"dp":4,"head":2,"hidden":4}
    return jax.shard_map(
        per_device_k1 if near else per_device, mesh=mesh, in_specs=in_specs, out_specs=out_specs, check_vma=False
    )
```

```python
import jax, jax.numpy as jnp
from jax import lax
from jax.experimental import pallas as pl
from jax.experimental.pallas import tpu as pltpu
from jax.sharding import PartitionSpec as P
BF=jnp.bfloat16; F32=jnp.float32
NT=(((1,),(1,)),((),()))
TN=(((0,),(0,)),((),()))
SB=256

def mm(a,b): return jnp.dot(a,b,preferred_element_type=F32)
def mm_nt(a,b): return lax.dot_general(a,b,NT,preferred_element_type=F32)
def mm_tn(a,b): return lax.dot_general(a,b,TN,preferred_element_type=F32)

def half_ones(width, size):
    r=lax.broadcasted_iota(jnp.int32,(width,width),0)//size
    c=lax.broadcasted_iota(jnp.int32,(width,width),1)//size
    return (r==c).astype(F32).astype(BF)

def first_half(shape, size):
    return lax.broadcasted_iota(jnp.int32,shape,1)%(2*size) < size

def half_sum(t, ones):
    hi=t.astype(BF); lo=(t-hi.astype(F32)).astype(BF)
    return mm(hi,ones)+mm(lo,ones)

def features(x, w2, ones, size):
    u=mm(x,w2)
    h0=first_half(u.shape,size)
    big=jnp.float32(3e38)
    def both(f, fill):
        return jnp.where(h0, f(jnp.where(h0,u,fill)), f(jnp.where(h0,fill,u)))
    top=both(lambda t: jnp.max(t,axis=1,keepdims=True), -big)
    low=both(lambda t: jnp.min(t,axis=1,keepdims=True), big)
    e=jnp.concatenate([jnp.exp(u-top),jnp.exp(low-u)],axis=1)
    s=mm(e.astype(BF),ones)
    return e/s

def halves(t, h0):
    z=jnp.zeros_like(t)
    return jnp.where(h0,t,z), jnp.where(h0,z,t)

def attend(fq, fk, v, size):
    n=fq.shape[0]
    h0=first_half(fq.shape,size)
    fqs=halves(fq,h0)
    hv=first_half(v.shape,size)
    one=jnp.ones(v.shape,BF)
    ve=halves(jnp.concatenate([v,one],axis=1),h0)
    outs=[]
    for r in range(0,n,SB):
        ext=r+SB
        keep=(lax.broadcasted_iota(jnp.int32,(SB,ext),0)+r)>=lax.broadcasted_iota(jnp.int32,(SB,ext),1)
        acc=None
        for s in range(2):
            sc=mm_nt(fqs[s][r:r+SB],fk[:ext])
            sc=jnp.where(keep,sc,0.0).astype(BF)
            t=mm(sc,ve[s][:ext])
            acc=t if acc is None else acc+t
        outs.append(acc)
    p=jnp.concatenate(outs,axis=0)
    w=v.shape[1]
    rden=1.0/p[:,w:]
    return p[:,:w]*rden, rden

def attend_back(fq,fk,v,mixed,rden,datt,ones,size):
    n,w=v.shape
    wide=(n,2*w)
    h0=first_half(wide,size)
    dn=(datt*rden).astype(BF)
    dd=-half_sum(datt*mixed.astype(F32),ones)*rden
    hi=dd.astype(BF); lo=(dd-hi.astype(F32)).astype(BF)
    lane=lax.broadcasted_iota(jnp.int32,(n,w),1)%size
    zero=jnp.zeros((n,w),BF)
    ext_=jnp.where(lane==0,hi,jnp.where(lane==1,lo,zero))
    nx=halves(jnp.concatenate([dn,ext_],axis=1),h0)
    vx=jnp.concatenate([v,jnp.ones((n,w),BF)],axis=1)
    fqs=halves(fq,h0); fks=halves(fk,h0)
    dfq=[];dfk=[];dv=[]
    for r in range(0,n,SB):
        ext=r+SB
        keep=(lax.broadcasted_iota(jnp.int32,(SB,ext),0)+r)>=lax.broadcasted_iota(jnp.int32,(SB,ext),1)
        acc=0.0
        for s in range(2):
            ds=jnp.where(keep,mm_nt(nx[s][r:r+SB],vx[:ext]),0.0).astype(BF)
            acc=acc+mm(ds,fks[s][:ext])
        dfq.append(acc)
        left=n-r
        keep=lax.broadcasted_iota(jnp.int32,(SB,left),0)<=lax.broadcasted_iota(jnp.int32,(SB,left),1)
        ak=0.0; av=0.0
        for s in range(2):
            ds=jnp.where(keep,mm_nt(vx[r:r+SB],nx[s][r:]),0.0).astype(BF)
            ak=ak+mm(ds,fqs[s][r:])
            sc=jnp.where(keep,mm_nt(fk[r:r+SB],fqs[s][r:]),0.0).astype(BF)
            av=av+mm(sc,nx[s][r:,:w])
        dfk.append(ak); dv.append(av)
    cat=lambda t: jnp.concatenate(t,axis=0)
    return cat(dfq),cat(dfk),cat(dv)

def feature_back(f, df, ones):
    w=f.shape[1]//2
    f=f.astype(F32)
    part=f*(df-half_sum(f*df,ones))
    return (part[:,:w]-part[:,w:]).astype(BF)

def pair_weights(wf_ref, w2_ref):
    hd=wf_ref.shape[-1]
    w2_ref[...]=jnp.zeros_like(w2_ref)
    for t in range(2):
        for p in range(w2_ref.shape[1]):
            w2_ref[t,p,:hd,:hd]=wf_ref[t,2*p]
            w2_ref[t,p,hd:,hd:]=wf_ref[t,2*p+1]

def fwd_kernel(len_ref, rows_ref, wqkv_ref, wf_ref, wout_ref, proj_ref, feat_ref, mixed_ref, rden_ref, branch_ref, w2_ref):
    hd=wf_ref.shape[-1]; w=2*hd; n=rows_ref.shape[0]; pairs=w2_ref.shape[1]
    pair_weights(wf_ref,w2_ref)
    for i in range(3):
        proj_ref[i]=mm(rows_ref[...],wqkv_ref[i]).astype(BF)
    ones=half_ones(2*w,hd)
    valid=lax.broadcasted_iota(jnp.int32,(n,2*w),0)<len_ref[0,0]
    def body(p,_):
        c=pl.ds(pl.multiple_of(p*w,w),w)
        fq=features(proj_ref[0,:,c],w2_ref[0,p],ones,hd).astype(BF)
        fk=jnp.where(valid,features(proj_ref[1,:,c],w2_ref[1,p],ones,hd),0.0).astype(BF)
        feat_ref[0,p]=fq; feat_ref[1,p]=fk
        m,rd=attend(fq,fk,proj_ref[2,:,c],hd)
        mixed_ref[:,c]=m.astype(BF); rden_ref[:,c]=rd
        return 0
    lax.fori_loop(0,pairs,body,0)
    branch_ref[...]=mm(mixed_ref[...],wout_ref[...]).astype(branch_ref.dtype)

def bwd_kernel(rows_ref,wqkv_ref,wf_ref,wout_ref,proj_ref,feat_ref,mixed_ref,rden_ref,dbr_ref,
               gq_ref,gf_ref,go_ref,dfirst_ref,w2_ref,datt_ref,dproj_ref):
    hd=wf_ref.shape[-1]; w=2*hd; n=rows_ref.shape[0]; pairs=w2_ref.shape[1]
    pair_weights(wf_ref,w2_ref)
    ones=half_ones(2*w,hd); ones1=half_ones(w,hd)
    datt_ref[...]=mm_nt(dbr_ref[...],wout_ref[...])
    go_ref[...]=mm_tn(mixed_ref[...],dbr_ref[...]).astype(go_ref.dtype)
    def body(p,_):
        c=pl.ds(pl.multiple_of(p*w,w),w)
        fq=feat_ref[0,p]; fk=feat_ref[1,p]
        dfq,dfk,dv=attend_back(fq,fk,proj_ref[2,:,c],mixed_ref[:,c],rden_ref[:,c],datt_ref[:,c],ones1,hd)
        for t,(f,df) in enumerate(((fq,dfq),(fk,dfk))):
            du=feature_back(f,df,ones)
            g=mm_tn(proj_ref[t,:,c],du)
            gf_ref[t,2*p]=g[:hd,:hd].astype(gf_ref.dtype); gf_ref[t,2*p+1]=g[hd:,hd:].astype(gf_ref.dtype)
            dproj_ref[t,:,c]=mm_nt(du,w2_ref[t,p]).astype(BF)
        dproj_ref[2,:,c]=dv.astype(BF)
        return 0
    lax.fori_loop(0,pairs,body,0)
    acc=None
    for i in range(3):
        gq_ref[i]=mm_tn(rows_ref[...],dproj_ref[i]).astype(gq_ref.dtype)
        t=mm_nt(dproj_ref[i],wqkv_ref[i])
        acc=t if acc is None else acc+t
    dfirst_ref[...]=acc.astype(dfirst_ref.dtype)
VM=pl.BlockSpec(memory_space=pltpu.VMEM)
SM=pl.BlockSpec(memory_space=pltpu.SMEM)
S=jax.ShapeDtypeStruct
def fwd(length,rows,wqkv,wf,wout):
    n,d=rows.shape; c=wout.shape[0]; h=wf.shape[1]; hd=wf.shape[-1]
    return pl.pallas_call(fwd_kernel,
      out_shape=(S((3,n,c),BF),S((2,h//2,n,4*hd),BF),S((n,c),BF),S((n,c),F32),S((n,d),BF)),
      in_specs=[SM,VM,VM,VM,VM],out_specs=[VM]*5,
      scratch_shapes=[pltpu.VMEM((2,h//2,2*hd,2*hd),BF)],
      compiler_params=pltpu.CompilerParams(vmem_limit_bytes=56*2**20))(length,rows,wqkv,wf,wout)
def bwd(rows,wqkv,wf,wout,proj,feat,mixed,rden,dbr):
    n,d=rows.shape; c=wout.shape[0]; h=wf.shape[1]; hd=wf.shape[-1]
    return pl.pallas_call(bwd_kernel,
      out_shape=(S((3,d,c),BF),S((2,h,hd,hd),F32),S((c,d),BF),S((n,d),BF)),
      in_specs=[VM]*9,out_specs=[VM]*4,
      scratch_shapes=[pltpu.VMEM((2,h//2,2*hd,2*hd),BF),pltpu.VMEM((n,c),F32),pltpu.VMEM((3,n,c),BF)],
      compiler_params=pltpu.CompilerParams(vmem_limit_bytes=56*2**20))(rows,wqkv,wf,wout,proj,feat,mixed,rden,dbr)

EPS=1e-05

def normalize(values, gain):
    average = jnp.mean(values, axis=-1, keepdims=True)
    centred = values - average
    spread = jnp.mean(centred * centred, axis=-1, keepdims=True)
    return centred * lax.rsqrt(spread + EPS) * gain

def smooth_gate(values):
    return jax.nn.gelu(values, approximate=True)

def per_device(
    tokens, lengths, norm_first, w_qkv, w_feature, w_out, norm_second, w_up, w_down, cotangent
):
    wqkv=jnp.transpose(w_qkv,(1,0,2))
    residual_in = tokens[0].astype(jnp.float32)
    normed_first, first_back = jax.vjp(normalize, residual_in, norm_first)
    first_low = normed_first.astype(jnp.bfloat16)
    first_rows = lax.all_gather(first_low, "head", axis=0, tiled=True)
    cot_low = cotangent[0]
    cot_rows = lax.all_gather(cot_low, "hidden", axis=0, tiled=True)
    proj,feat,mixed,rden,part=fwd(lengths,first_rows,wqkv,w_feature,w_out)
    branch = lax.psum_scatter(part, "head", scatter_dimension=0, tiled=True).astype(jnp.float32)
    middle = residual_in + branch
    normed_second, second_back = jax.vjp(normalize, middle, norm_second)
    second_low = normed_second.astype(jnp.bfloat16)
    second_rows = lax.all_gather(second_low, "hidden", axis=0, tiled=True)
    hidden_pre = jnp.dot(second_rows, w_up, preferred_element_type=jnp.float32)
    active = smooth_gate(hidden_pre).astype(jnp.bfloat16)
    gate_grad = jax.vjp(smooth_gate, hidden_pre)[1]
    d_active = jnp.einsum("nd,fd->nf", cot_rows, w_down, preferred_element_type=jnp.float32)
    d_pre = gate_grad(d_active)[0].astype(jnp.bfloat16)
    d_second = lax.psum_scatter(
        jnp.einsum("nf,df->nd", d_pre, w_up, preferred_element_type=jnp.float32).astype(jnp.bfloat16),
        "hidden",
        scatter_dimension=0,
        tiled=True,
    ).astype(jnp.float32)
    mlp_result = lax.psum_scatter(
        jnp.dot(active, w_down, preferred_element_type=jnp.float32).astype(jnp.bfloat16),
        "hidden",
        scatter_dimension=0,
        tiled=True,
    ).astype(jnp.float32)
    block_out = (middle + mlp_result).astype(jnp.bfloat16)
    grad_down = jnp.einsum("nf,nd->fd", active, cot_rows, preferred_element_type=jnp.float32)
    grad_up = jnp.einsum("nd,nf->df", second_rows, d_pre, preferred_element_type=jnp.float32)
    d_middle_norm, grad_norm_second = second_back(d_second)
    d_middle = cot_low.astype(jnp.float32) + d_middle_norm
    d_branch_rows = lax.all_gather(d_middle.astype(jnp.bfloat16), "head", axis=0, tiled=True)
    gq,grad_feature,go,dfirst=bwd(first_rows,wqkv,w_feature,w_out,proj,feat,mixed,rden,d_branch_rows)
    d_first = lax.psum_scatter(dfirst, "head", scatter_dimension=0, tiled=True).astype(jnp.float32)
    d_input_norm, grad_norm_first = first_back(d_first)
    grad_tokens = d_middle + d_input_norm
    grad_up, grad_down = (
        lax.psum(grad_up.astype(jnp.bfloat16), ("dp", "head")).astype(jnp.float32),
        lax.psum(grad_down.astype(jnp.bfloat16), ("dp", "head")).astype(jnp.float32),
    )
    gq, grad_feature, go = (
        lax.psum(gq, ("dp", "hidden")).astype(jnp.float32),
        lax.psum(grad_feature.astype(jnp.bfloat16), ("dp", "hidden")).astype(jnp.float32),
        lax.psum(go, ("dp", "hidden")).astype(jnp.float32),
    )
    grad_norm_first, grad_norm_second = lax.psum(
        (grad_norm_first, grad_norm_second), ("dp", "head", "hidden")
    )
    return (
        block_out[None],
        grad_tokens[None],
        grad_norm_first,
        jnp.transpose(gq,(1,0,2)),
        grad_feature,
        go,
        grad_norm_second,
        grad_up,
        grad_down,
    )


ORDER=("n0","w","t","n1","a","cy","pt","cz","po","w","cx","pa","sa","pb","sb","cy","tr","w","ya","xa","cz","xb","yb","w","bx","by","bo","ya","xb","bd","gu","Yb","gd","Xa","u","Da","Db","v","dno","dn","A!","Da","Db","fin","B!","u","dm","v","b","go","do","u","0","p0","B","p1","1","0","v","p2","0","3","A","2","1","p3","3","4","0","u","2","v","3","fo","0","1","4","fm","0","3","n","2","u","4","1","3","B","2","4","1","A","3","4","n","2","v","1","u","u","n","4","0","2","f","1","3","v","0","n","3","4","v","2","1","4","n","2")
EARLY_X=(3,)
SUM_ALL=()
GATHER_ALL=()
ROWS_X_FIRST=True

MESH=pl.DeviceIdType.MESH
ANY=pl.BlockSpec(memory_space=pl.ANY)
EPS=1e-05

def place():
    dp=lax.axis_index("dp")
    return dp//2, dp%2, lax.axis_index("head"), lax.axis_index("hidden")

def only(when,act):
    if when is None: act()
    else: pl.when(when)(act)

class Wires:
    def __init__(self,sems):
        self.sems=sems; self.count=0; self.all=[]
    def send(self,src,dst,dev,when=None):
        i=self.count
        self.count+=1
        k=pltpu.make_async_remote_copy(src_ref=src,dst_ref=dst,send_sem=self.sems.at[0,i],recv_sem=self.sems.at[1,i],device_id=dev,device_id_type=MESH)
        only(when,k.start)
        self.all.append((k,when))
        return k

def greet(peers):
    bar=pltpu.get_barrier_semaphore()
    for d in peers: pl.semaphore_signal(bar,inc=1,device_id=d,device_id_type=MESH)
    pl.semaphore_wait(bar,len(peers))

def unit(values):
    centred=values-jnp.mean(values,axis=-1,keepdims=True)
    r=lax.rsqrt(jnp.mean(centred*centred,axis=-1,keepdims=True)+EPS)
    return centred*r, r

def norm_back(values,grad,gain):
    xh,r=unit(values)
    e=grad*gain
    inner=e-jnp.mean(e,axis=-1,keepdims=True)-xh*jnp.mean(e*xh,axis=-1,keepdims=True)
    return r*inner, jnp.sum(grad*xh,axis=0,keepdims=True)

def gate(v):
    k=0.7978845608; a=0.044715
    sq=v*v
    t=jnp.tanh(k*v*(1.0+a*sq))
    half=0.5*(1.0+t)
    return v*half, half+0.5*v*(1.0-t*t)*(k+(3.0*a*k)*sq)

def add_into(dst,src,step):
    rows=dst.shape[0]
    def body(i,_):
        r=pl.ds(pl.multiple_of(i*step,step),step)
        dst[r]=(dst[r].astype(F32)+src[r].astype(F32)).astype(dst.dtype)
        return 0
    lax.fori_loop(0,rows//step,body,0)

def layer_kernel(len_ref,tok,cot,g1,g2,wqkv,wf,wout,wup,wdn,
                 bo_o,gt_o,go_o,gp_o,gu_o,gd_o,gn_o,
                 T,rows,rowsT,wq,wo,proj,feat,mixed,rden,own,snd,rcv,mid,
                 SA,CA,Wu,Wd,act,dpre,P,ML,gu,gd,cu,cd,zu,zd,mu,md,yu,yd,rx,ry,rdx,rdy,
                 dmid,db,datt,dproj,G0,GP,C0,CP,X0,XP,U0,UP,W0,WP,
                 ma,mb,na,nb,bo,dfs,dfr,gn2,gsum,gn,gr,w2,loc,sems):
    x,c,y,z=place()
    nh=lax.axis_size("hidden"); last=nh-1
    nx,ny,nc=((1-x)*2+c,y,z),(x*2+c,1-y,z),(x*2+1-c,y,z)
    low,side=z%2,z//2
    z1,z2=z+1-2*low,(z+2)%nh
    inner=low!=side
    mate=(x*2+c,y,last-z)
    n1,n2=(x*2+c,y,z1),(x*2+c,y,z2)
    R,d=tok.shape; n=2*R; H=R//2
    hd=wf.shape[-1]; w=2*hd; pairs=w2.shape[1]; f=wup.shape[1]; fs=f//4
    qo,qx,qy,qd=x*2+y,(1-x)*2+y,x*2+1-y,(1-x)*2+1-y
    mine=pl.ds(pl.multiple_of(y*R,R),R); other=pl.ds(pl.multiple_of((1-y)*R,R),R)
    A=pl.ds(0,H); B=pl.ds(H,H)
    half=lambda size,b: pl.ds(pl.multiple_of(b*size,size),size)
    hu,hw=d//2,fs//2
    uo,ua,vo,va=half(hu,c),half(hu,1-c),half(hw,c),half(hw,1-c)
    at=lambda q: pl.ds(pl.multiple_of(q*fs,fs),fs)
    nloc=[0]; pend=[]; seen=[]
    def lc(s,t,out=False):
        k=pltpu.make_async_copy(s,t,loc.at[nloc[0]]); nloc[0]+=1
        k.start()
        if out: pend.append(k)
        return k
    wires=Wires(sems)
    send=wires.send
    l_tok=lc(tok,T.at[mine])
    l_wq=[lc(wqkv.at[i],wq.at[i]) for i in range(3)]
    greet((nx,ny,nc)+tuple((x*2+c,y,(z+t)%nh) for t in range(1,nh)))

    def simple(src,dst,dev):
        k=send(src,dst,dev)
        yield
        k.wait_recv()

    def onward(src,dst,dev,src2,dst2,dev2,between=None):
        k=send(src,dst,dev)
        yield
        k.wait_recv()
        if between is not None: between()
        k=send(src2,dst2,dev2)
        yield
        k.wait_recv()

    def weights():
        wdh=lambda q: pl.ds(pl.multiple_of(q*fs+c*hw,hw),hw)
        wdo=lambda q: pl.ds(pl.multiple_of(q*fs+(1-c)*hw,hw),hw)
        for s in range(1,nh):
            now=[]
            for right in (True,False):
                j=(z-s+1) if right else (z+s-1)
                when=((z<last)&(j>=0)) if right else ((z>0)&(j<=last))
                jj=jnp.clip(j,0,last)
                dev=(x*2+c,y,jnp.clip(z+1 if right else z-1,0,last))
                if s==1: su,sd=wup.at[uo,at(qo)],wdn.at[wdh(qo)]
                else: su,sd=Wu.at[uo,at(jj)],Wd.at[wdh(jj)]
                got=(z-s>=0) if right else (z+s<=last)
                now.append((send(su,Wu.at[uo,at(jj)],dev,when),send(sd,Wd.at[wdh(jj)],dev,when),got))
            yield
            for a,b,got in now: only(got,a.wait_recv); only(got,b.wait_recv)
            for right,(_,_,got) in zip((True,False),now):
                jj=jnp.clip((z-s) if right else (z+s),0,last)
                shared.append((send(Wu.at[uo,at(jj)],Wu.at[uo,at(jj)],nc,got),got))
                shared.append((send(Wd.at[wdh(jj)],Wd.at[wdh(jj)],nc,got),got))
        yield
        for k,got in shared: only(got,k.wait_recv)
    shared=[]

    def grads(G,bufs,O,early,sum_all,gather_all):
        steps=[(nc,c),(nx,x),(n1,low),(n2,side)]
        size=G.shape[0]; base=0
        for i in range(2 if sum_all else 4):
            dev,bit=steps[i]
            size//=2
            away=pl.multiple_of(base+(1-bit)*size,16)
            base=pl.multiple_of(base+bit*size,16)
            k=send(G.at[pl.ds(away,size)],bufs[i],dev)
            yield
            k.wait_recv()
            add_into(G.at[pl.ds(base,size)],bufs[i],size//2 if size%32==0 else size)
        if sum_all:
            size//=4
            slots=[bufs[2].at[pl.ds(0,size)],bufs[2].at[pl.ds(size,size)],bufs[3]]
            ks=[]
            for t in (2,1,3):
                j=(z+t)%nh
                piece=pl.ds(pl.multiple_of(base+(2*(j%2)+j//2)*size,16),size)
                ks.append(send(G.at[piece],slots[t-1],(x*2+c,y,j)))
            yield
            base=pl.multiple_of(base+(2*low+side)*size,16)
            for k in ks: k.wait_recv()
            for s in slots: add_into(G.at[pl.ds(base,size)],s,size)
        src=G.at[pl.ds(base,size)]
        place_=[c,x,low,side]
        copy=lc(src,O.at[tuple(place_)])
        def gather(devs,*dims):
            nonlocal src,copy
            ks=[send(O.at[tuple(place_)] if src is None else src,O.at[tuple(place_)],dev) for dev in devs]
            src=None
            yield
            for k in ks: k.wait_recv()
            if copy is not None: copy.wait()
            copy=None
            for i in dims: place_[i]=slice(None)
        if early: yield from gather([nx],1)
        if gather_all: yield from gather([(x*2+c,y,(z+t)%nh) for t in (2,1,3)],2,3)
        else:
            yield from gather([n2],3)
            yield from gather([n1],2)
        if not early: yield from gather([nx],1)
        yield from gather([nc],0)

    def mlp_grads(W,kept,away,core,far,middle,final,whole,piece,step):
        two=lambda i: pl.ds(pl.multiple_of(2*i,2),2)
        k=send(W.at[:,away],core,nc)
        yield
        k.wait_recv()
        for j in range(nh): add_into(W.at[j,kept],core.at[j],step)
        k=send(W.at[two(1-low),kept],far,n1)
        yield
        k.wait_recv()
        for j in range(2): add_into(W.at[2*low+j,kept],far.at[j],step)
        m=send(W.at[two(low),kept],middle,mate,inner)
        yield
        def take():
            m.wait_recv()
            k.wait_send()
            for j in range(2): W[2*side+j,kept]=middle[j]
        pl.when(inner)(take)
        seen.append(k)
        k2=send(W.at[2*side+1-low,kept],final,n1)
        yield
        k2.wait_recv()
        add_into(W.at[z,kept],final,step)
        l=lc(W.at[z,kept],piece(qo))
        k=send(W.at[z,kept],piece(qo),nx)
        k2=send(W.at[z,kept],piece(qo),ny)
        yield
        k.wait_recv()
        k=send(piece(qx),piece(qx),ny)
        yield
        k.wait_recv(); k2.wait_recv(); l.wait()
        k=send(whole,whole,nc)
        yield
        k.wait_recv()

    def mlp_rows(r,near,dev,q1,q2,buf,far,q3):
        k=[send(ML.at[q1,r],buf.at[0],near),send(ML.at[q2,r],buf.at[1],near)]
        yield
        for t in k: t.wait_recv()
        add_into(ML.at[qo,r],buf.at[0],H); add_into(ML.at[q3,r],buf.at[1],H)
        k=send(ML.at[q3,r],far,dev)
        yield
        k.wait_recv()
        bo[r]=(mid[r]+(ML[qo,r].astype(F32)+far[...].astype(F32))).astype(BF)
        lc(bo.at[r],bo_o.at[r],True)

    def first_grad(r):
        t=mm_nt(dproj[0,r],wq[0])+mm_nt(dproj[1,r],wq[1])
        return t+mm_nt(dproj[2,r],wq[2])

    def first_rows():
        t=first_grad(other)
        dfs[...]=t.astype(BF)
        k=send(dfs,dfr,ny)
        xo,_=unit(T[other].astype(F32))
        gsum[...]=jnp.sum(t*xo,axis=0,keepdims=True)
        yield
        k.wait_recv()
        dx,_=norm_back(T[mine].astype(F32),own[...]+dfr[...].astype(F32),g1[...])
        dmid[...]=dmid[...]+dx
        lc(dmid,gt_o,True)

    def gains():
        t=first_grad(mine)
        own[...]=t
        xm,_=unit(T[mine].astype(F32))
        gn[...]=jnp.zeros_like(gn)
        gn[0,0:1]=gsum[...]+jnp.sum(t*xm,axis=0,keepdims=True)
        gn[0,1:2]=gn2[...]
        order=[nc,nx,ny,n1,n2]
        for i,dev in enumerate(order):
            k=send(gn.at[i],gr.at[i],dev)
            yield
            k.wait_recv()
            gn[i+1]=gn[i]+gr[i]
        gn_o[...]=gn[len(order)]

    def sum_a(): P[qy,A]=(P[qy,A].astype(F32)+rdx[...].astype(F32)).astype(BF)
    def sum_b(): P[qx,B]=(P[qx,B].astype(F32)+rdy[...].astype(F32)).astype(BF)
    S_=lambda q,r: SA.at[q,r]
    chains={
        "t":simple(tok,T.at[mine],ny),
        "w":weights(),
        "cx":simple(cot,CA.at[qo],nx),
        "cy":onward(cot.at[A],CA.at[qo,A],ny,CA.at[qy,A],CA.at[qy,A],nx),
        "cz":onward(cot.at[B],CA.at[qo,B],ny,CA.at[qy,B],CA.at[qy,B],nx),
        "pa":simple(snd.at[A],rcv.at[A],ny),
        "pb":simple(snd.at[B],rcv.at[B],ny),
        "xa":simple(S_(qo,A),S_(qo,A),nx),
        "yb":simple(S_(qo,B),S_(qo,B),ny),
        "xb":onward(S_(qo,B),S_(qo,B),nx,S_(qx,B),S_(qx,B),ny),
        "ya":onward(S_(qo,A),S_(qo,A),ny,S_(qy,A),S_(qy,A),nx),
        "Xa":simple(P.at[qx,A],rx.at[A],nx),
        "Yb":simple(P.at[qy,B],ry.at[B],ny),
        "Da":onward(P.at[qd,A],rdx,nx,P.at[qy,A],ry.at[A],ny,sum_a),
        "Db":onward(P.at[qd,B],rdy,ny,P.at[qx,B],rx.at[B],nx,sum_b),
        "b":simple(db.at[mine],db.at[mine],ny),
        "u":mlp_grads(gu,uo,ua,cu,zu,mu,yu,gu_o.at[uo],lambda q: gu_o.at[uo,at(q)],64),
        "v":mlp_grads(gd,vo,va,cd,zd,md,yd,gd_o.at[:,vo],lambda q: gd_o.at[q,vo],16),
        "A":mlp_rows(A,nx,ny,qx,qd,ma,na,qy),"B":mlp_rows(B,nx,ny,qx,qd,mb,nb,qy) if ROWS_X_FIRST else mlp_rows(B,ny,nx,qy,qd,mb,nb,qx),
        "f":first_rows(),"n":gains(),
        "0":grads(G0,(C0,X0,U0,W0),go_o,-1 in EARLY_X,-1 in SUM_ALL,-1 in GATHER_ALL)}
    for p in range(pairs): chains[str(p+1)]=grads(GP.at[p],(CP.at[p],XP.at[p],UP.at[p],WP.at[p]),gp_o.at[p],p in EARLY_X,p in SUM_ALL,p in GATHER_ALL)
    turns={name:-1 for name in chains}
    def go(*names):
        for name in names:
            next(chains[name],None)
            turns[name]+=1
    def need(**steps):
        for name,count in steps.items():
            while turns[name]<count: go(name)

    ones=half_ones(2*w,hd); ones1=half_ones(w,hd)
    valid=lax.broadcasted_iota(jnp.int32,(n,2*w),0)<len_ref[0,0]
    def first(r):
        xh,_=unit(T[r].astype(F32))
        rows[r]=(xh*g1[...]).astype(BF)
    def project(r):
        for i in range(3): proj[i,r]=mm(rows[r],wq[i]).astype(BF)
    def heads(p,_):
        cc=pl.ds(pl.multiple_of(p*w,w),w)
        fq=features(proj[0,:,cc],w2[0,p],ones,hd).astype(BF)
        fk=jnp.where(valid,features(proj[1,:,cc],w2[1,p],ones,hd),0.0).astype(BF)
        feat[0,p]=fq; feat[1,p]=fk
        m,rd=attend(fq,fk,proj[2,:,cc],hd)
        mixed[:,cc]=m.astype(BF); rden[:,cc]=rd
        return 0
    def second(start):
        r=pl.ds(start,H)
        middle=T[pl.ds(pl.multiple_of(y*R+start,H),H)].astype(F32)+(own[r]+rcv[r].astype(F32))
        mid[r]=middle
        xh,_=unit(middle)
        SA[qo,r]=(xh*g2[...]).astype(BF)
    def block(qi,keep):
        need(w=nh)
        while l_own: l_own.pop().wait()
        a,ga=gate(mm(SA[qi],Wu[...]))
        act[qi]=a.astype(BF)
        dp=(mm_nt(CA[qi],Wd[...])*ga).astype(BF)
        dpre[qi]=dp
        d2=mm_nt(dp,Wu[...])
        if keep: own[...]=d2
        else: P[qi]=d2.astype(BF)
    def down(qi): ML[qi]=mm(act[qi],Wd[...]).astype(BF)
    def pair(p):
        cc=slice(p*w,(p+1)*w)
        fq=feat[0,p]; fk=feat[1,p]
        dfq,dfk,dv=attend_back(fq,fk,proj[2,:,cc],mixed[:,cc],rden[:,cc],datt[:,cc],ones1,hd)
        parts=[]
        for t,(ft,df) in enumerate(((fq,dfq),(fk,dfk))):
            du=feature_back(ft,df,ones)
            GP[p,pl.ds(3*d+t*w,w)]=mm_tn(proj[t,:,cc],du).astype(BF)
            parts.append(mm_nt(du,w2[t,p]).astype(BF))
        parts.append(dv.astype(BF))
        for t in range(3): dproj[t,:,cc]=parts[t]
        g=mm(rowsT[...],jnp.concatenate(parts,axis=1)).astype(BF)
        for t in range(3): GP[p,pl.ds(t*d,d)]=g[:,t*w:(t+1)*w]
    def do(name):
        if name=="n0":
            pair_weights(wf,w2)
            l_tok.wait()
            first(mine)
            for k in l_wq: k.wait()
            project(mine)
        elif name=="n1":
            need(t=1)
            first(other); project(other)
        elif name=="a": lax.fori_loop(0,pairs,heads,0)
        elif name=="pt":
            l_wo.wait()
            snd[...]=mm(mixed[other],wo[...]).astype(BF)
            go("pa","pb")
        elif name=="po": own[...]=mm(mixed[mine],wo[...])
        elif name=="tr": rowsT[...]=rows[...].T
        elif name=="sa": need(pa=1); second(0); go("xa","ya")
        elif name=="sb": need(pb=1); second(H); go("xb","yb")
        elif name=="bo":
            block(qo,True)
        elif name=="dno": down(qo)
        elif name=="bx":
            need(xa=1,xb=1,cx=1)
            block(qx,False); go("Xa")
        elif name=="by":
            need(ya=1,yb=1,cy=1,cz=1)
            block(qy,False); go("Yb")
        elif name=="bd":
            need(xb=2,ya=2,cy=2,cz=2)
            block(qd,False); go("Da","Db")
        elif name=="gu":
            sa=SA[...].reshape(4*R,d)
            for j in range(nh//2):
                t=mm_tn(sa,dpre[:,:,pl.ds(2*j*fs,2*fs)].reshape(4*R,2*fs)).astype(BF)
                gu[2*j]=t[:,:fs]; gu[2*j+1]=t[:,fs:]
            go("u")
        elif name=="dn":
            for q in (qx,qy,qd): down(q)
        elif name=="gd":
            ca=CA[...].reshape(4*R,d)
            for j in range(nh): gd[j]=mm_tn(act[:,:,pl.ds(j*fs,fs)].reshape(4*R,fs),ca).astype(BF)
            go("v")
        elif name=="A!": go("A")
        elif name=="B!": go("B")
        elif name=="fin":
            need(Da=2,Db=2,Xa=1,Yb=1)
            dx,g=norm_back(mid[...],own[...]+(rx[...].astype(F32)+ry[...].astype(F32)),g2[...])
            gn2[...]=g
            dm=CA[qo].astype(F32)+dx
            dmid[...]=dm
            db[mine]=dm.astype(BF)
            go("b")
        elif name=="dm": datt[mine]=mm_nt(db[mine],wo[...])
        elif name=="do":
            need(b=1)
            datt[other]=mm_nt(db[other],wo[...])
        elif name=="go":
            G0[...]=mm_tn(mixed[...],db[...]).astype(BF)
            go("0")
        elif name[0]=="p" and len(name)==2 and name[1].isdigit():
            p=int(name[1])
            if p<pairs: pair(p); go(str(p+1))
        elif name=="fo": go("f")
        elif name=="fm": go("n")
        elif name in chains: go(name)
    go("t","cy","cz","cx","w")
    l_wo=lc(wout,wo)
    l_own=[lc(wup.at[:,at(qo)],Wu.at[:,at(z)]),lc(wdn.at[at(qo)],Wd.at[at(z)]),lc(cot,CA.at[qo])]
    for name in ORDER: do(name)
    for name in chains:
        for _ in chains[name]: pass
    outer=jnp.logical_not(inner)
    for k,when in wires.all: only(outer if any(k is t for t in seen) else when,k.wait_send)
    for k in pend: k.wait()

def layer(length,tok,cot,g1,g2,wqkv,wf,wout,wup,wdn):
    R,d=tok.shape; n=2*R; H=R//2; c=wout.shape[0]; h=wf.shape[1]; hd=wf.shape[-1]; pairs=h//2; w=2*hd; q=3*d+2*w
    f=wup.shape[1]; fs=f//4; nz=lax.axis_size("hidden")
    D=pltpu.SemaphoreType.DMA
    b=lambda *s: pltpu.VMEM(s,BF)
    e=lambda *s: pltpu.VMEM(s,F32)
    return pl.pallas_call(layer_kernel,
      out_shape=(S((R,d),BF),S((R,d),F32),S((2,2,2,2,c//16,d),BF),S((pairs,2,2,2,2,q//16,w),BF),S((d,f),BF),S((4,fs,d),BF),S((8,d),F32)),
      in_specs=[SM,ANY,ANY,VM,VM,ANY,VM,ANY,ANY,ANY],
      out_specs=[ANY]*6+[VM],
      scratch_shapes=[b(n,d),b(n,d),b(d,n),b(3,d,c),b(c,d),b(3,n,c),b(2,pairs,n,2*w),b(n,c),e(n,c),e(R,d),b(R,d),b(R,d),e(R,d),
        b(4,R,d),b(4,R,d),b(d,f),b(f,d),b(4,R,f),b(4,R,f),b(4,R,d),b(4,R,d),b(nz,d,fs),b(nz,fs,d),b(nz,d//2,fs),b(nz,fs//2,d),
        b(2,d//2,fs),b(2,fs//2,d),b(2,d//2,fs),b(2,fs//2,d),b(d//2,fs),b(fs//2,d),b(R,d),b(R,d),b(H,d),b(H,d),
        e(R,d),b(n,d),e(n,c),b(3,n,c),b(c,d),b(pairs,q,w),b(c//2,d),b(pairs,q//2,w),b(c//4,d),b(pairs,q//4,w),
        b(c//8,d),b(pairs,q//8,w),b(c//16,d),b(pairs,q//16,w),
        b(2,H,d),b(2,H,d),b(H,d),b(H,d),b(R,d),b(R,d),b(R,d),e(1,d),e(1,d),e(6,8,d),e(5,8,d),
        b(2,pairs,w,w),D((24,)),D((2,128))],
      compiler_params=pltpu.CompilerParams(vmem_limit_bytes=63*2**20,collective_id=1,has_side_effects=True),
      cost_estimate=pl.CostEstimate(flops=24*10**9,bytes_accessed=40*10**6,transcendentals=2*10**6))(
      length,tok,cot,g1,g2,wqkv,wf,wout,wup,wdn)

def per_device_k1(
    tokens, lengths, norm_first, w_qkv, w_feature, w_out, norm_second, w_up, w_down, cotangent
):
    h,hd=w_feature.shape[1],w_feature.shape[3]; w=2*hd
    block_out,grad_tokens,go,gp,gu,gd,gn=layer(lengths,tokens[0],cotangent[0],norm_first[None],norm_second[None],jnp.transpose(w_qkv,(1,0,2)),w_feature,w_out,w_up,w_down)
    go=go.reshape(w_out.shape); gp=gp.reshape(h//2,-1,w)
    go,gq,gf,gu,gd,block_out,grad_tokens,n1,n2=finish(go,gp,gu,gd.reshape(gd.shape[0]*gd.shape[1],-1),block_out,grad_tokens,gn,hd)
    return (
        block_out[None],
        grad_tokens[None],
        n1[0],
        jnp.transpose(gq,(1,0,2)),
        gf,
        go,
        n2[0],
        gu,
        gd,
    )

def finish_kernel(go,g0,g1,g2,gf,gu,gd,bo,gt,gn,go_o,gq_o,gf_o,gu_o,gd_o,bo_o,gt_o,n1_o,n2_o):
    for a,b in ((go,go_o),(gu,gu_o),(gd,gd_o)): b[...]=a[...].astype(F32)
    bo_o[...]=bo[...]
    gt_o[...]=gt[...]
    pairs,_,w=g0.shape; hd=w//2
    for t,g in enumerate((g0,g1,g2)):
        for p in range(pairs): gq_o[t,:,p*w:(p+1)*w]=g[p].astype(F32)
    @pl.when(pl.program_id(0)==0)
    def _():
        n1_o[...]=gn[0:1]; n2_o[...]=gn[1:2]
        for t in range(2):
            for p in range(pairs):
                for s in range(2):
                    gf_o[t,2*p+s]=gf[p,t*w+s*hd:t*w+(s+1)*hd,s*hd:(s+1)*hd].astype(F32)

def finish(go,gp,gu,gd,bo,gt,gn,hd,N=2):
    c,d=go.shape; pairs,_,w=gp.shape; f=gu.shape[1]
    B=pl.BlockSpec
    row=lambda a: B((a.shape[0]//N,a.shape[1]),lambda i:(i,0))
    all_=lambda a: B(a.shape,lambda i:(0,)*len(a.shape))
    part=lambda t: B((pairs,d//N,w),lambda i:(0,i+N*t,0))
    gf=S((2,2*pairs,hd,hd),F32); n=S((1,d),F32)
    return pl.pallas_call(finish_kernel,grid=(N,),
      out_shape=(S((c,d),F32),S((3,d,c),F32),gf,S((d,f),F32),S((f,d),F32),S(bo.shape,BF),S(gt.shape,F32),n,n),
      in_specs=[row(go),part(0),part(1),part(2),B((pairs,2*w,w),lambda i:(0,3*d//(2*w),0)),row(gu),row(gd),row(bo),row(gt),all_(gn)],
      out_specs=[row(go),B((3,d//N,c),lambda i:(0,i,0)),all_(gf),row(gu),row(gd),row(bo),row(gt),all_(n),all_(n)],
      compiler_params=pltpu.CompilerParams(vmem_limit_bytes=62*2**20))(go,gp,gp,gp,gp,gu,gd,bo,gt,gn)


def solution(mesh):
    in_specs = (
        P(("dp", "hidden"), "head", None),
        P(("dp", "hidden"), None),
        P(),
        P(None, None, "head"),
        P(None, "head", None, None),
        P("head", None),
        P(),
        P(None, "hidden"),
        P("hidden", None),
        P(("dp", "hidden"), "head", None),
    )
    out_specs = (
        P(("dp", "hidden"), "head", None),
        P(("dp", "hidden"), "head", None),
        P(),
        P(None, None, "head"),
        P(None, "head", None, None),
        P("head", None),
        P(),
        P(None, "hidden"),
        P("hidden", None),
    )
    near=dict(mesh.shape)=={"dp":4,"head":2,"hidden":4}
    return jax.shard_map(
        per_device_k1 if near else per_device, mesh=mesh, in_specs=in_specs, out_specs=out_specs, check_vma=False
    )
```

```python
import jax, jax.numpy as jnp
from jax import lax
from jax.experimental import pallas as pl
from jax.experimental.pallas import tpu as pltpu
from jax.sharding import PartitionSpec as P
BF=jnp.bfloat16; F32=jnp.float32
NT=(((1,),(1,)),((),()))
TN=(((0,),(0,)),((),()))
SB=256

def mm(a,b): return jnp.dot(a,b,preferred_element_type=F32)
def mm_nt(a,b): return lax.dot_general(a,b,NT,preferred_element_type=F32)
def mm_tn(a,b): return lax.dot_general(a,b,TN,preferred_element_type=F32)

def half_ones(width, size):
    r=lax.broadcasted_iota(jnp.int32,(width,width),0)//size
    c=lax.broadcasted_iota(jnp.int32,(width,width),1)//size
    return (r==c).astype(F32).astype(BF)

def first_half(shape, size):
    return lax.broadcasted_iota(jnp.int32,shape,1)%(2*size) < size

def half_sum(t, ones):
    hi=t.astype(BF); lo=(t-hi.astype(F32)).astype(BF)
    return mm(hi,ones)+mm(lo,ones)

def features(x, w2, ones, size):
    u=mm(x,w2)
    h0=first_half(u.shape,size)
    big=jnp.float32(3e38)
    def both(f, fill):
        return jnp.where(h0, f(jnp.where(h0,u,fill)), f(jnp.where(h0,fill,u)))
    top=both(lambda t: jnp.max(t,axis=1,keepdims=True), -big)
    low=both(lambda t: jnp.min(t,axis=1,keepdims=True), big)
    e=jnp.concatenate([jnp.exp(u-top),jnp.exp(low-u)],axis=1)
    s=mm(e.astype(BF),ones)
    return e/s

def halves(t, h0):
    z=jnp.zeros_like(t)
    return jnp.where(h0,t,z), jnp.where(h0,z,t)

def attend(fq, fk, v, size):
    n=fq.shape[0]
    h0=first_half(fq.shape,size)
    fqs=halves(fq,h0)
    hv=first_half(v.shape,size)
    one=jnp.ones(v.shape,BF)
    ve=halves(jnp.concatenate([v,one],axis=1),h0)
    outs=[]
    for r in range(0,n,SB):
        ext=r+SB
        keep=(lax.broadcasted_iota(jnp.int32,(SB,ext),0)+r)>=lax.broadcasted_iota(jnp.int32,(SB,ext),1)
        acc=None
        for s in range(2):
            sc=mm_nt(fqs[s][r:r+SB],fk[:ext])
            sc=jnp.where(keep,sc,0.0).astype(BF)
            t=mm(sc,ve[s][:ext])
            acc=t if acc is None else acc+t
        outs.append(acc)
    p=jnp.concatenate(outs,axis=0)
    w=v.shape[1]
    rden=1.0/p[:,w:]
    return p[:,:w]*rden, rden

def attend_back(fq,fk,v,mixed,rden,datt,ones,size):
    n,w=v.shape
    wide=(n,2*w)
    h0=first_half(wide,size)
    dn=(datt*rden).astype(BF)
    dd=-half_sum(datt*mixed.astype(F32),ones)*rden
    hi=dd.astype(BF); lo=(dd-hi.astype(F32)).astype(BF)
    lane=lax.broadcasted_iota(jnp.int32,(n,w),1)%size
    zero=jnp.zeros((n,w),BF)
    ext_=jnp.where(lane==0,hi,jnp.where(lane==1,lo,zero))
    nx=halves(jnp.concatenate([dn,ext_],axis=1),h0)
    vx=jnp.concatenate([v,jnp.ones((n,w),BF)],axis=1)
    fqs=halves(fq,h0); fks=halves(fk,h0)
    dfq=[];dfk=[];dv=[]
    for r in range(0,n,SB):
        ext=r+SB
        keep=(lax.broadcasted_iota(jnp.int32,(SB,ext),0)+r)>=lax.broadcasted_iota(jnp.int32,(SB,ext),1)
        acc=0.0
        for s in range(2):
            ds=jnp.where(keep,mm_nt(nx[s][r:r+SB],vx[:ext]),0.0).astype(BF)
            acc=acc+mm(ds,fks[s][:ext])
        dfq.append(acc)
        left=n-r
        keep=lax.broadcasted_iota(jnp.int32,(SB,left),0)<=lax.broadcasted_iota(jnp.int32,(SB,left),1)
        ak=0.0; av=0.0
        for s in range(2):
            ds=jnp.where(keep,mm_nt(vx[r:r+SB],nx[s][r:]),0.0).astype(BF)
            ak=ak+mm(ds,fqs[s][r:])
            sc=jnp.where(keep,mm_nt(fk[r:r+SB],fqs[s][r:]),0.0).astype(BF)
            av=av+mm(sc,nx[s][r:,:w])
        dfk.append(ak); dv.append(av)
    cat=lambda t: jnp.concatenate(t,axis=0)
    return cat(dfq),cat(dfk),cat(dv)

def feature_back(f, df, ones):
    w=f.shape[1]//2
    f=f.astype(F32)
    part=f*(df-half_sum(f*df,ones))
    return (part[:,:w]-part[:,w:]).astype(BF)

def pair_weights(wf_ref, w2_ref):
    hd=wf_ref.shape[-1]
    w2_ref[...]=jnp.zeros_like(w2_ref)
    for t in range(2):
        for p in range(w2_ref.shape[1]):
            w2_ref[t,p,:hd,:hd]=wf_ref[t,2*p]
            w2_ref[t,p,hd:,hd:]=wf_ref[t,2*p+1]

def fwd_kernel(len_ref, rows_ref, wqkv_ref, wf_ref, wout_ref, proj_ref, feat_ref, mixed_ref, rden_ref, branch_ref, w2_ref):
    hd=wf_ref.shape[-1]; w=2*hd; n=rows_ref.shape[0]; pairs=w2_ref.shape[1]
    pair_weights(wf_ref,w2_ref)
    for i in range(3):
        proj_ref[i]=mm(rows_ref[...],wqkv_ref[i]).astype(BF)
    ones=half_ones(2*w,hd)
    valid=lax.broadcasted_iota(jnp.int32,(n,2*w),0)<len_ref[0,0]
    def body(p,_):
        c=pl.ds(pl.multiple_of(p*w,w),w)
        fq=features(proj_ref[0,:,c],w2_ref[0,p],ones,hd).astype(BF)
        fk=jnp.where(valid,features(proj_ref[1,:,c],w2_ref[1,p],ones,hd),0.0).astype(BF)
        feat_ref[0,p]=fq; feat_ref[1,p]=fk
        m,rd=attend(fq,fk,proj_ref[2,:,c],hd)
        mixed_ref[:,c]=m.astype(BF); rden_ref[:,c]=rd
        return 0
    lax.fori_loop(0,pairs,body,0)
    branch_ref[...]=mm(mixed_ref[...],wout_ref[...]).astype(branch_ref.dtype)

def bwd_kernel(rows_ref,wqkv_ref,wf_ref,wout_ref,proj_ref,feat_ref,mixed_ref,rden_ref,dbr_ref,
               gq_ref,gf_ref,go_ref,dfirst_ref,w2_ref,datt_ref,dproj_ref):
    hd=wf_ref.shape[-1]; w=2*hd; n=rows_ref.shape[0]; pairs=w2_ref.shape[1]
    pair_weights(wf_ref,w2_ref)
    ones=half_ones(2*w,hd); ones1=half_ones(w,hd)
    datt_ref[...]=mm_nt(dbr_ref[...],wout_ref[...])
    go_ref[...]=mm_tn(mixed_ref[...],dbr_ref[...]).astype(go_ref.dtype)
    def body(p,_):
        c=pl.ds(pl.multiple_of(p*w,w),w)
        fq=feat_ref[0,p]; fk=feat_ref[1,p]
        dfq,dfk,dv=attend_back(fq,fk,proj_ref[2,:,c],mixed_ref[:,c],rden_ref[:,c],datt_ref[:,c],ones1,hd)
        for t,(f,df) in enumerate(((fq,dfq),(fk,dfk))):
            du=feature_back(f,df,ones)
            g=mm_tn(proj_ref[t,:,c],du)
            gf_ref[t,2*p]=g[:hd,:hd].astype(gf_ref.dtype); gf_ref[t,2*p+1]=g[hd:,hd:].astype(gf_ref.dtype)
            dproj_ref[t,:,c]=mm_nt(du,w2_ref[t,p]).astype(BF)
        dproj_ref[2,:,c]=dv.astype(BF)
        return 0
    lax.fori_loop(0,pairs,body,0)
    acc=None
    for i in range(3):
        gq_ref[i]=mm_tn(rows_ref[...],dproj_ref[i]).astype(gq_ref.dtype)
        t=mm_nt(dproj_ref[i],wqkv_ref[i])
        acc=t if acc is None else acc+t
    dfirst_ref[...]=acc.astype(dfirst_ref.dtype)
VM=pl.BlockSpec(memory_space=pltpu.VMEM)
SM=pl.BlockSpec(memory_space=pltpu.SMEM)
S=jax.ShapeDtypeStruct
def fwd(length,rows,wqkv,wf,wout):
    n,d=rows.shape; c=wout.shape[0]; h=wf.shape[1]; hd=wf.shape[-1]
    return pl.pallas_call(fwd_kernel,
      out_shape=(S((3,n,c),BF),S((2,h//2,n,4*hd),BF),S((n,c),BF),S((n,c),F32),S((n,d),BF)),
      in_specs=[SM,VM,VM,VM,VM],out_specs=[VM]*5,
      scratch_shapes=[pltpu.VMEM((2,h//2,2*hd,2*hd),BF)],
      compiler_params=pltpu.CompilerParams(vmem_limit_bytes=56*2**20))(length,rows,wqkv,wf,wout)
def bwd(rows,wqkv,wf,wout,proj,feat,mixed,rden,dbr):
    n,d=rows.shape; c=wout.shape[0]; h=wf.shape[1]; hd=wf.shape[-1]
    return pl.pallas_call(bwd_kernel,
      out_shape=(S((3,d,c),BF),S((2,h,hd,hd),F32),S((c,d),BF),S((n,d),BF)),
      in_specs=[VM]*9,out_specs=[VM]*4,
      scratch_shapes=[pltpu.VMEM((2,h//2,2*hd,2*hd),BF),pltpu.VMEM((n,c),F32),pltpu.VMEM((3,n,c),BF)],
      compiler_params=pltpu.CompilerParams(vmem_limit_bytes=56*2**20))(rows,wqkv,wf,wout,proj,feat,mixed,rden,dbr)

EPS=1e-05

def normalize(values, gain):
    average = jnp.mean(values, axis=-1, keepdims=True)
    centred = values - average
    spread = jnp.mean(centred * centred, axis=-1, keepdims=True)
    return centred * lax.rsqrt(spread + EPS) * gain

def smooth_gate(values):
    return jax.nn.gelu(values, approximate=True)

def per_device(
    tokens, lengths, norm_first, w_qkv, w_feature, w_out, norm_second, w_up, w_down, cotangent
):
    wqkv=jnp.transpose(w_qkv,(1,0,2))
    residual_in = tokens[0].astype(jnp.float32)
    normed_first, first_back = jax.vjp(normalize, residual_in, norm_first)
    first_low = normed_first.astype(jnp.bfloat16)
    first_rows = lax.all_gather(first_low, "head", axis=0, tiled=True)
    cot_low = cotangent[0]
    cot_rows = lax.all_gather(cot_low, "hidden", axis=0, tiled=True)
    proj,feat,mixed,rden,part=fwd(lengths,first_rows,wqkv,w_feature,w_out)
    branch = lax.psum_scatter(part, "head", scatter_dimension=0, tiled=True).astype(jnp.float32)
    middle = residual_in + branch
    normed_second, second_back = jax.vjp(normalize, middle, norm_second)
    second_low = normed_second.astype(jnp.bfloat16)
    second_rows = lax.all_gather(second_low, "hidden", axis=0, tiled=True)
    hidden_pre = jnp.dot(second_rows, w_up, preferred_element_type=jnp.float32)
    active = smooth_gate(hidden_pre).astype(jnp.bfloat16)
    gate_grad = jax.vjp(smooth_gate, hidden_pre)[1]
    d_active = jnp.einsum("nd,fd->nf", cot_rows, w_down, preferred_element_type=jnp.float32)
    d_pre = gate_grad(d_active)[0].astype(jnp.bfloat16)
    d_second = lax.psum_scatter(
        jnp.einsum("nf,df->nd", d_pre, w_up, preferred_element_type=jnp.float32).astype(jnp.bfloat16),
        "hidden",
        scatter_dimension=0,
        tiled=True,
    ).astype(jnp.float32)
    mlp_result = lax.psum_scatter(
        jnp.dot(active, w_down, preferred_element_type=jnp.float32).astype(jnp.bfloat16),
        "hidden",
        scatter_dimension=0,
        tiled=True,
    ).astype(jnp.float32)
    block_out = (middle + mlp_result).astype(jnp.bfloat16)
    grad_down = jnp.einsum("nf,nd->fd", active, cot_rows, preferred_element_type=jnp.float32)
    grad_up = jnp.einsum("nd,nf->df", second_rows, d_pre, preferred_element_type=jnp.float32)
    d_middle_norm, grad_norm_second = second_back(d_second)
    d_middle = cot_low.astype(jnp.float32) + d_middle_norm
    d_branch_rows = lax.all_gather(d_middle.astype(jnp.bfloat16), "head", axis=0, tiled=True)
    gq,grad_feature,go,dfirst=bwd(first_rows,wqkv,w_feature,w_out,proj,feat,mixed,rden,d_branch_rows)
    d_first = lax.psum_scatter(dfirst, "head", scatter_dimension=0, tiled=True).astype(jnp.float32)
    d_input_norm, grad_norm_first = first_back(d_first)
    grad_tokens = d_middle + d_input_norm
    grad_up, grad_down = (
        lax.psum(grad_up.astype(jnp.bfloat16), ("dp", "head")).astype(jnp.float32),
        lax.psum(grad_down.astype(jnp.bfloat16), ("dp", "head")).astype(jnp.float32),
    )
    gq, grad_feature, go = (
        lax.psum(gq, ("dp", "hidden")).astype(jnp.float32),
        lax.psum(grad_feature.astype(jnp.bfloat16), ("dp", "hidden")).astype(jnp.float32),
        lax.psum(go, ("dp", "hidden")).astype(jnp.float32),
    )
    grad_norm_first, grad_norm_second = lax.psum(
        (grad_norm_first, grad_norm_second), ("dp", "head", "hidden")
    )
    return (
        block_out[None],
        grad_tokens[None],
        grad_norm_first,
        jnp.transpose(gq,(1,0,2)),
        grad_feature,
        go,
        grad_norm_second,
        grad_up,
        grad_down,
    )


ORDER=("n0","w","t","n1","a","cy","pt","po","cz","w","pa","sa","cy","tr","pb","sb","w","w","xa","ya","cz","xb","cx","yb","bx","by","ya","bo","xb","bd","gu","gd","u","Yb","Db","Da","dno","Dc","Dd","dn","A!","Da","Xa","Dd","v","Dc","fi","u","B!","Db","fj","dm","v","b","d","go","u","0","do","p0","p1","0","1","2","u","v","A","p2","0","1","p3","2","fo","4","0","1","fm","2","3","0","1","4","v","3","2","f","u","4","3","0","v","2","1","4","u","n","3","B","2","4","0","1","n","3","A","n","4","3","B","2","1","v","0","n","2","v","u","4","1","3","4","n","3")
EARLY_X=(3,)
SUM_ALL=()
GATHER_ALL=()
ROWS_X_FIRST=True

MESH=pl.DeviceIdType.MESH
ANY=pl.BlockSpec(memory_space=pl.ANY)
EPS=1e-05

def place():
    dp=lax.axis_index("dp")
    return dp//2, dp%2, lax.axis_index("head"), lax.axis_index("hidden")

def only(when,act):
    if when is None: act()
    else: pl.when(when)(act)

class Wires:
    def __init__(self,sems):
        self.sems=sems; self.count=0; self.all=[]
    def send(self,src,dst,dev,when=None):
        i=self.count
        self.count+=1
        k=pltpu.make_async_remote_copy(src_ref=src,dst_ref=dst,send_sem=self.sems.at[0,i],recv_sem=self.sems.at[1,i],device_id=dev,device_id_type=MESH)
        only(when,k.start)
        self.all.append((k,when))
        return k

def greet(peers):
    bar=pltpu.get_barrier_semaphore()
    for d in peers: pl.semaphore_signal(bar,inc=1,device_id=d,device_id_type=MESH)
    pl.semaphore_wait(bar,len(peers))

def unit(values):
    centred=values-jnp.mean(values,axis=-1,keepdims=True)
    r=lax.rsqrt(jnp.mean(centred*centred,axis=-1,keepdims=True)+EPS)
    return centred*r, r

def norm_back(values,grad,gain):
    xh,r=unit(values)
    e=grad*gain
    inner=e-jnp.mean(e,axis=-1,keepdims=True)-xh*jnp.mean(e*xh,axis=-1,keepdims=True)
    return r*inner, jnp.sum(grad*xh,axis=0,keepdims=True)

def gate(v):
    k=0.7978845608; a=0.044715
    sq=v*v
    t=jnp.tanh(k*v*(1.0+a*sq))
    half=0.5*(1.0+t)
    return v*half, half+0.5*v*(1.0-t*t)*(k+(3.0*a*k)*sq)

def add_into(dst,src,step):
    rows=dst.shape[0]
    def body(i,_):
        r=pl.ds(pl.multiple_of(i*step,step),step)
        dst[r]=(dst[r].astype(F32)+src[r].astype(F32)).astype(dst.dtype)
        return 0
    lax.fori_loop(0,rows//step,body,0)

def layer_kernel(len_ref,tok,cot,g1,g2,wqkv,wf,wout,wup,wdn,
                 bo_o,gt_o,go_o,gp_o,gu_o,gd_o,gn_o,
                 T,rows,rowsT,wq,wo,proj,feat,mixed,rden,own,snd,rcv,mid,
                 SA,CA,Wu,Wd,act,dpre,P,ML,gu,gd,cu,cd,zu,zd,mu,md,yu,yd,rx,ry,rdx,rdy,
                 dmid,db,datt,dproj,G0,GP,C0,CP,X0,XP,U0,UP,W0,WP,
                 ma,mb,na,nb,bo,dfs,dfr,gn2,gsum,gn,gr,w2,loc,sems):
    x,c,y,z=place()
    nh=lax.axis_size("hidden"); last=nh-1
    nx,ny,nc=((1-x)*2+c,y,z),(x*2+c,1-y,z),(x*2+1-c,y,z)
    low,side=z%2,z//2
    z1,z2=z+1-2*low,(z+2)%nh
    inner=low!=side
    mate=(x*2+c,y,last-z)
    n1,n2=(x*2+c,y,z1),(x*2+c,y,z2)
    R,d=tok.shape; n=2*R; H=R//2
    hd=wf.shape[-1]; w=2*hd; pairs=w2.shape[1]; f=wup.shape[1]; fs=f//4
    qo,qx,qy,qd=x*2+y,(1-x)*2+y,x*2+1-y,(1-x)*2+1-y
    mine=pl.ds(pl.multiple_of(y*R,R),R); other=pl.ds(pl.multiple_of((1-y)*R,R),R)
    A=pl.ds(0,H); B=pl.ds(H,H)
    top,end=(pl.ds(pl.multiple_of(y*R+i*H,H),H) for i in range(2))
    half=lambda size,b: pl.ds(pl.multiple_of(b*size,size),size)
    hu,hw=d//2,fs//2
    uo,ua,vo,va=half(hu,c),half(hu,1-c),half(hw,c),half(hw,1-c)
    at=lambda q: pl.ds(pl.multiple_of(q*fs,fs),fs)
    nloc=[0]; pend=[]; seen=[]
    def lc(s,t,out=False):
        k=pltpu.make_async_copy(s,t,loc.at[nloc[0]]); nloc[0]+=1
        k.start()
        if out: pend.append(k)
        return k
    wires=Wires(sems)
    send=wires.send
    l_tok=lc(tok,T.at[mine])
    l_wq=[lc(wqkv.at[i],wq.at[i]) for i in range(3)]
    greet((nx,ny,nc)+tuple((x*2+c,y,(z+t)%nh) for t in range(1,nh)))

    def simple(src,dst,dev):
        k=send(src,dst,dev)
        yield
        k.wait_recv()

    def onward(src,dst,dev,src2,dst2,dev2,between=None):
        k=send(src,dst,dev)
        yield
        k.wait_recv()
        if between is not None: between()
        k=send(src2,dst2,dev2)
        yield
        k.wait_recv()

    def weights():
        wdh=lambda q: pl.ds(pl.multiple_of(q*fs+c*hw,hw),hw)
        wdo=lambda q: pl.ds(pl.multiple_of(q*fs+(1-c)*hw,hw),hw)
        for s in range(1,nh):
            now=[]
            for right in (True,False):
                j=(z-s+1) if right else (z+s-1)
                when=((z<last)&(j>=0)) if right else ((z>0)&(j<=last))
                jj=jnp.clip(j,0,last)
                dev=(x*2+c,y,jnp.clip(z+1 if right else z-1,0,last))
                if s==1: su,sd=wup.at[uo,at(qo)],wdn.at[wdh(qo)]
                else: su,sd=Wu.at[uo,at(jj)],Wd.at[wdh(jj)]
                got=(z-s>=0) if right else (z+s<=last)
                now.append((send(su,Wu.at[uo,at(jj)],dev,when),send(sd,Wd.at[wdh(jj)],dev,when),got))
            yield
            for a,b,got in now: only(got,a.wait_recv); only(got,b.wait_recv)
            for right,(_,_,got) in zip((True,False),now):
                jj=jnp.clip((z-s) if right else (z+s),0,last)
                shared.append((send(Wu.at[uo,at(jj)],Wu.at[uo,at(jj)],nc,got),got))
                shared.append((send(Wd.at[wdh(jj)],Wd.at[wdh(jj)],nc,got),got))
        yield
        for k,got in shared: only(got,k.wait_recv)
    shared=[]

    def grads(G,bufs,O,early,sum_all,gather_all):
        steps=[(nc,c),(nx,x),(n1,low),(n2,side)]
        size=G.shape[0]; base=0
        for i in range(2 if sum_all else 4):
            dev,bit=steps[i]
            size//=2
            away=pl.multiple_of(base+(1-bit)*size,16)
            base=pl.multiple_of(base+bit*size,16)
            k=send(G.at[pl.ds(away,size)],bufs[i],dev)
            yield
            k.wait_recv()
            add_into(G.at[pl.ds(base,size)],bufs[i],size//2 if size%32==0 else size)
        if sum_all:
            size//=4
            slots=[bufs[2].at[pl.ds(0,size)],bufs[2].at[pl.ds(size,size)],bufs[3]]
            ks=[]
            for t in (2,1,3):
                j=(z+t)%nh
                piece=pl.ds(pl.multiple_of(base+(2*(j%2)+j//2)*size,16),size)
                ks.append(send(G.at[piece],slots[t-1],(x*2+c,y,j)))
            yield
            base=pl.multiple_of(base+(2*low+side)*size,16)
            for k in ks: k.wait_recv()
            for s in slots: add_into(G.at[pl.ds(base,size)],s,size)
        src=G.at[pl.ds(base,size)]
        place_=[c,x,low,side]
        copy=lc(src,O.at[tuple(place_)])
        def gather(devs,*dims):
            nonlocal src,copy
            ks=[send(O.at[tuple(place_)] if src is None else src,O.at[tuple(place_)],dev) for dev in devs]
            src=None
            yield
            for k in ks: k.wait_recv()
            if copy is not None: copy.wait()
            copy=None
            for i in dims: place_[i]=slice(None)
        if early: yield from gather([nx],1)
        if gather_all: yield from gather([(x*2+c,y,(z+t)%nh) for t in (2,1,3)],2,3)
        else:
            yield from gather([n2],3)
            yield from gather([n1],2)
        if not early: yield from gather([nx],1)
        yield from gather([nc],0)

    def mlp_grads(W,kept,away,core,far,middle,final,whole,piece,step):
        two=lambda i: pl.ds(pl.multiple_of(2*i,2),2)
        k=send(W.at[:,away],core,nc)
        yield
        k.wait_recv()
        for j in range(nh): add_into(W.at[j,kept],core.at[j],step)
        k=send(W.at[two(1-low),kept],far,n1)
        yield
        k.wait_recv()
        for j in range(2): add_into(W.at[2*low+j,kept],far.at[j],step)
        m=send(W.at[two(low),kept],middle,mate,inner)
        yield
        def take():
            m.wait_recv()
            k.wait_send()
            for j in range(2): W[2*side+j,kept]=middle[j]
        pl.when(inner)(take)
        seen.append(k)
        k2=send(W.at[2*side+1-low,kept],final,n1)
        yield
        k2.wait_recv()
        add_into(W.at[z,kept],final,step)
        l=lc(W.at[z,kept],piece(qo))
        k=send(W.at[z,kept],piece(qo),nx)
        k2=send(W.at[z,kept],piece(qo),ny)
        yield
        k.wait_recv()
        k=send(piece(qx),piece(qx),ny)
        yield
        k.wait_recv(); k2.wait_recv(); l.wait()
        k=send(whole,whole,nc)
        yield
        k.wait_recv()

    def mlp_rows(r,near,dev,q1,q2,buf,far,q3):
        k=[send(ML.at[q1,r],buf.at[0],near),send(ML.at[q2,r],buf.at[1],near)]
        yield
        for t in k: t.wait_recv()
        add_into(ML.at[qo,r],buf.at[0],H); add_into(ML.at[q3,r],buf.at[1],H)
        k=send(ML.at[q3,r],far,dev)
        yield
        k.wait_recv()
        bo[r]=(mid[r]+(ML[qo,r].astype(F32)+far[...].astype(F32))).astype(BF)
        lc(bo.at[r],bo_o.at[r],True)

    def first_grad(r):
        t=mm_nt(dproj[0,r],wq[0])+mm_nt(dproj[1,r],wq[1])
        return t+mm_nt(dproj[2,r],wq[2])

    def first_rows():
        t=first_grad(other)
        dfs[...]=t.astype(BF)
        k=send(dfs,dfr,ny)
        xo,_=unit(T[other].astype(F32))
        gsum[...]=jnp.sum(t*xo,axis=0,keepdims=True)
        yield
        k.wait_recv()
        dx,_=norm_back(T[mine].astype(F32),own[...]+dfr[...].astype(F32),g1[...])
        dmid[...]=dmid[...]+dx
        lc(dmid,gt_o,True)

    def gains():
        t=first_grad(mine)
        own[...]=t
        xm,_=unit(T[mine].astype(F32))
        gn[...]=jnp.zeros_like(gn)
        gn[0,0:1]=gsum[...]+jnp.sum(t*xm,axis=0,keepdims=True)
        gn[0,1:2]=gn2[...]
        order=[nc,nx,ny,n1,n2]
        for i,dev in enumerate(order):
            k=send(gn.at[i],gr.at[i],dev)
            yield
            k.wait_recv()
            gn[i+1]=gn[i]+gr[i]
        gn_o[...]=gn[len(order)]

    Q=H//2
    quarters=[pl.ds(i*Q,Q) for i in range(4)]
    def diagonal(i):
        r=quarters[i]; s=pl.ds((i%2)*Q,Q)
        near,q,buf,out,far=(nx,qy,rdx,ry,ny) if i<2 else (ny,qx,rdy,rx,nx)
        def add(): P[q,r]=(P[q,r].astype(F32)+buf[s].astype(F32)).astype(BF)
        return onward(P.at[qd,r],buf.at[s],near,P.at[q,r],out.at[r],far,add)
    S_=lambda q,r: SA.at[q,r]
    chains={
        "t":simple(tok,T.at[mine],ny),
        "w":weights(),
        "cx":simple(cot,CA.at[qo],nx),
        "cy":onward(cot.at[A],CA.at[qo,A],ny,CA.at[qy,A],CA.at[qy,A],nx),
        "cz":onward(cot.at[B],CA.at[qo,B],ny,CA.at[qy,B],CA.at[qy,B],nx),
        "pa":simple(snd.at[A],rcv.at[A],ny),
        "pb":simple(snd.at[B],rcv.at[B],ny),
        "xa":simple(S_(qo,A),S_(qo,A),nx),
        "yb":simple(S_(qo,B),S_(qo,B),ny),
        "xb":onward(S_(qo,B),S_(qo,B),nx,S_(qx,B),S_(qx,B),ny),
        "ya":onward(S_(qo,A),S_(qo,A),ny,S_(qy,A),S_(qy,A),nx),
        "Xa":simple(P.at[qx,A],rx.at[A],nx),
        "Yb":simple(P.at[qy,B],ry.at[B],ny),
        "Da":diagonal(0),"Dc":diagonal(1),"Db":diagonal(2),"Dd":diagonal(3),
        "b":simple(db.at[top],db.at[top],ny),
        "d":simple(db.at[end],db.at[end],ny),
        "u":mlp_grads(gu,uo,ua,cu,zu,mu,yu,gu_o.at[uo],lambda q: gu_o.at[uo,at(q)],64),
        "v":mlp_grads(gd,vo,va,cd,zd,md,yd,gd_o.at[:,vo],lambda q: gd_o.at[q,vo],16),
        "A":mlp_rows(A,nx,ny,qx,qd,ma,na,qy),"B":mlp_rows(B,nx,ny,qx,qd,mb,nb,qy) if ROWS_X_FIRST else mlp_rows(B,ny,nx,qy,qd,mb,nb,qx),
        "f":first_rows(),"n":gains(),
        "0":grads(G0,(C0,X0,U0,W0),go_o,-1 in EARLY_X,-1 in SUM_ALL,-1 in GATHER_ALL)}
    for p in range(pairs): chains[str(p+1)]=grads(GP.at[p],(CP.at[p],XP.at[p],UP.at[p],WP.at[p]),gp_o.at[p],p in EARLY_X,p in SUM_ALL,p in GATHER_ALL)
    turns={name:-1 for name in chains}
    def go(*names):
        for name in names:
            next(chains[name],None)
            turns[name]+=1
    def need(**steps):
        for name,count in steps.items():
            while turns[name]<count: go(name)

    ones=half_ones(2*w,hd); ones1=half_ones(w,hd)
    valid=lax.broadcasted_iota(jnp.int32,(n,2*w),0)<len_ref[0,0]
    def first(r):
        xh,_=unit(T[r].astype(F32))
        rows[r]=(xh*g1[...]).astype(BF)
    def project(r):
        for i in range(3): proj[i,r]=mm(rows[r],wq[i]).astype(BF)
    def heads(p,_):
        cc=pl.ds(pl.multiple_of(p*w,w),w)
        fq=features(proj[0,:,cc],w2[0,p],ones,hd).astype(BF)
        fk=jnp.where(valid,features(proj[1,:,cc],w2[1,p],ones,hd),0.0).astype(BF)
        feat[0,p]=fq; feat[1,p]=fk
        m,rd=attend(fq,fk,proj[2,:,cc],hd)
        mixed[:,cc]=m.astype(BF); rden[:,cc]=rd
        return 0
    def second(start):
        r=pl.ds(start,H)
        middle=T[pl.ds(pl.multiple_of(y*R+start,H),H)].astype(F32)+(own[r]+rcv[r].astype(F32))
        mid[r]=middle
        xh,_=unit(middle)
        SA[qo,r]=(xh*g2[...]).astype(BF)
    def block(qi,keep):
        need(w=nh)
        while l_own: l_own.pop().wait()
        a,ga=gate(mm(SA[qi],Wu[...]))
        act[qi]=a.astype(BF)
        dp=(mm_nt(CA[qi],Wd[...])*ga).astype(BF)
        dpre[qi]=dp
        d2=mm_nt(dp,Wu[...])
        if keep: own[...]=d2
        else: P[qi]=d2.astype(BF)
    def middle_grad(r,there):
        dx,g=norm_back(mid[r],own[r]+(rx[r].astype(F32)+ry[r].astype(F32)),g2[...])
        dm=CA[qo,r].astype(F32)+dx
        dmid[r]=dm
        db[there]=dm.astype(BF)
        return g
    def down(qi): ML[qi]=mm(act[qi],Wd[...]).astype(BF)
    def pair(p):
        cc=slice(p*w,(p+1)*w)
        fq=feat[0,p]; fk=feat[1,p]
        dfq,dfk,dv=attend_back(fq,fk,proj[2,:,cc],mixed[:,cc],rden[:,cc],datt[:,cc],ones1,hd)
        parts=[]
        for t,(ft,df) in enumerate(((fq,dfq),(fk,dfk))):
            du=feature_back(ft,df,ones)
            GP[p,pl.ds(3*d+t*w,w)]=mm_tn(proj[t,:,cc],du).astype(BF)
            parts.append(mm_nt(du,w2[t,p]).astype(BF))
        parts.append(dv.astype(BF))
        for t in range(3): dproj[t,:,cc]=parts[t]
        g=mm(rowsT[...],jnp.concatenate(parts,axis=1)).astype(BF)
        for t in range(3): GP[p,pl.ds(t*d,d)]=g[:,t*w:(t+1)*w]
    def do(name):
        if name=="n0":
            pair_weights(wf,w2)
            l_tok.wait()
            first(mine)
            for k in l_wq: k.wait()
            project(mine)
        elif name=="n1":
            need(t=1)
            first(other); project(other)
        elif name=="a": lax.fori_loop(0,pairs,heads,0)
        elif name=="pt":
            l_wo.wait()
            snd[...]=mm(mixed[other],wo[...]).astype(BF)
            go("pa","pb")
        elif name=="po": own[...]=mm(mixed[mine],wo[...])
        elif name=="tr": rowsT[...]=rows[...].T
        elif name=="sa": need(pa=1); second(0); go("xa","ya")
        elif name=="sb": need(pb=1); second(H); go("xb","yb")
        elif name=="bo":
            block(qo,True)
        elif name=="dno": down(qo)
        elif name=="bx":
            need(xa=1,xb=1,cx=1)
            block(qx,False); go("Xa")
        elif name=="by":
            need(ya=1,yb=1,cy=1,cz=1)
            block(qy,False); go("Yb")
        elif name=="bd":
            need(xb=2,ya=2,cy=2,cz=2)
            block(qd,False); go("Da","Db","Dc","Dd")
        elif name=="gu":
            sa=SA[...].reshape(4*R,d)
            for j in range(nh//2):
                t=mm_tn(sa,dpre[:,:,pl.ds(2*j*fs,2*fs)].reshape(4*R,2*fs)).astype(BF)
                gu[2*j]=t[:,:fs]; gu[2*j+1]=t[:,fs:]
            go("u")
        elif name=="dn":
            for q in (qx,qy,qd): down(q)
        elif name=="gd":
            ca=CA[...].reshape(4*R,d)
            for j in range(nh): gd[j]=mm_tn(act[:,:,pl.ds(j*fs,fs)].reshape(4*R,fs),ca).astype(BF)
            go("v")
        elif name=="A!": go("A")
        elif name=="B!": go("B")
        elif name=="fi":
            need(Da=2,Dc=2,Xa=1)
            gn2[...]=middle_grad(A,top)
            go("b")
        elif name=="fj":
            need(Db=2,Dd=2,Yb=1)
            gn2[...]=gn2[...]+middle_grad(B,end)
            go("d")
        elif name=="dm": datt[mine]=mm_nt(db[mine],wo[...])
        elif name=="do":
            need(b=1,d=1)
            datt[other]=mm_nt(db[other],wo[...])
        elif name=="go":
            G0[...]=mm_tn(mixed[...],db[...]).astype(BF)
            go("0")
        elif name[0]=="p" and len(name)==2 and name[1].isdigit():
            p=int(name[1])
            if p<pairs: pair(p); go(str(p+1))
        elif name=="fo": go("f")
        elif name=="fm": go("n")
        elif name in chains: go(name)
    go("t","cy","cz","cx","w")
    l_wo=lc(wout,wo)
    l_own=[lc(wup.at[:,at(qo)],Wu.at[:,at(z)]),lc(wdn.at[at(qo)],Wd.at[at(z)]),lc(cot,CA.at[qo])]
    for name in ORDER: do(name)
    for name in chains:
        for _ in chains[name]: pass
    outer=jnp.logical_not(inner)
    for k,when in wires.all: only(outer if any(k is t for t in seen) else when,k.wait_send)
    for k in pend: k.wait()

def layer(length,tok,cot,g1,g2,wqkv,wf,wout,wup,wdn):
    R,d=tok.shape; n=2*R; H=R//2; c=wout.shape[0]; h=wf.shape[1]; hd=wf.shape[-1]; pairs=h//2; w=2*hd; q=3*d+2*w
    f=wup.shape[1]; fs=f//4; nz=lax.axis_size("hidden")
    D=pltpu.SemaphoreType.DMA
    b=lambda *s: pltpu.VMEM(s,BF)
    e=lambda *s: pltpu.VMEM(s,F32)
    return pl.pallas_call(layer_kernel,
      out_shape=(S((R,d),BF),S((R,d),F32),S((2,2,2,2,c//16,d),BF),S((pairs,2,2,2,2,q//16,w),BF),S((d,f),BF),S((4,fs,d),BF),S((8,d),F32)),
      in_specs=[SM,ANY,ANY,VM,VM,ANY,VM,ANY,ANY,ANY],
      out_specs=[ANY]*6+[VM],
      scratch_shapes=[b(n,d),b(n,d),b(d,n),b(3,d,c),b(c,d),b(3,n,c),b(2,pairs,n,2*w),b(n,c),e(n,c),e(R,d),b(R,d),b(R,d),e(R,d),
        b(4,R,d),b(4,R,d),b(d,f),b(f,d),b(4,R,f),b(4,R,f),b(4,R,d),b(4,R,d),b(nz,d,fs),b(nz,fs,d),b(nz,d//2,fs),b(nz,fs//2,d),
        b(2,d//2,fs),b(2,fs//2,d),b(2,d//2,fs),b(2,fs//2,d),b(d//2,fs),b(fs//2,d),b(R,d),b(R,d),b(H,d),b(H,d),
        e(R,d),b(n,d),e(n,c),b(3,n,c),b(c,d),b(pairs,q,w),b(c//2,d),b(pairs,q//2,w),b(c//4,d),b(pairs,q//4,w),
        b(c//8,d),b(pairs,q//8,w),b(c//16,d),b(pairs,q//16,w),
        b(2,H,d),b(2,H,d),b(H,d),b(H,d),b(R,d),b(R,d),b(R,d),e(1,d),e(1,d),e(6,8,d),e(5,8,d),
        b(2,pairs,w,w),D((24,)),D((2,128))],
      compiler_params=pltpu.CompilerParams(vmem_limit_bytes=63*2**20,collective_id=1,has_side_effects=True),
      cost_estimate=pl.CostEstimate(flops=24*10**9,bytes_accessed=40*10**6,transcendentals=2*10**6))(
      length,tok,cot,g1,g2,wqkv,wf,wout,wup,wdn)

def per_device_k1(
    tokens, lengths, norm_first, w_qkv, w_feature, w_out, norm_second, w_up, w_down, cotangent
):
    h,hd=w_feature.shape[1],w_feature.shape[3]; w=2*hd
    block_out,grad_tokens,go,gp,gu,gd,gn=layer(lengths,tokens[0],cotangent[0],norm_first[None],norm_second[None],jnp.transpose(w_qkv,(1,0,2)),w_feature,w_out,w_up,w_down)
    go=go.reshape(w_out.shape); gp=gp.reshape(h//2,-1,w)
    go,gq,gf,gu,gd,block_out,grad_tokens,n1,n2=finish(go,gp,gu,gd.reshape(gd.shape[0]*gd.shape[1],-1),block_out,grad_tokens,gn,hd)
    return (
        block_out[None],
        grad_tokens[None],
        n1[0],
        jnp.transpose(gq,(1,0,2)),
        gf,
        go,
        n2[0],
        gu,
        gd,
    )

def finish_kernel(go,g0,g1,g2,gf,gu,gd,bo,gt,gn,go_o,gq_o,gf_o,gu_o,gd_o,bo_o,gt_o,n1_o,n2_o):
    for a,b in ((go,go_o),(gu,gu_o),(gd,gd_o)): b[...]=a[...].astype(F32)
    bo_o[...]=bo[...]
    gt_o[...]=gt[...]
    pairs,_,w=g0.shape; hd=w//2
    for t,g in enumerate((g0,g1,g2)):
        for p in range(pairs): gq_o[t,:,p*w:(p+1)*w]=g[p].astype(F32)
    @pl.when(pl.program_id(0)==0)
    def _():
        n1_o[...]=gn[0:1]; n2_o[...]=gn[1:2]
        for t in range(2):
            for p in range(pairs):
                for s in range(2):
                    gf_o[t,2*p+s]=gf[p,t*w+s*hd:t*w+(s+1)*hd,s*hd:(s+1)*hd].astype(F32)

def finish(go,gp,gu,gd,bo,gt,gn,hd,N=2):
    c,d=go.shape; pairs,_,w=gp.shape; f=gu.shape[1]
    B=pl.BlockSpec
    row=lambda a: B((a.shape[0]//N,a.shape[1]),lambda i:(i,0))
    all_=lambda a: B(a.shape,lambda i:(0,)*len(a.shape))
    part=lambda t: B((pairs,d//N,w),lambda i:(0,i+N*t,0))
    gf=S((2,2*pairs,hd,hd),F32); n=S((1,d),F32)
    return pl.pallas_call(finish_kernel,grid=(N,),
      out_shape=(S((c,d),F32),S((3,d,c),F32),gf,S((d,f),F32),S((f,d),F32),S(bo.shape,BF),S(gt.shape,F32),n,n),
      in_specs=[row(go),part(0),part(1),part(2),B((pairs,2*w,w),lambda i:(0,3*d//(2*w),0)),row(gu),row(gd),row(bo),row(gt),all_(gn)],
      out_specs=[row(go),B((3,d//N,c),lambda i:(0,i,0)),all_(gf),row(gu),row(gd),row(bo),row(gt),all_(n),all_(n)],
      compiler_params=pltpu.CompilerParams(vmem_limit_bytes=62*2**20))(go,gp,gp,gp,gp,gu,gd,bo,gt,gn)


def solution(mesh):
    in_specs = (
        P(("dp", "hidden"), "head", None),
        P(("dp", "hidden"), None),
        P(),
        P(None, None, "head"),
        P(None, "head", None, None),
        P("head", None),
        P(),
        P(None, "hidden"),
        P("hidden", None),
        P(("dp", "hidden"), "head", None),
    )
    out_specs = (
        P(("dp", "hidden"), "head", None),
        P(("dp", "hidden"), "head", None),
        P(),
        P(None, None, "head"),
        P(None, "head", None, None),
        P("head", None),
        P(),
        P(None, "hidden"),
        P("hidden", None),
    )
    near=dict(mesh.shape)=={"dp":4,"head":2,"hidden":4}
    return jax.shard_map(
        per_device_k1 if near else per_device, mesh=mesh, in_specs=in_specs, out_specs=out_specs, check_vma=False
    )
```
